256 devices in a mesh: op: 16 (over z, x_lo), tp: 16 (over y, x_hi, core).
Axes of the slice: x: 4 (x_hi: 2, x_lo: 2; x = x_hi * 2 + x_lo), y: 4, z: 8, core: 2. Of those that a mesh axis runs over, the one named last changes fastest.
Arguments:
- token_ids: int32 [2048], P('op'), may hold values from 0 to 31999
- embed_small: bfloat16 [32000, 4096], P('op', 'tp'), may hold values from -6 to 6
- proj_small: bfloat16 [4096, 4096], P(None, 'tp'), may hold values from -0.09375 to 0.09375
- grow_op: bfloat16 [6656, 4096], P('tp', 'op'), may hold values from -1.5 to 1.5
- norm_gain: bfloat16 [6656], P('tp'), may hold values from 0.099609375 to 1.8984375
- out_grad: bfloat16 [2048, 6656], P('op', 'tp'), may hold values from -0.21875 to 0.21875
Outputs:
- grad_op: float32 [6656, 4096], P('tp', 'op')
The draws below stay inside these ranges and needn't reach their ends.
All inputs are finite; a program needn't handle non-finite values.
Results may differ from the reference program's by a relative error of at most 0.023.
Values may be sent and summed in bfloat16 or wider, within the bound.
No kernel may reach another device: no remote copies, remote signals or barrier semaphores. Data moves between devices by JAX's collectives and lax.ppermute only.
A program may use at most 64 MiB of HBM per device.

```python
import math
import jax
import jax.numpy as jnp
import numpy as np
from jax import lax

D1 = 4096
D2 = 6656
V = 32000
TOK_DEV = 128
TOKENS = 2048
N_OP = 16


def draw_grow_op(key, part):
    key = jax.random.fold_in(key, 11)
    first, second = jax.random.split(key)
    base = jnp.clip(jax.random.normal(first, (D2, D1), jnp.float32), -5.0, 5.0)
    rows = jnp.arange(D2, dtype=jnp.float32) / (D2 - 1)
    rise = jnp.exp(rows * math.log(9.0))
    rough = jnp.exp(jax.random.uniform(second, (D2,), jnp.float32, -0.35, 0.35))
    scale = rise * rough / math.sqrt(D1)
    return jnp.clip(base * scale[:, None], -1.5, 1.5).astype(jnp.bfloat16)


def place_ends(result, own_key, smallest, largest):
    index_at = [jax.random.randint(jax.random.fold_in(own_key, axis), (), 0, length) for axis, length in enumerate(result.shape)]
    longest = result.shape.index(max(result.shape))
    next_to = index_at[:longest] + [(index_at[longest] + 1) % result.shape[longest]] + index_at[longest + 1:]
    return result.at[tuple(index_at)].set(smallest).at[tuple(next_to)].set(largest)


def steps_of(rng, dims, pieces, smallest, largest):
    loudness, own = 1.0, jax.random.fold_in(rng, 6)
    for axis_at, blocks in pieces:
        draws = jnp.exp(jax.random.uniform(jax.random.fold_in(own, axis_at), (blocks,), jnp.float32, smallest / len(pieces), largest / len(pieces)))
        loudness = loudness * jnp.repeat(draws, dims[axis_at] // blocks).reshape([-1 if axis == axis_at else 1 for axis in range(len(dims))])
    return loudness


def rank_table(number_of, skew):
    weights = [(1 << 20) // math.isqrt(rank ** skew) + 1 for rank in range(1, number_of + 1)]
    spread = 1 + sum(weights) // (1 << 30)
    return np.cumsum(np.array([max(1, weight // spread) for weight in weights]))


def ranked_ids(stream_key, extent, number_of, slope):
    listing = rank_table(number_of, slope)
    ticket = jax.random.randint(jax.random.fold_in(stream_key, 1), extent, 0, int(listing[number_of - 1]))
    rank = jnp.searchsorted(jnp.asarray(listing, jnp.int32), ticket, side="right")
    return jax.random.permutation(jax.random.fold_in(stream_key, 2), number_of)[rank].astype(jnp.int32)


def centred(rng, shape, scale, reach, cuts=(), kind=jnp.bfloat16):
    level = steps_of(rng, shape, cuts, -0.22, 0.18) if cuts else 1.0
    drawn = jax.random.normal(rng, shape, jnp.float32) * scale * level
    return jnp.minimum(jnp.maximum(drawn, -reach), reach).astype(kind)


def setup_inputs(seed: int = 0) -> dict:
    key_list = jax.random.split(jax.random.key(seed), 7)
    return {
        "token_ids": place_ends(ranked_ids(key_list[0], (TOKENS,), V, 2), jax.random.fold_in(key_list[0], 3), 0, V - 1).astype(jnp.int32),
        "embed_small": centred(key_list[1], (V, D1), 1.0, 6.0, ((0, 16), (1, 16))),
        "proj_small": centred(key_list[2], (D1, D1), D1 ** -0.5, 0.09375, ((1, 16),)),
        "grow_op": draw_grow_op(jax.random.fold_in(key_list[6], 71), 0),
        "norm_gain": jnp.clip(1.0 + 0.18 * jax.random.normal(key_list[4], (D2,), jnp.float32), 0.099609375, 1.8984375).astype(jnp.bfloat16),
        "out_grad": centred(key_list[5], (TOKENS, D2), 0.015, 0.21875, ((0, 16), (1, 16))),
    }


def reference(token_ids, embed_small, proj_small, grow_op, norm_gain, out_grad):
    f32 = jnp.float32
    bf16 = jnp.bfloat16
    emb = jnp.take(embed_small, token_ids.astype(jnp.int32), axis=0)
    hidden = jnp.dot(emb, grow_op.T, preferred_element_type=f32)
    inv = lax.rsqrt(lax.optimization_barrier(jnp.mean(hidden * hidden, axis=1, keepdims=True)) + 1e-05)
    gain = norm_gain.astype(f32)
    normed = (hidden * inv * gain).astype(bf16)
    small_in = jnp.dot(normed, grow_op, preferred_element_type=f32).astype(bf16)
    small_out = jnp.dot(small_in, proj_small, preferred_element_type=f32).astype(bf16)
    back_small = jnp.dot(out_grad, grow_op, preferred_element_type=f32).astype(bf16)
    back_proj = jnp.dot(back_small, proj_small.T, preferred_element_type=f32).astype(bf16)
    normed_grad = jnp.dot(back_proj, grow_op.T, preferred_element_type=f32)
    scaled = normed_grad * gain
    stat = lax.optimization_barrier(jnp.mean(scaled * hidden, axis=1, keepdims=True))
    hidden_grad = (out_grad.astype(f32) + inv * scaled - hidden * inv * inv * inv * stat).astype(bf16)
    left = jnp.concatenate([hidden_grad.reshape(N_OP, TOK_DEV, D2), normed.reshape(N_OP, TOK_DEV, D2), out_grad.reshape(N_OP, TOK_DEV, D2)], axis=1)
    right = jnp.concatenate([emb.reshape(N_OP, TOK_DEV, D1), back_proj.reshape(N_OP, TOK_DEV, D1), small_out.reshape(N_OP, TOK_DEV, D1)], axis=1)

    def add_block(total, pair):
        block_left, block_right = pair
        partial_grad = lax.dot_general(block_left, block_right, (((0,), (0,)), ((), ())), preferred_element_type=f32)
        rounded = lax.optimization_barrier(partial_grad.astype(bf16))
        return (total + rounded.astype(f32), None)
    grad_op, _ = lax.scan(add_block, jnp.zeros((D2, D1), f32), (left, right))
    return grad_op
```

```python
import functools

import jax
import jax.numpy as jnp
import numpy as np
from jax import lax
from jax.experimental import pallas as pl
from jax.experimental.pallas import tpu as pltpu
from jax.sharding import Mesh, PartitionSpec as P

D2 = 6656
EPS = 1e-05
TOK = 128
ROWS = 416
COLS = 256
TAIL = 16
OP = ("z", "xl")
TP = ("y", "xh", "c")
YX = ("y", "xh")
F32 = jnp.float32
BF16 = jnp.bfloat16
NT = (((1,), (1,)), ((), ()))


def call(kernel, out_shape, *args, flops=0):
    smem = pl.BlockSpec(memory_space=pltpu.SMEM)
    vmem = pl.BlockSpec(memory_space=pltpu.VMEM)
    single = not isinstance(out_shape, (list, tuple))
    outs = [out_shape] if single else list(out_shape)
    nbytes = sum(int(np.prod(a.shape)) * a.dtype.itemsize for a in list(args) + outs)
    return pl.pallas_call(
        kernel,
        out_shape=out_shape,
        in_specs=[smem if a.dtype == jnp.int32 and a.ndim == 1 else vmem for a in args],
        out_specs=vmem if single else [vmem] * len(outs),
        compiler_params=pltpu.CompilerParams(vmem_limit_bytes=48 * 1024 * 1024),
        cost_estimate=pl.CostEstimate(flops=flops, bytes_accessed=nbytes, transcendentals=0),
    )(*args)


def sds(shape, dtype=BF16):
    return jax.ShapeDtypeStruct(shape, dtype)


def dot(a, b):
    return jnp.dot(a, b, preferred_element_type=F32)


def dot_nt(a, b):
    return lax.dot_general(a, b, NT, preferred_element_type=F32)


def swap(x, axis):
    return lax.ppermute(x, axis, [(0, 1), (1, 0)])


def exchange(x):
    return lax.all_to_all(x, YX, 0, 0, tiled=False)


def look_kernel(ids_ref, table_ref, out_ref):
    vocab = table_ref.shape[0]
    lanes = lax.broadcasted_iota(jnp.int32, (TOK, vocab), 1)
    table = table_ref[...]
    for o in range(ids_ref.shape[0]):
        hot = jnp.where(lanes == ids_ref[o], 1.0, 0.0).astype(BF16)
        out_ref[o] = dot(hot, table).astype(BF16)


def split_row(row):
    hi = row.astype(BF16)
    lo = (row - hi.astype(F32)).astype(BF16)
    return jnp.broadcast_to(jnp.concatenate([hi, lo], axis=1), (TAIL, COLS))


def join_row(tail):
    both = tail.astype(F32)[0:1]
    return both[:, :TOK] + both[:, TOK:]


def front_kernel(place, mine, other, grow, gain, og, hidden_ref, keep, send):
    c = place[0]
    hidden = jnp.zeros((TOK, ROWS), F32)
    for b in range(8):
        hidden += dot_nt(mine[b], grow[2 * b + c])
        hidden += dot_nt(other[b], grow[2 * b + 1 - c])
    hidden_ref[...] = hidden
    raw = (hidden * gain[...].astype(F32)).astype(BF16)
    square = jnp.sum(hidden * hidden, axis=1, keepdims=True)
    tail = split_row(jnp.broadcast_to(square, (TOK, TOK)).T[0:1])
    left = jnp.concatenate([raw, og[...]], axis=0)
    for b in range(8):
        for to, par in ((keep, c), (send, 1 - c)):
            to[b, : 2 * TOK] = dot(left, grow[2 * b + par]).astype(BF16)
            to[b, 2 * TOK :] = tail


def add_front_kernel(keep, recv, out):
    total = join_row(keep[0, 2 * TOK :]) + join_row(recv[0, 2 * TOK :])
    tail = split_row(total)
    for b in range(8):
        out[b, : 2 * TOK] = (
            keep[b, : 2 * TOK].astype(F32) + recv[b, : 2 * TOK].astype(F32)
        ).astype(BF16)
        out[b, 2 * TOK :] = tail


def mid_kernel(place, got, proj, small_in_ref, inv_ref, keep, send):
    c = place[0]
    both = got[0, : 2 * TOK].astype(F32)
    row = join_row(got[0, 2 * TOK :])
    for b in range(1, 8):
        both += got[b, : 2 * TOK].astype(F32)
        row += join_row(got[b, 2 * TOK :])
    square = jnp.broadcast_to(row, (TOK, TOK)).T
    inv = lax.rsqrt(square / D2 + EPS)
    inv_ref[...] = inv
    small_in_ref[...] = (both[:TOK] * inv[:, 0:1]).astype(BF16)
    back = both[TOK:].astype(BF16)
    for b in range(8):
        keep[b] = dot_nt(back, proj[2 * b + c]).astype(BF16)
        send[b] = dot_nt(back, proj[2 * b + 1 - c]).astype(BF16)


def add_mid_kernel(small_in, keep, recv, out):
    for b in range(8):
        out[b, :TOK] = small_in[...]
        out[b, TOK:] = (keep[b].astype(F32) + recv[b].astype(F32)).astype(BF16)


def out_kernel(place, got, other, proj, out):
    c = place[0]
    total = jnp.zeros((TOK, COLS), F32)
    back = jnp.zeros((TOK, COLS), F32)
    for b in range(8):
        total += dot(got[b, :TOK], proj[2 * b + c])
        total += dot(other[b], proj[2 * b + 1 - c])
        back += got[b, TOK:].astype(F32)
    total = total.astype(BF16)
    back = back.astype(BF16)
    for b in range(8):
        out[b, :TOK] = total
        out[b, TOK:] = back


def last_kernel(
    place, late, late_o, in_m, in_o, emb_m, emb_o, grow, hidden_ref, inv_ref, gain_ref, og_ref, *outs
):
    c = place[0]
    z = place[1]
    grad = jnp.zeros((TOK, ROWS), F32)
    stat = jnp.zeros((TOK, COLS), F32)
    for b in range(8):
        mine = late[b, TOK:]
        other = late_o[b, TOK:]
        grad += dot_nt(mine, grow[2 * b + c])
        grad += dot_nt(other, grow[2 * b + 1 - c])
        stat += mine.astype(F32) * in_m[b, :TOK].astype(F32)
        stat += other.astype(F32) * in_o[b].astype(F32)
    inv = inv_ref[:, 0:1]
    mean = jnp.sum(stat, axis=1, keepdims=True) / inv / D2
    gain = gain_ref[...].astype(F32)
    hidden = hidden_ref[...]
    og = og_ref[...]
    scaled = grad * gain
    hidden_grad = og.astype(F32) + inv * scaled - hidden * inv * inv * inv * mean
    normed = hidden * inv * gain
    left = jnp.concatenate([hidden_grad, normed, og.astype(F32)], axis=0).T.astype(BF16)
    for d in range(8):
        b = lax.rem(z + d, 8)
        for par, emb, tail in ((c, emb_m, late), (1 - c, emb_o, late_o)):
            right = jnp.concatenate([emb[b], tail[b, TOK:], tail[b, :TOK]], axis=0)
            outs[d][par] = dot(left, right).astype(BF16)


def shards(token_ids, embed, proj, grow_op, norm_gain, out_grad):
    c = lax.axis_index("c")
    z = lax.axis_index("z")
    xl = lax.axis_index("xl")
    place = jnp.stack([c, z]).astype(jnp.int32)
    gain = norm_gain.reshape(1, ROWS)
    proj = proj.reshape(16, COLS, COLS)

    with jax.named_scope("gather_operator"):
        grow_other = swap(grow_op, "xl")
        pair = jnp.stack(
            [jnp.where(xl == 0, grow_op, grow_other), jnp.where(xl == 0, grow_other, grow_op)]
        )
        grow = lax.all_gather(pair, "z", axis=0, tiled=True)

    with jax.named_scope("embedding"):
        ids = lax.all_to_all(
            jnp.broadcast_to(token_ids.reshape(1, 1, TOK), (16, 1, TOK)), OP, 0, 0, tiled=False
        )
        local = (ids - (z * 2 + xl) * embed.shape[0]).reshape(16, TOK, 1)
        rows = call(
            look_kernel,
            sds((16, TOK, COLS)),
            local,
            embed,
            flops=2 * 16 * TOK * embed.shape[0] * COLS,
        )
        rows = lax.all_to_all(rows, OP, 0, 0, tiled=False)
        emb_part = jnp.sum(rows.astype(F32), axis=0).astype(BF16)
        emb_mine = exchange(jnp.broadcast_to(emb_part[None], (8, TOK, COLS)))
        emb_other = swap(emb_mine, "c")

    work = 2 * TOK * ROWS * 4096
    with jax.named_scope("front"):
        hidden, keep, send = call(
            front_kernel,
            [sds((TOK, ROWS), F32), sds((8, 272, COLS)), sds((8, 272, COLS))],
            place,
            emb_mine,
            emb_other,
            grow,
            gain,
            out_grad,
            flops=3 * work,
        )
        got = exchange(call(add_front_kernel, sds((8, 272, COLS)), keep, swap(send, "c")))

    with jax.named_scope("mid"):
        small_in, inv, keep, send = call(
            mid_kernel,
            [sds((TOK, COLS)), sds((TOK, TOK), F32), sds((8, TOK, COLS)), sds((8, TOK, COLS))],
            place,
            got,
            proj,
            flops=2 * TOK * COLS * 4096,
        )
        got = exchange(
            call(add_mid_kernel, sds((8, 2 * TOK, COLS)), small_in, keep, swap(send, "c"))
        )
        in_other = swap(got[:, :TOK], "c")

    with jax.named_scope("out"):
        late = exchange(
            call(
                out_kernel,
                sds((8, 2 * TOK, COLS)),
                place,
                got,
                in_other,
                proj,
                flops=2 * TOK * COLS * 4096,
            )
        )
        late_other = swap(late, "c")

    with jax.named_scope("last"):
        x = call(
            last_kernel,
            [sds((2, ROWS, COLS))] * 8,
            place,
            late,
            late_other,
            got,
            in_other,
            emb_mine,
            emb_other,
            grow,
            hidden,
            inv,
            gain,
            out_grad,
            flops=4 * work,
        )

    def up(v):
        return lax.ppermute(v, "z", [(i, (i + 1) % 8) for i in range(8)])

    def down(v):
        return lax.ppermute(v, "z", [(i, (i - 1) % 8) for i in range(8)])

    def add(a, b):
        return (a.astype(F32) + b.astype(F32)).astype(BF16)

    with jax.named_scope("scatter"):
        u0 = up(x[4][0])
        d1 = down(x[4][1])
        u1 = up(x[3][1])
        d0 = down(x[5][0])
        u0 = up(add(u0, x[3][0]))
        d1 = down(add(d1, x[5][1]))
        u1 = up(add(u1, x[2][1]))
        d0 = down(add(d0, x[6][0]))
        u0 = up(add(u0, x[2][0]))
        d1 = down(add(d1, x[6][1]))
        u1 = up(add(u1, x[1][1]))
        d0 = down(add(d0, x[7][0]))
        u0 = up(add(u0, x[1][0]))
        d1 = down(add(d1, x[7][1]))
        y0 = x[0][0].astype(F32) + d0.astype(F32) + u0.astype(F32)
        y1 = x[0][1].astype(F32) + u1.astype(F32) + d1.astype(F32)
        theirs = swap(jnp.where(xl == 0, y1, y0).astype(BF16), "xl")
        return jnp.where(xl == 0, y0, y1) + theirs.astype(F32)


def solution(mesh):
    fine = Mesh(mesh.devices.reshape(8, 2, 4, 2, 2), ("z", "xl", "y", "xh", "c"))
    in_specs = (P(OP), P(OP, TP), P(None, TP), P(TP, OP), P(TP), P(OP, TP))
    return jax.shard_map(shards, mesh=fine, in_specs=in_specs, out_specs=P(TP, OP), check_vma=False)
```

```python
import functools

import jax
import jax.numpy as jnp
import numpy as np
from jax import lax
from jax.experimental import pallas as pl
from jax.experimental.pallas import tpu as pltpu
from jax.sharding import Mesh, PartitionSpec as P

D2 = 6656
EPS = 1e-05
TOK = 128
ROWS = 416
COLS = 256
TAIL = 16
OP = ("z", "xl")
TP = ("y", "xh", "c")
YX = ("y", "xh")
F32 = jnp.float32
BF16 = jnp.bfloat16
NT = (((1,), (1,)), ((), ()))


def call(kernel, out_shape, *args, flops=0):
    smem = pl.BlockSpec(memory_space=pltpu.SMEM)
    vmem = pl.BlockSpec(memory_space=pltpu.VMEM)
    single = not isinstance(out_shape, (list, tuple))
    outs = [out_shape] if single else list(out_shape)
    nbytes = sum(int(np.prod(a.shape)) * a.dtype.itemsize for a in list(args) + outs)
    return pl.pallas_call(
        kernel,
        out_shape=out_shape,
        in_specs=[smem if a.dtype == jnp.int32 and a.ndim == 1 else vmem for a in args],
        out_specs=vmem if single else [vmem] * len(outs),
        compiler_params=pltpu.CompilerParams(vmem_limit_bytes=48 * 1024 * 1024),
        cost_estimate=pl.CostEstimate(flops=flops, bytes_accessed=nbytes, transcendentals=0),
    )(*args)


def sds(shape, dtype=BF16):
    return jax.ShapeDtypeStruct(shape, dtype)


def dot(a, b):
    return jnp.dot(a, b, preferred_element_type=F32)


def dot_nt(a, b):
    return lax.dot_general(a, b, NT, preferred_element_type=F32)


def swap(x, axis):
    return lax.ppermute(x, axis, [(0, 1), (1, 0)])


def exchange(x):
    return lax.all_to_all(x, YX, 0, 0, tiled=False)


def look_kernel(ids_ref, table_ref, out_ref):
    vocab = table_ref.shape[0]
    lanes = lax.broadcasted_iota(jnp.int32, (TOK, vocab), 1)
    table = table_ref[...]
    for o in range(ids_ref.shape[0]):
        hot = jnp.where(lanes == ids_ref[o], 1.0, 0.0).astype(BF16)
        out_ref[o] = dot(hot, table).astype(BF16)


def split_row(row):
    hi = row.astype(BF16)
    lo = (row - hi.astype(F32)).astype(BF16)
    return jnp.broadcast_to(jnp.concatenate([hi, lo], axis=1), (TAIL, COLS))


def join_row(tail):
    both = tail.astype(F32)[0:1]
    return both[:, :TOK] + both[:, TOK:]


def back_kernel(place, og, grow, keep, send):
    c = place[0]
    left = jnp.concatenate([og[c], og[1 - c]], axis=0)
    for b in range(8):
        part = dot(left, grow[b]).astype(BF16)
        keep[b] = part[:TOK]
        send[b] = part[TOK:]


def first_kernel(emb, keep, recv, out):
    for b in range(8):
        out[b, :TOK] = emb[...]
        out[b, TOK:] = (keep[b].astype(F32) + recv[b].astype(F32)).astype(BF16)


def sum_kernel(got, out):
    total = got[0, TOK:].astype(F32)
    for b in range(1, 8):
        total += got[b, TOK:].astype(F32)
    out[...] = total.astype(BF16)


def hidden_kernel(place, got, other, grow, part, sent):
    c = place[0]
    total = jnp.zeros((2 * TOK, ROWS), F32)
    for b in range(8):
        total += dot_nt(jnp.concatenate([got[b, :TOK], other[b]], axis=0), grow[b])
    part[c] = total[:TOK]
    part[1 - c] = total[TOK:]
    sent[c] = total[:TOK].astype(BF16)
    sent[1 - c] = total[TOK:].astype(BF16)


def proj_kernel(place, back, proj, keep, send):
    c = place[0]
    for b in range(8):
        keep[b] = dot_nt(back[...], proj[2 * b + c]).astype(BF16)
        send[b] = dot_nt(back[...], proj[2 * b + 1 - c]).astype(BF16)


def in_kernel(place, part, peer, gain, grow, hidden_ref, keep, send):
    c = place[0]
    left = []
    for t, to in ((c, keep), (1 - c, send)):
        hidden = part[t] + peer[t].astype(F32)
        hidden_ref[t] = hidden
        left.append((hidden * gain[...].astype(F32)).astype(BF16))
        square = jnp.sum(hidden * hidden, axis=1, keepdims=True)
        tail = split_row(jnp.broadcast_to(square, (TOK, TOK)).T[0:1])
        for b in range(8):
            to[b, TOK:] = tail
    left = jnp.concatenate(left, axis=0)
    for b in range(8):
        both = dot(left, grow[b]).astype(BF16)
        keep[b, :TOK] = both[:TOK]
        send[b, :TOK] = both[TOK:]


def second_kernel(keep, recv, proj_keep, proj_recv, out):
    tail = split_row(join_row(keep[0, TOK:]) + join_row(recv[0, TOK:]))
    for b in range(8):
        out[b, :TOK] = (keep[b, :TOK].astype(F32) + recv[b, :TOK].astype(F32)).astype(BF16)
        out[b, TOK : 2 * TOK] = (proj_keep[b].astype(F32) + proj_recv[b].astype(F32)).astype(BF16)
        out[b, 2 * TOK :] = tail


def mid_kernel(got, out, inv_ref):
    both = got[0, : 2 * TOK].astype(F32)
    row = join_row(got[0, 2 * TOK :])
    for b in range(1, 8):
        both += got[b, : 2 * TOK].astype(F32)
        row += join_row(got[b, 2 * TOK :])
    inv = lax.rsqrt(jnp.broadcast_to(row, (TOK, TOK)).T / D2 + EPS)
    inv_ref[...] = inv
    out[:TOK] = (both[:TOK] * inv[:, 0:1]).astype(BF16)
    out[TOK:] = both[TOK:].astype(BF16)


def third_kernel(before, after, out):
    stat = jnp.sum(before[TOK:].astype(F32) * after[:TOK].astype(F32), axis=1, keepdims=True)
    tail = split_row(jnp.broadcast_to(stat, (TOK, TOK)).T[0:1])
    for b in range(8):
        out[b, : 2 * TOK] = after[...]
        out[b, 2 * TOK :] = tail


def out_kernel(place, got, other, proj, out, stat_ref):
    c = place[0]
    total = jnp.zeros((TOK, COLS), F32)
    stat = jnp.zeros((1, TOK), F32)
    for b in range(8):
        total += dot(got[b, :TOK], proj[2 * b + c])
        total += dot(other[b, :TOK], proj[2 * b + 1 - c])
        stat += join_row(got[b, 2 * TOK :]) + join_row(other[b, 2 * TOK :])
    out[...] = total.astype(BF16)
    stat_ref[...] = jnp.broadcast_to(stat, (TOK, TOK)).T


def grad_kernel(place, got, other, grow, part, sent):
    c = place[0]
    total = jnp.zeros((2 * TOK, ROWS), F32)
    for b in range(8):
        total += dot_nt(
            jnp.concatenate([got[b, TOK : 2 * TOK], other[b, TOK : 2 * TOK]], axis=0), grow[b]
        )
    part[c] = total[:TOK]
    part[1 - c] = total[TOK:]
    sent[c] = total[:TOK].astype(BF16)
    sent[1 - c] = total[TOK:].astype(BF16)


def left_kernel(place, part, peer, hidden_ref, inv_c, inv_o, stat_own, stat_peer, gain_ref, og_ref, out):
    c = place[0]
    xl = place[2]
    gain = gain_ref[...].astype(F32)
    hidden_grads, normeds, ogs = [], [], []
    for t, inv_ref in ((c, inv_c), (1 - c, inv_o)):
        inv = inv_ref[:, 0:1]
        stat = jnp.where(t == xl, stat_own[:, 0:1], stat_peer[:, 0:1])
        mean = stat / inv / D2
        hidden = hidden_ref[t]
        og = og_ref[t].astype(F32)
        scaled = (part[t] + peer[t].astype(F32)) * gain
        hidden_grads.append(og + inv * scaled - hidden * inv * inv * inv * mean)
        normeds.append(hidden * inv * gain)
        ogs.append(og)
    out[...] = jnp.concatenate(hidden_grads + normeds + ogs, axis=0).T.astype(BF16)


def last_kernel(place, left_ref, emb_m, emb_o, got, other, late, late_o, *outs):
    z = place[1]
    left = left_ref[...]
    half = ROWS // 2
    for d in (4, 3, 5, 2, 6, 1, 7, 0):
        b = lax.rem(z + d, 8)
        right = jnp.concatenate(
            [
                emb_m[b, :TOK],
                emb_o[b],
                got[b, TOK : 2 * TOK],
                other[b, TOK : 2 * TOK],
                late[b],
                late_o[b],
            ],
            axis=0,
        )
        total = dot(left, right).astype(BF16)
        outs[2 * d][...] = total[:half]
        outs[2 * d + 1][...] = total[half:]


def turn(x):
    return lax.ppermute(x, ("xl", "c"), [(0, 0), (1, 2), (2, 1), (3, 3)])


def shards(token_ids, embed, proj, grow_op, norm_gain, out_grad):
    c = lax.axis_index("c")
    z = lax.axis_index("z")
    xl = lax.axis_index("xl")
    place = jnp.stack([c, z, xl]).astype(jnp.int32)
    gain = norm_gain.reshape(1, ROWS)
    proj = proj.reshape(16, COLS, COLS)
    block = sds((8, TOK, COLS))
    work = 2 * TOK * ROWS * 4096

    with jax.named_scope("embedding"):
        ids = lax.all_to_all(
            jnp.broadcast_to(token_ids.reshape(1, 1, TOK), (16, 1, TOK)), OP, 0, 0, tiled=False
        )
        local = (ids - (z * 2 + xl) * embed.shape[0]).reshape(16, TOK, 1)
        rows = call(
            look_kernel,
            sds((16, TOK, COLS)),
            local,
            embed,
            flops=2 * 16 * TOK * embed.shape[0] * COLS,
        )
        rows = lax.all_to_all(rows, OP, 0, 0, tiled=False)
        emb_part = turn(jnp.sum(rows.astype(F32), axis=0).astype(BF16))

    with jax.named_scope("operator"):
        grow = lax.all_gather(grow_op, "z", axis=0, tiled=False)
        og_peer = swap(out_grad, "xl")
        og = jnp.stack([jnp.where(xl == 0, out_grad, og_peer), jnp.where(xl == 0, og_peer, out_grad)])
        keep, send = call(back_kernel, [block, block], place, og, grow, flops=work)
        recv = swap(send, "c")

    with jax.named_scope("first"):
        emb = exchange(call(first_kernel, sds((8, 2 * TOK, COLS)), emb_part, keep, recv))
        emb_other = swap(emb[:, :TOK], "c")
        back = turn(call(sum_kernel, sds((TOK, COLS)), emb))

    with jax.named_scope("hidden"):
        pair = sds((2, TOK, ROWS), F32)
        pair_sent = sds((2, TOK, ROWS))
        part, sent = call(
            hidden_kernel, [pair, pair_sent], place, emb, emb_other, grow, flops=work
        )
        peer = swap(sent, "xl")
        proj_keep, send = call(
            proj_kernel, [block, block], place, back, proj, flops=2 * TOK * COLS * 4096
        )
        proj_recv = swap(send, "c")
        longer = sds((8, TOK + TAIL, COLS))
        hidden, keep, send = call(
            in_kernel, [pair, longer, longer], place, part, peer, gain, grow, flops=work
        )

    with jax.named_scope("second"):
        got = exchange(
            call(
                second_kernel,
                sds((8, 2 * TOK + TAIL, COLS)),
                keep,
                swap(send, "c"),
                proj_keep,
                proj_recv,
            )
        )
        before, inv = call(mid_kernel, [sds((2 * TOK, COLS)), sds((TOK, TOK), F32)], got)
        after = turn(before)
        inv_other = swap(inv, "c")

    with jax.named_scope("third"):
        got = exchange(call(third_kernel, sds((8, 2 * TOK + TAIL, COLS)), before, after))
        other = swap(got, "c")
        out, stat = call(
            out_kernel,
            [sds((TOK, COLS)), sds((TOK, TOK), F32)],
            place,
            got,
            other,
            proj,
            flops=2 * TOK * COLS * 4096,
        )
        out = turn(out)
        stat_peer = swap(stat, "xl")
        part, sent = call(grad_kernel, [pair, pair_sent], place, got, other, grow, flops=work)
        peer = swap(sent, "xl")

    with jax.named_scope("fourth"):
        late = exchange(jnp.broadcast_to(out[None], (8, TOK, COLS)))
        late_other = swap(late, "c")
        left = call(
            left_kernel,
            sds((ROWS, 6 * TOK)),
            place,
            part,
            peer,
            hidden,
            inv,
            inv_other,
            stat,
            stat_peer,
            gain,
            og,
        )
        x = call(
            last_kernel,
            [sds((ROWS // 2, COLS))] * 16,
            place,
            left,
            emb,
            emb_other,
            got,
            other,
            late,
            late_other,
            flops=3 * work,
        )

    def up(v):
        return lax.ppermute(v, "z", [(i, (i + 1) % 8) for i in range(8)])

    def down(v):
        return lax.ppermute(v, "z", [(i, (i - 1) % 8) for i in range(8)])

    def add(a, b):
        return (a.astype(F32) + b.astype(F32)).astype(BF16)

    with jax.named_scope("scatter"):
        x = [x[2 * d : 2 * d + 2] for d in range(8)]
        u0 = up(x[4][0])
        d1 = down(x[4][1])
        u1 = up(x[3][1])
        d0 = down(x[5][0])
        u0 = up(add(u0, x[3][0]))
        d1 = down(add(d1, x[5][1]))
        u1 = up(add(u1, x[2][1]))
        d0 = down(add(d0, x[6][0]))
        u0 = up(add(u0, x[2][0]))
        d1 = down(add(d1, x[6][1]))
        u1 = up(add(u1, x[1][1]))
        d0 = down(add(d0, x[7][0]))
        u0 = up(add(u0, x[1][0]))
        d1 = down(add(d1, x[7][1]))
        y0 = x[0][0].astype(F32) + d0.astype(F32) + u0.astype(F32)
        y1 = x[0][1].astype(F32) + u1.astype(F32) + d1.astype(F32)
        return jnp.concatenate([y0, y1], axis=0)


def solution(mesh):
    fine = Mesh(mesh.devices.reshape(8, 2, 4, 2, 2), ("z", "xl", "y", "xh", "c"))
    in_specs = (P(OP), P(OP, TP), P(None, TP), P(TP, OP), P(TP), P(OP, TP))
    return jax.shard_map(shards, mesh=fine, in_specs=in_specs, out_specs=P(TP, OP), check_vma=False)
```

```python
import functools

import jax
import jax.numpy as jnp
import numpy as np
from jax import lax
from jax.experimental import pallas as pl
from jax.experimental.pallas import tpu as pltpu
from jax.sharding import Mesh, PartitionSpec as P

D2 = 6656
EPS = 1e-05
TOK = 128
ROWS = 416
COLS = 256
TAIL = 16
SLOTS = 48
OP = ("z", "xl")
TP = ("y", "xh", "c")
YX = ("y", "xh")
F32 = jnp.float32
BF16 = jnp.bfloat16
NT = (((1,), (1,)), ((), ()))


def call(kernel, out_shape, *args, flops=0):
    smem = pl.BlockSpec(memory_space=pltpu.SMEM)
    vmem = pl.BlockSpec(memory_space=pltpu.VMEM)
    single = not isinstance(out_shape, (list, tuple))
    outs = [out_shape] if single else list(out_shape)
    nbytes = sum(int(np.prod(a.shape)) * a.dtype.itemsize for a in list(args) + outs)
    return pl.pallas_call(
        kernel,
        out_shape=out_shape,
        in_specs=[smem if a.dtype == jnp.int32 and a.ndim == 1 else vmem for a in args],
        out_specs=vmem if single else [vmem] * len(outs),
        compiler_params=pltpu.CompilerParams(vmem_limit_bytes=48 * 1024 * 1024),
        cost_estimate=pl.CostEstimate(flops=flops, bytes_accessed=nbytes, transcendentals=0),
    )(*args)


def sds(shape, dtype=BF16):
    return jax.ShapeDtypeStruct(shape, dtype)


def dot(a, b):
    return jnp.dot(a, b, preferred_element_type=F32)


def dot_nt(a, b):
    return lax.dot_general(a, b, NT, preferred_element_type=F32)


def swap(x, axis):
    return lax.ppermute(x, axis, [(0, 1), (1, 0)])


def exchange(x):
    return lax.all_to_all(x, YX, 0, 0, tiled=False)


def ranks(inside, base):
    before = lax.broadcasted_iota(jnp.int32, (TOK, TOK), 0)
    after = lax.broadcasted_iota(jnp.int32, (TOK, TOK), 1)
    marks = jnp.where(inside, 1.0, 0.0).astype(BF16)
    rank = dot(marks, jnp.where(before < after, 1.0, 0.0).astype(BF16))
    return jnp.where(inside, rank - base, -1.0)


def look_kernel(at, ids_ref, table_ref, out_ref, most_ref):
    vocab = table_ref.shape[0]
    most = jnp.zeros((16, 1), F32)
    for v in range(16):
        here = (ids_ref[...] >= v * vocab) & (ids_ref[...] < (v + 1) * vocab)
        most = jnp.maximum(most, jnp.sum(jnp.where(here, 1.0, 0.0), axis=1, keepdims=True))
    most_ref[...] = jnp.broadcast_to(jnp.max(most, axis=0, keepdims=True), (8, TOK))
    ids = ids_ref[...] - at[0]
    key = ranks((ids >= 0) & (ids < vocab), (at[1] * SLOTS).astype(F32))
    ids = ids.astype(F32) + 1.0
    slot = lax.broadcasted_iota(jnp.int32, (SLOTS, TOK), 0).astype(F32)
    lanes = lax.broadcasted_iota(jnp.int32, (4 * SLOTS, vocab), 1).astype(F32)
    table = table_ref[...]
    for g in range(4):
        rows = []
        for o in range(4 * g, 4 * g + 4):
            hit = jnp.where(slot == key[o : o + 1], ids[o : o + 1], 0.0)
            rows.append(jnp.sum(hit, axis=1, keepdims=True) - 1.0)
        hot = jnp.where(lanes == jnp.concatenate(rows, axis=0), 1.0, 0.0).astype(BF16)
        found = dot(hot, table).astype(BF16)
        for o in range(4):
            out_ref[4 * g + o] = found[o * SLOTS : (o + 1) * SLOTS]


def place_kernel(vocab, at, ids_ref, rows_ref, out_ref):
    ids = jnp.broadcast_to(ids_ref[...], (16, TOK))
    first = lax.broadcasted_iota(jnp.int32, (16, TOK), 0) * vocab
    key = ranks((ids >= first) & (ids < first + vocab), (at[1] * SLOTS).astype(F32))
    slot = lax.broadcasted_iota(jnp.int32, (SLOTS, TOK), 0).astype(F32)
    hits = [jnp.where(slot == key[v : v + 1], 1.0, 0.0) for v in range(16)]
    hits = jnp.concatenate(hits, axis=0).T.astype(BF16)
    rows = jnp.concatenate([rows_ref[v] for v in range(16)], axis=0)
    out_ref[...] = dot(hits, rows).astype(BF16)


def split_row(row):
    hi = row.astype(BF16)
    lo = (row - hi.astype(F32)).astype(BF16)
    return jnp.broadcast_to(jnp.concatenate([hi, lo], axis=1), (TAIL, COLS))


def join_row(tail):
    both = tail.astype(F32)[0:1]
    return both[:, :TOK] + both[:, TOK:]


def back_kernel(place, og, grow, keep, send):
    c = place[0]
    left = jnp.concatenate([og[c], og[1 - c]], axis=0)
    for b in range(8):
        part = dot(left, grow[b]).astype(BF16)
        keep[b] = part[:TOK]
        send[b] = part[TOK:]


def first_kernel(emb, keep, recv, out):
    for b in range(8):
        out[b, :TOK] = emb[...]
        out[b, TOK:] = (keep[b].astype(F32) + recv[b].astype(F32)).astype(BF16)


def sum_kernel(got, out):
    total = got[0, TOK:].astype(F32)
    for b in range(1, 8):
        total += got[b, TOK:].astype(F32)
    out[...] = total.astype(BF16)


def hidden_kernel(place, got, other, grow, part, sent):
    c = place[0]
    total = jnp.zeros((2 * TOK, ROWS), F32)
    for b in range(8):
        total += dot_nt(jnp.concatenate([got[b, :TOK], other[b]], axis=0), grow[b])
    part[c] = total[:TOK]
    part[1 - c] = total[TOK:]
    sent[c] = total[:TOK].astype(BF16)
    sent[1 - c] = total[TOK:].astype(BF16)


def proj_kernel(place, back, proj, keep, send):
    c = place[0]
    for b in range(8):
        keep[b] = dot_nt(back[...], proj[2 * b + c]).astype(BF16)
        send[b] = dot_nt(back[...], proj[2 * b + 1 - c]).astype(BF16)


def in_kernel(place, part, peer, gain, grow, hidden_ref, keep, send):
    c = place[0]
    left = []
    for t, to in ((c, keep), (1 - c, send)):
        hidden = part[t] + peer[t].astype(F32)
        hidden_ref[t] = hidden
        left.append((hidden * gain[...].astype(F32)).astype(BF16))
        square = jnp.sum(hidden * hidden, axis=1, keepdims=True)
        tail = split_row(jnp.broadcast_to(square, (TOK, TOK)).T[0:1])
        for b in range(8):
            to[b, TOK:] = tail
    left = jnp.concatenate(left, axis=0)
    for b in range(8):
        both = dot(left, grow[b]).astype(BF16)
        keep[b, :TOK] = both[:TOK]
        send[b, :TOK] = both[TOK:]


def second_kernel(keep, recv, proj_keep, proj_recv, out):
    tail = split_row(join_row(keep[0, TOK:]) + join_row(recv[0, TOK:]))
    for b in range(8):
        out[b, :TOK] = (keep[b, :TOK].astype(F32) + recv[b, :TOK].astype(F32)).astype(BF16)
        out[b, TOK : 2 * TOK] = (proj_keep[b].astype(F32) + proj_recv[b].astype(F32)).astype(BF16)
        out[b, 2 * TOK :] = tail


def mid_kernel(got, out, inv_ref):
    both = got[0, : 2 * TOK].astype(F32)
    row = join_row(got[0, 2 * TOK :])
    for b in range(1, 8):
        both += got[b, : 2 * TOK].astype(F32)
        row += join_row(got[b, 2 * TOK :])
    inv = lax.rsqrt(jnp.broadcast_to(row, (TOK, TOK)).T / D2 + EPS)
    inv_ref[...] = inv
    out[:TOK] = (both[:TOK] * inv[:, 0:1]).astype(BF16)
    out[TOK:] = both[TOK:].astype(BF16)


def third_kernel(before, after, out):
    stat = jnp.sum(before[TOK:].astype(F32) * after[:TOK].astype(F32), axis=1, keepdims=True)
    tail = split_row(jnp.broadcast_to(stat, (TOK, TOK)).T[0:1])
    for b in range(8):
        out[b, : 2 * TOK] = after[...]
        out[b, 2 * TOK :] = tail


def out_kernel(place, got, other, proj, out, stat_ref):
    c = place[0]
    total = jnp.zeros((TOK, COLS), F32)
    stat = jnp.zeros((1, TOK), F32)
    for b in range(8):
        total += dot(got[b, :TOK], proj[2 * b + c])
        total += dot(other[b, :TOK], proj[2 * b + 1 - c])
        stat += join_row(got[b, 2 * TOK :]) + join_row(other[b, 2 * TOK :])
    out[...] = total.astype(BF16)
    stat_ref[...] = jnp.broadcast_to(stat, (TOK, TOK)).T


def grad_kernel(place, got, other, grow, part, sent):
    c = place[0]
    total = jnp.zeros((2 * TOK, ROWS), F32)
    for b in range(8):
        total += dot_nt(
            jnp.concatenate([got[b, TOK : 2 * TOK], other[b, TOK : 2 * TOK]], axis=0), grow[b]
        )
    part[c] = total[:TOK]
    part[1 - c] = total[TOK:]
    sent[c] = total[:TOK].astype(BF16)
    sent[1 - c] = total[TOK:].astype(BF16)


def left_kernel(place, part, peer, hidden_ref, inv_c, inv_o, stat_own, stat_peer, gain_ref, og_ref, out):
    c = place[0]
    xl = place[2]
    gain = gain_ref[...].astype(F32)
    hidden_grads, normeds, ogs = [], [], []
    for t, inv_ref in ((c, inv_c), (1 - c, inv_o)):
        inv = inv_ref[:, 0:1]
        stat = jnp.where(t == xl, stat_own[:, 0:1], stat_peer[:, 0:1])
        mean = stat / inv / D2
        hidden = hidden_ref[t]
        og = og_ref[t].astype(F32)
        scaled = (part[t] + peer[t].astype(F32)) * gain
        hidden_grads.append(og + inv * scaled - hidden * inv * inv * inv * mean)
        normeds.append(hidden * inv * gain)
        ogs.append(og)
    out[...] = jnp.concatenate(hidden_grads + normeds + ogs, axis=0).T.astype(BF16)


def last_kernel(place, left_ref, emb_m, emb_o, got, other, late, late_o, *outs):
    z = place[1]
    left = left_ref[...]
    half = ROWS // 2
    for d in (4, 3, 5, 2, 6, 1, 7, 0):
        b = lax.rem(z + d, 8)
        right = jnp.concatenate(
            [
                emb_m[b, :TOK],
                emb_o[b],
                got[b, TOK : 2 * TOK],
                other[b, TOK : 2 * TOK],
                late[b],
                late_o[b],
            ],
            axis=0,
        )
        total = dot(left, right).astype(BF16)
        outs[2 * d][...] = total[:half]
        outs[2 * d + 1][...] = total[half:]


def end_kernel(x0, x1, u0, d0, u1, d1, out):
    half = ROWS // 2
    out[:half] = x0[...].astype(F32) + u0[...].astype(F32) + d0[...].astype(F32)
    out[half:] = x1[...].astype(F32) + u1[...].astype(F32) + d1[...].astype(F32)


def turn(x):
    return lax.ppermute(x, ("xl", "c"), [(0, 0), (1, 2), (2, 1), (3, 3)])


def shards(token_ids, embed, proj, grow_op, norm_gain, out_grad):
    c = lax.axis_index("c")
    z = lax.axis_index("z")
    xl = lax.axis_index("xl")
    place = jnp.stack([c, z, xl]).astype(jnp.int32)
    gain = norm_gain.reshape(1, ROWS)
    proj = proj.reshape(16, COLS, COLS)
    block = sds((8, TOK, COLS))
    work = 2 * TOK * ROWS * 4096

    with jax.named_scope("embedding"):
        ids = lax.all_to_all(
            jnp.broadcast_to(token_ids.reshape(1, 1, TOK), (16, 1, TOK)), OP, 0, 0, tiled=False
        )
        ids = ids.reshape(16, TOK)
        vocab = embed.shape[0]
        first = (z * 2 + xl) * vocab
        own = token_ids.reshape(1, TOK)

        def one(k):
            at = jnp.stack([first, k]).astype(jnp.int32)
            rows, most = call(
                look_kernel,
                [sds((16, SLOTS, COLS)), sds((8, TOK), F32)],
                at,
                ids,
                embed,
                flops=2 * 16 * SLOTS * vocab * COLS,
            )
            rows = lax.all_to_all(rows, OP, 0, 0, tiled=False)
            part = call(
                functools.partial(place_kernel, vocab),
                sds((TOK, COLS)),
                at,
                own,
                rows,
                flops=2 * 16 * SLOTS * TOK * COLS,
            )
            return part, most[0, 0]

        found, most = one(jnp.int32(0))
        found = lax.while_loop(
            lambda state: (state[0] * SLOTS).astype(F32) < most,
            lambda state: (state[0] + 1, state[1] + one(state[0])[0]),
            (jnp.int32(1), found),
        )
        emb_part = turn(found[1])

    with jax.named_scope("operator"):
        grow = lax.all_gather(grow_op, "z", axis=0, tiled=False)
        og_peer = swap(out_grad, "xl")
        og = jnp.stack([jnp.where(xl == 0, out_grad, og_peer), jnp.where(xl == 0, og_peer, out_grad)])
        og, emb_part = lax.optimization_barrier((og, emb_part))
        keep, send = call(back_kernel, [block, block], place, og, grow, flops=work)
        recv = swap(send, "c")

    with jax.named_scope("first"):
        emb = exchange(call(first_kernel, sds((8, 2 * TOK, COLS)), emb_part, keep, recv))
        emb_other = swap(emb[:, :TOK], "c")
        back = call(sum_kernel, sds((TOK, COLS)), emb)
        emb, back = lax.optimization_barrier((emb, back))
        back = turn(back)

    with jax.named_scope("hidden"):
        pair = sds((2, TOK, ROWS), F32)
        pair_sent = sds((2, TOK, ROWS))
        part, sent = call(
            hidden_kernel, [pair, pair_sent], place, emb, emb_other, grow, flops=work
        )
        peer = swap(sent, "xl")
        proj_keep, send = call(
            proj_kernel, [block, block], place, back, proj, flops=2 * TOK * COLS * 4096
        )
        part, peer, send = lax.optimization_barrier((part, peer, send))
        proj_recv = swap(send, "c")
        longer = sds((8, TOK + TAIL, COLS))
        hidden, keep, send = call(
            in_kernel, [pair, longer, longer], place, part, peer, gain, grow, flops=work
        )

    with jax.named_scope("second"):
        got = exchange(
            call(
                second_kernel,
                sds((8, 2 * TOK + TAIL, COLS)),
                keep,
                swap(send, "c"),
                proj_keep,
                proj_recv,
            )
        )
        before, inv = call(mid_kernel, [sds((2 * TOK, COLS)), sds((TOK, TOK), F32)], got)
        after, inv_other = lax.optimization_barrier((turn(before), swap(inv, "c")))

    with jax.named_scope("third"):
        got = exchange(call(third_kernel, sds((8, 2 * TOK + TAIL, COLS)), before, after))
        other = swap(got, "c")
        part, sent = call(grad_kernel, [pair, pair_sent], place, got, other, grow, flops=work)
        got_in, sent = lax.optimization_barrier((got, sent))
        peer = swap(sent, "xl")
        out, stat = call(
            out_kernel,
            [sds((TOK, COLS)), sds((TOK, TOK), F32)],
            place,
            got_in,
            other,
            proj,
            flops=2 * TOK * COLS * 4096,
        )
        out, stat_peer, peer = lax.optimization_barrier((turn(out), swap(stat, "xl"), peer))

    with jax.named_scope("fourth"):
        late = exchange(jnp.broadcast_to(out[None], (8, TOK, COLS)))
        late_other = swap(late, "c")
        left = call(
            left_kernel,
            sds((ROWS, 6 * TOK)),
            place,
            part,
            peer,
            hidden,
            inv,
            inv_other,
            stat,
            stat_peer,
            gain,
            og,
        )
        x = call(
            last_kernel,
            [sds((ROWS // 2, COLS))] * 16,
            place,
            left,
            emb,
            emb_other,
            got,
            other,
            late,
            late_other,
            flops=3 * work,
        )

    def up(v):
        return lax.ppermute(v, "z", [(i, (i + 1) % 8) for i in range(8)])

    def down(v):
        return lax.ppermute(v, "z", [(i, (i - 1) % 8) for i in range(8)])

    def add(a, b):
        return (a.astype(F32) + b.astype(F32)).astype(BF16)

    with jax.named_scope("scatter"):
        x = [x[2 * d : 2 * d + 2] for d in range(8)]
        u0 = up(x[4][0])
        d1 = down(x[4][1])
        u1 = up(x[3][1])
        d0 = down(x[5][0])
        u0 = up(add(u0, x[3][0]))
        d1 = down(add(d1, x[5][1]))
        u1 = up(add(u1, x[2][1]))
        d0 = down(add(d0, x[6][0]))
        u0 = up(add(u0, x[2][0]))
        d1 = down(add(d1, x[6][1]))
        u1 = up(add(u1, x[1][1]))
        d0 = down(add(d0, x[7][0]))
        u0 = up(add(u0, x[1][0]))
        d1 = down(add(d1, x[7][1]))
        return call(end_kernel, sds((ROWS, COLS), F32), *x[0], u0, d0, u1, d1)


def solution(mesh):
    fine = Mesh(mesh.devices.reshape(8, 2, 4, 2, 2), ("z", "xl", "y", "xh", "c"))
    in_specs = (P(OP), P(OP, TP), P(None, TP), P(TP, OP), P(TP), P(OP, TP))
    return jax.shard_map(shards, mesh=fine, in_specs=in_specs, out_specs=P(TP, OP), check_vma=False)
```

```python
import functools

import jax
import jax.numpy as jnp
import numpy as np
from jax import lax
from jax.experimental import pallas as pl
from jax.experimental.pallas import tpu as pltpu
from jax.sharding import Mesh, PartitionSpec as P

D2 = 6656
EPS = 1e-05
TOK = 128
ROWS = 416
COLS = 256
TAIL = 16
SLOTS = 48
OP = ("z", "xl")
TP = ("y", "xh", "c")
YX = ("y", "xh")
F32 = jnp.float32
BF16 = jnp.bfloat16
NT = (((1,), (1,)), ((), ()))


def call(kernel, out_shape, *args, flops=0):
    smem = pl.BlockSpec(memory_space=pltpu.SMEM)
    vmem = pl.BlockSpec(memory_space=pltpu.VMEM)
    single = not isinstance(out_shape, (list, tuple))
    outs = [out_shape] if single else list(out_shape)
    nbytes = sum(int(np.prod(a.shape)) * a.dtype.itemsize for a in list(args) + outs)
    return pl.pallas_call(
        kernel,
        out_shape=out_shape,
        in_specs=[smem if a.dtype == jnp.int32 and a.ndim == 1 else vmem for a in args],
        out_specs=vmem if single else [vmem] * len(outs),
        compiler_params=pltpu.CompilerParams(vmem_limit_bytes=48 * 1024 * 1024),
        cost_estimate=pl.CostEstimate(flops=flops, bytes_accessed=nbytes, transcendentals=0),
    )(*args)


def sds(shape, dtype=BF16):
    return jax.ShapeDtypeStruct(shape, dtype)


def dot(a, b):
    return jnp.dot(a, b, preferred_element_type=F32)


def dot_nt(a, b):
    return lax.dot_general(a, b, NT, preferred_element_type=F32)


def swap(x, axis):
    return lax.ppermute(x, axis, [(0, 1), (1, 0)])


def exchange(x):
    return lax.all_to_all(x, YX, 0, 0, tiled=False)


def ranks(inside, base):
    before = lax.broadcasted_iota(jnp.int32, (TOK, TOK), 0)
    after = lax.broadcasted_iota(jnp.int32, (TOK, TOK), 1)
    marks = jnp.where(inside, 1.0, 0.0).astype(BF16)
    rank = dot(marks, jnp.where(before < after, 1.0, 0.0).astype(BF16))
    return jnp.where(inside, rank - base, -1.0)


def look_kernel(at, ids_ref, table_ref, out_ref, most_ref):
    vocab = table_ref.shape[0]
    most = jnp.zeros((16, 1), F32)
    for v in range(16):
        here = (ids_ref[...] >= v * vocab) & (ids_ref[...] < (v + 1) * vocab)
        most = jnp.maximum(most, jnp.sum(jnp.where(here, 1.0, 0.0), axis=1, keepdims=True))
    most_ref[...] = jnp.broadcast_to(jnp.max(most, axis=0, keepdims=True), (8, TOK))
    ids = ids_ref[...] - at[0]
    key = ranks((ids >= 0) & (ids < vocab), (at[1] * SLOTS).astype(F32))
    ids = ids.astype(F32) + 1.0
    slot = lax.broadcasted_iota(jnp.int32, (SLOTS, TOK), 0).astype(F32)
    lanes = lax.broadcasted_iota(jnp.int32, (4 * SLOTS, vocab), 1).astype(F32)
    table = table_ref[...]
    for g in range(4):
        rows = []
        for o in range(4 * g, 4 * g + 4):
            hit = jnp.where(slot == key[o : o + 1], ids[o : o + 1], 0.0)
            rows.append(jnp.sum(hit, axis=1, keepdims=True) - 1.0)
        hot = jnp.where(lanes == jnp.concatenate(rows, axis=0), 1.0, 0.0).astype(BF16)
        found = dot(hot, table).astype(BF16)
        for o in range(4):
            out_ref[4 * g + o] = found[o * SLOTS : (o + 1) * SLOTS]


def place_kernel(vocab, at, ids_ref, rows_ref, out_ref):
    ids = jnp.broadcast_to(ids_ref[...], (16, TOK))
    first = lax.broadcasted_iota(jnp.int32, (16, TOK), 0) * vocab
    key = ranks((ids >= first) & (ids < first + vocab), (at[1] * SLOTS).astype(F32))
    slot = lax.broadcasted_iota(jnp.int32, (SLOTS, TOK), 0).astype(F32)
    hits = [jnp.where(slot == key[v : v + 1], 1.0, 0.0) for v in range(16)]
    hits = jnp.concatenate(hits, axis=0).T.astype(BF16)
    rows = jnp.concatenate([rows_ref[v] for v in range(16)], axis=0)
    out_ref[...] = dot(hits, rows).astype(BF16)


def split_row(row):
    hi = row.astype(BF16)
    lo = (row - hi.astype(F32)).astype(BF16)
    return jnp.broadcast_to(jnp.concatenate([hi, lo], axis=1), (TAIL, COLS))


def join_row(tail):
    both = tail.astype(F32)[0:1]
    return both[:, :TOK] + both[:, TOK:]


def blocks(place, grow):
    for d in range(8):
        yield lax.rem(place[1] + d, 8), grow[d]


def back_kernel(place, og, *refs):
    grow, (keep, send) = refs[:8], refs[8:]
    c = place[0]
    left = jnp.concatenate([og[c], og[1 - c]], axis=0)
    for b, cols in blocks(place, grow):
        part = dot(left, cols[...]).astype(BF16)
        keep[b] = part[:TOK]
        send[b] = part[TOK:]


def first_kernel(emb, keep, recv, out):
    for b in range(8):
        out[b, :TOK] = emb[...]
        out[b, TOK:] = (keep[b].astype(F32) + recv[b].astype(F32)).astype(BF16)


def sum_kernel(got, out):
    total = got[0, TOK:].astype(F32)
    for b in range(1, 8):
        total += got[b, TOK:].astype(F32)
    out[...] = total.astype(BF16)


def hidden_kernel(place, got, other, *refs):
    grow, (part, sent) = refs[:8], refs[8:]
    c = place[0]
    total = jnp.zeros((2 * TOK, ROWS), F32)
    for b, cols in blocks(place, grow):
        total += dot_nt(jnp.concatenate([got[b, :TOK], other[b]], axis=0), cols[...])
    part[c] = total[:TOK]
    part[1 - c] = total[TOK:]
    sent[c] = total[:TOK].astype(BF16)
    sent[1 - c] = total[TOK:].astype(BF16)


def proj_kernel(place, back, proj, keep, send):
    c = place[0]
    for b in range(8):
        keep[b] = dot_nt(back[...], proj[2 * b + c]).astype(BF16)
        send[b] = dot_nt(back[...], proj[2 * b + 1 - c]).astype(BF16)


def in_kernel(place, part, peer, gain, *refs):
    grow, (hidden_ref, keep, send) = refs[:8], refs[8:]
    c = place[0]
    left = []
    for t, to in ((c, keep), (1 - c, send)):
        hidden = part[t] + peer[t].astype(F32)
        hidden_ref[t] = hidden
        left.append((hidden * gain[...].astype(F32)).astype(BF16))
        square = jnp.sum(hidden * hidden, axis=1, keepdims=True)
        tail = split_row(jnp.broadcast_to(square, (TOK, TOK)).T[0:1])
        for b in range(8):
            to[b, TOK:] = tail
    left = jnp.concatenate(left, axis=0)
    for b, cols in blocks(place, grow):
        both = dot(left, cols[...]).astype(BF16)
        keep[b, :TOK] = both[:TOK]
        send[b, :TOK] = both[TOK:]


def second_kernel(keep, recv, proj_keep, proj_recv, out):
    tail = split_row(join_row(keep[0, TOK:]) + join_row(recv[0, TOK:]))
    for b in range(8):
        out[b, :TOK] = (keep[b, :TOK].astype(F32) + recv[b, :TOK].astype(F32)).astype(BF16)
        out[b, TOK : 2 * TOK] = (proj_keep[b].astype(F32) + proj_recv[b].astype(F32)).astype(BF16)
        out[b, 2 * TOK :] = tail


def mid_kernel(got, out, inv_ref):
    both = got[0, : 2 * TOK].astype(F32)
    row = join_row(got[0, 2 * TOK :])
    for b in range(1, 8):
        both += got[b, : 2 * TOK].astype(F32)
        row += join_row(got[b, 2 * TOK :])
    inv = lax.rsqrt(jnp.broadcast_to(row, (TOK, TOK)).T / D2 + EPS)
    inv_ref[...] = inv
    out[:TOK] = (both[:TOK] * inv[:, 0:1]).astype(BF16)
    out[TOK:] = both[TOK:].astype(BF16)


def third_kernel(before, after, out):
    stat = jnp.sum(before[TOK:].astype(F32) * after[:TOK].astype(F32), axis=1, keepdims=True)
    tail = split_row(jnp.broadcast_to(stat, (TOK, TOK)).T[0:1])
    for b in range(8):
        out[b, : 2 * TOK] = after[...]
        out[b, 2 * TOK :] = tail


def out_kernel(place, got, other, proj, out, stat_ref):
    c = place[0]
    total = jnp.zeros((TOK, COLS), F32)
    stat = jnp.zeros((1, TOK), F32)
    for b in range(8):
        total += dot(got[b, :TOK], proj[2 * b + c])
        total += dot(other[b, :TOK], proj[2 * b + 1 - c])
        stat += join_row(got[b, 2 * TOK :]) + join_row(other[b, 2 * TOK :])
    out[...] = total.astype(BF16)
    stat_ref[...] = jnp.broadcast_to(stat, (TOK, TOK)).T


def grad_kernel(place, got, other, *refs):
    grow, (part, sent) = refs[:8], refs[8:]
    c = place[0]
    total = jnp.zeros((2 * TOK, ROWS), F32)
    for b, cols in blocks(place, grow):
        pair = jnp.concatenate([got[b, TOK : 2 * TOK], other[b, TOK : 2 * TOK]], axis=0)
        total += dot_nt(pair, cols[...])
    part[c] = total[:TOK]
    part[1 - c] = total[TOK:]
    sent[c] = total[:TOK].astype(BF16)
    sent[1 - c] = total[TOK:].astype(BF16)


def left_kernel(place, part, peer, hidden_ref, inv_c, inv_o, stat_own, stat_peer, gain_ref, og_ref, out):
    c = place[0]
    xl = place[2]
    gain = gain_ref[...].astype(F32)
    hidden_grads, normeds, ogs = [], [], []
    for t, inv_ref in ((c, inv_c), (1 - c, inv_o)):
        inv = inv_ref[:, 0:1]
        stat = jnp.where(t == xl, stat_own[:, 0:1], stat_peer[:, 0:1])
        mean = stat / inv / D2
        hidden = hidden_ref[t]
        og = og_ref[t].astype(F32)
        scaled = (part[t] + peer[t].astype(F32)) * gain
        hidden_grads.append(og + inv * scaled - hidden * inv * inv * inv * mean)
        normeds.append(hidden * inv * gain)
        ogs.append(og)
    out[...] = jnp.concatenate(hidden_grads + normeds + ogs, axis=0).T.astype(BF16)


def last_kernel(steps, place, left_ref, emb_m, emb_o, got, other, late, late_o, *outs):
    z = place[1]
    left = left_ref[...]
    half = ROWS // 2
    for at, d in enumerate(steps):
        b = lax.rem(z + d, 8)
        right = jnp.concatenate(
            [
                emb_m[b, :TOK],
                emb_o[b],
                got[b, TOK : 2 * TOK],
                other[b, TOK : 2 * TOK],
                late[b],
                late_o[b],
            ],
            axis=0,
        )
        total = dot(left, right).astype(BF16)
        outs[2 * at][...] = total[:half]
        outs[2 * at + 1][...] = total[half:]


def end_kernel(x0, x1, u0, d0, u1, d1, out):
    half = ROWS // 2
    out[:half] = x0[...].astype(F32) + u0[...].astype(F32) + d0[...].astype(F32)
    out[half:] = x1[...].astype(F32) + u1[...].astype(F32) + d1[...].astype(F32)


def turn(x):
    return lax.ppermute(x, ("xl", "c"), [(0, 0), (1, 2), (2, 1), (3, 3)])


def up(v):
    return lax.ppermute(v, "z", [(i, (i + 1) % 8) for i in range(8)])


def down(v):
    return lax.ppermute(v, "z", [(i, (i - 1) % 8) for i in range(8)])


def shards(token_ids, embed, proj, grow_op, norm_gain, out_grad):
    c = lax.axis_index("c")
    z = lax.axis_index("z")
    xl = lax.axis_index("xl")
    place = jnp.stack([c, z, xl]).astype(jnp.int32)
    gain = norm_gain.reshape(1, ROWS)
    proj = proj.reshape(16, COLS, COLS)
    block = sds((8, TOK, COLS))
    work = 2 * TOK * ROWS * 4096

    with jax.named_scope("embedding"):
        ids = lax.all_to_all(
            jnp.broadcast_to(token_ids.reshape(1, 1, TOK), (16, 1, TOK)), OP, 0, 0, tiled=False
        )
        ups, downs = [up(grow_op)], [down(grow_op)]
        ids, ups[0], downs[0] = lax.optimization_barrier((ids, ups[0], downs[0]))
        ups.append(up(ups[0]))
        downs.append(down(downs[0]))
        ids = ids.reshape(16, TOK)
        vocab = embed.shape[0]
        first = (z * 2 + xl) * vocab
        own = token_ids.reshape(1, TOK)

        def one(k, held=(), send=lambda held: (held, ())):
            at = jnp.stack([first, k]).astype(jnp.int32)
            rows, most = call(
                look_kernel,
                [sds((16, SLOTS, COLS)), sds((8, TOK), F32)],
                at,
                ids,
                embed,
                flops=2 * 16 * SLOTS * vocab * COLS,
            )
            rows, held = lax.optimization_barrier((rows, held))
            rows = lax.all_to_all(rows, OP, 0, 0, tiled=False)
            held, og_peer = send(held)
            rows, held, og_peer = lax.optimization_barrier((rows, held, og_peer))
            part = call(
                functools.partial(place_kernel, vocab),
                sds((TOK, COLS)),
                at,
                own,
                rows,
                flops=2 * 16 * SLOTS * TOK * COLS,
            )
            return part, most[0, 0], held, og_peer

        half = ROWS // 2
        found, most, (ups3, downs3), og_peer = one(
            jnp.int32(0),
            (ups[1], downs[1]),
            lambda held: ((up(held[0]), down(held[1])), swap(out_grad, "xl")),
        )
        ups.append(ups3)
        downs.append(downs3)
        far = jnp.concatenate([up(ups3[:half]), down(downs3[half:])], axis=0)
        found = lax.while_loop(
            lambda state: (state[0] * SLOTS).astype(F32) < most,
            lambda state: (state[0] + 1, state[1] + one(state[0])[0]),
            (jnp.int32(1), found),
        )
        emb_part = turn(found[1])

    with jax.named_scope("operator"):
        grow = [grow_op, *downs, far, *ups[::-1]]
        og = jnp.stack([jnp.where(xl == 0, out_grad, og_peer), jnp.where(xl == 0, og_peer, out_grad)])
        og, emb_part = lax.optimization_barrier((og, emb_part))
        keep, send = call(back_kernel, [block, block], place, og, *grow, flops=work)
        recv = swap(send, "c")

    with jax.named_scope("first"):
        emb = exchange(call(first_kernel, sds((8, 2 * TOK, COLS)), emb_part, keep, recv))
        emb_other = swap(emb[:, :TOK], "c")
        back = call(sum_kernel, sds((TOK, COLS)), emb)
        emb, back = lax.optimization_barrier((emb, back))
        back = turn(back)

    with jax.named_scope("hidden"):
        pair = sds((2, TOK, ROWS), F32)
        pair_sent = sds((2, TOK, ROWS))
        part, sent = call(
            hidden_kernel, [pair, pair_sent], place, emb, emb_other, *grow, flops=work
        )
        peer = swap(sent, "xl")
        proj_keep, send = call(
            proj_kernel, [block, block], place, back, proj, flops=2 * TOK * COLS * 4096
        )
        part, peer, send = lax.optimization_barrier((part, peer, send))
        proj_recv = swap(send, "c")
        longer = sds((8, TOK + TAIL, COLS))
        hidden, keep, send = call(
            in_kernel, [pair, longer, longer], place, part, peer, gain, *grow, flops=work
        )

    with jax.named_scope("second"):
        got = exchange(
            call(
                second_kernel,
                sds((8, 2 * TOK + TAIL, COLS)),
                keep,
                swap(send, "c"),
                proj_keep,
                proj_recv,
            )
        )
        before, inv = call(mid_kernel, [sds((2 * TOK, COLS)), sds((TOK, TOK), F32)], got)
        after, inv_other = lax.optimization_barrier((turn(before), swap(inv, "c")))

    with jax.named_scope("third"):
        got = exchange(call(third_kernel, sds((8, 2 * TOK + TAIL, COLS)), before, after))
        other = swap(got, "c")
        part, sent = call(grad_kernel, [pair, pair_sent], place, got, other, *grow, flops=work)
        got_in, sent = lax.optimization_barrier((got, sent))
        peer = swap(sent, "xl")
        out, stat = call(
            out_kernel,
            [sds((TOK, COLS)), sds((TOK, TOK), F32)],
            place,
            got_in,
            other,
            proj,
            flops=2 * TOK * COLS * 4096,
        )
        out, stat_peer, peer = lax.optimization_barrier((turn(out), swap(stat, "xl"), peer))

    with jax.named_scope("fourth"):
        late = exchange(jnp.broadcast_to(out[None], (8, TOK, COLS)))
        late_other = swap(late, "c")
        left = call(
            left_kernel,
            sds((ROWS, 6 * TOK)),
            place,
            part,
            peer,
            hidden,
            inv,
            inv_other,
            stat,
            stat_peer,
            gain,
            og,
        )
        x = {}
        for steps in ((4, 3, 5), (2, 6, 1, 7, 0)):
            parts = call(
                functools.partial(last_kernel, steps),
                [sds((ROWS // 2, COLS))] * (2 * len(steps)),
                place,
                left,
                emb,
                emb_other,
                got,
                other,
                late,
                late_other,
                flops=3 * work * len(steps) // 8,
            )
            for at, d in enumerate(steps):
                x[d] = parts[2 * at : 2 * at + 2]

    def add(a, b):
        return (a.astype(F32) + b.astype(F32)).astype(BF16)

    with jax.named_scope("scatter"):
        u0 = up(x[4][0])
        d1 = down(x[4][1])
        u1 = up(x[3][1])
        d0 = down(x[5][0])
        u0 = up(add(u0, x[3][0]))
        d1 = down(add(d1, x[5][1]))
        u1 = up(add(u1, x[2][1]))
        d0 = down(add(d0, x[6][0]))
        u0 = up(add(u0, x[2][0]))
        d1 = down(add(d1, x[6][1]))
        u1 = up(add(u1, x[1][1]))
        d0 = down(add(d0, x[7][0]))
        u0 = up(add(u0, x[1][0]))
        d1 = down(add(d1, x[7][1]))
        return call(end_kernel, sds((ROWS, COLS), F32), *x[0], u0, d0, u1, d1)


def solution(mesh):
    fine = Mesh(mesh.devices.reshape(8, 2, 4, 2, 2), ("z", "xl", "y", "xh", "c"))
    in_specs = (P(OP), P(OP, TP), P(None, TP), P(TP, OP), P(TP), P(OP, TP))
    return jax.shard_map(shards, mesh=fine, in_specs=in_specs, out_specs=P(TP, OP), check_vma=False)
```

```python
import functools

import jax
import jax.numpy as jnp
import numpy as np
from jax import lax
from jax.experimental import pallas as pl
from jax.experimental.pallas import tpu as pltpu
from jax.sharding import Mesh, PartitionSpec as P

D2 = 6656
EPS = 1e-05
TOK = 128
ROWS = 416
COLS = 256
TAIL = 16
SLOTS = 48
OP = ("z", "xl")
TP = ("y", "xh", "c")
YX = ("y", "xh")
F32 = jnp.float32
BF16 = jnp.bfloat16
NT = (((1,), (1,)), ((), ()))


def call(kernel, out_shape, *args, flops=0):
    smem = pl.BlockSpec(memory_space=pltpu.SMEM)
    vmem = pl.BlockSpec(memory_space=pltpu.VMEM)
    single = not isinstance(out_shape, (list, tuple))
    outs = [out_shape] if single else list(out_shape)
    nbytes = sum(int(np.prod(a.shape)) * a.dtype.itemsize for a in list(args) + outs)
    return pl.pallas_call(
        kernel,
        out_shape=out_shape,
        in_specs=[smem if a.dtype == jnp.int32 and a.ndim == 1 else vmem for a in args],
        out_specs=vmem if single else [vmem] * len(outs),
        compiler_params=pltpu.CompilerParams(vmem_limit_bytes=48 * 1024 * 1024),
        cost_estimate=pl.CostEstimate(flops=flops, bytes_accessed=nbytes, transcendentals=0),
    )(*args)


def sds(shape, dtype=BF16):
    return jax.ShapeDtypeStruct(shape, dtype)


def dot(a, b):
    return jnp.dot(a, b, preferred_element_type=F32)


def dot_nt(a, b):
    return lax.dot_general(a, b, NT, preferred_element_type=F32)


def swap(x, axis):
    return lax.ppermute(x, axis, [(0, 1), (1, 0)])


def exchange(x):
    return lax.all_to_all(x, YX, 0, 0, tiled=False)


def ranks(inside, base):
    before = lax.broadcasted_iota(jnp.int32, (TOK, TOK), 0)
    after = lax.broadcasted_iota(jnp.int32, (TOK, TOK), 1)
    marks = jnp.where(inside, 1.0, 0.0).astype(BF16)
    rank = dot(marks, jnp.where(before < after, 1.0, 0.0).astype(BF16))
    return jnp.where(inside, rank - base, -1.0)


def look_kernel(at, ids_ref, table_ref, out_ref, most_ref):
    vocab = table_ref.shape[0]
    most = jnp.zeros((16, 1), F32)
    for v in range(16):
        here = (ids_ref[...] >= v * vocab) & (ids_ref[...] < (v + 1) * vocab)
        most = jnp.maximum(most, jnp.sum(jnp.where(here, 1.0, 0.0), axis=1, keepdims=True))
    most_ref[...] = jnp.broadcast_to(jnp.max(most, axis=0, keepdims=True), (8, TOK))
    ids = ids_ref[...] - at[0]
    key = ranks((ids >= 0) & (ids < vocab), (at[1] * SLOTS).astype(F32))
    ids = ids.astype(F32) + 1.0
    slot = lax.broadcasted_iota(jnp.int32, (SLOTS, TOK), 0).astype(F32)
    lanes = lax.broadcasted_iota(jnp.int32, (4 * SLOTS, vocab), 1).astype(F32)
    table = table_ref[...]
    for g in range(4):
        rows = []
        for o in range(4 * g, 4 * g + 4):
            hit = jnp.where(slot == key[o : o + 1], ids[o : o + 1], 0.0)
            rows.append(jnp.sum(hit, axis=1, keepdims=True) - 1.0)
        hot = jnp.where(lanes == jnp.concatenate(rows, axis=0), 1.0, 0.0).astype(BF16)
        found = dot(hot, table).astype(BF16)
        for o in range(4):
            out_ref[4 * g + o] = found[o * SLOTS : (o + 1) * SLOTS]


def place_kernel(vocab, at, ids_ref, rows_ref, out_ref):
    ids = jnp.broadcast_to(ids_ref[...], (16, TOK))
    first = lax.broadcasted_iota(jnp.int32, (16, TOK), 0) * vocab
    key = ranks((ids >= first) & (ids < first + vocab), (at[1] * SLOTS).astype(F32))
    slot = lax.broadcasted_iota(jnp.int32, (SLOTS, TOK), 0).astype(F32)
    hits = [jnp.where(slot == key[v : v + 1], 1.0, 0.0) for v in range(16)]
    hits = jnp.concatenate(hits, axis=0).T.astype(BF16)
    rows = jnp.concatenate([rows_ref[v] for v in range(16)], axis=0)
    out_ref[...] = dot(hits, rows).astype(BF16)


def split_row(row):
    hi = row.astype(BF16)
    lo = (row - hi.astype(F32)).astype(BF16)
    return jnp.broadcast_to(jnp.concatenate([hi, lo], axis=1), (TAIL, COLS))


def join_row(tail):
    both = tail.astype(F32)[0:1]
    return both[:, :TOK] + both[:, TOK:]


def blocks(place, grow):
    for d in range(8):
        yield lax.rem(place[1] + d, 8), grow[d]


def back_kernel(place, og, *refs):
    grow, (keep, send) = refs[:8], refs[8:]
    c = place[0]
    left = jnp.concatenate([og[c], og[1 - c]], axis=0)
    for b, cols in blocks(place, grow):
        part = dot(left, cols[...]).astype(BF16)
        keep[b] = part[:TOK]
        send[b] = part[TOK:]


def pair_kernel(keep, recv, out):
    for b in range(8):
        out[b] = (keep[b].astype(F32) + recv[b].astype(F32)).astype(BF16)


def sum_kernel(got, out):
    total = got[0].astype(F32)
    for b in range(1, 8):
        total += got[b].astype(F32)
    out[...] = total.astype(BF16)


def hidden_kernel(place, got, other, *refs):
    grow, (part, sent) = refs[:8], refs[8:]
    c = place[0]
    total = jnp.zeros((2 * TOK, ROWS), F32)
    for b, cols in blocks(place, grow):
        total += dot_nt(jnp.concatenate([got[b], other[b]], axis=0), cols[...])
    part[c] = total[:TOK]
    part[1 - c] = total[TOK:]
    sent[c] = total[:TOK].astype(BF16)
    sent[1 - c] = total[TOK:].astype(BF16)


def proj_kernel(place, back, proj, keep, send):
    c = place[0]
    for b in range(8):
        keep[b] = dot_nt(back[...], proj[2 * b + c]).astype(BF16)
        send[b] = dot_nt(back[...], proj[2 * b + 1 - c]).astype(BF16)


def in_kernel(place, part, peer, gain, *refs):
    grow, (hidden_ref, keep, send) = refs[:8], refs[8:]
    c = place[0]
    left = []
    for t, to in ((c, keep), (1 - c, send)):
        hidden = part[t] + peer[t].astype(F32)
        hidden_ref[t] = hidden
        left.append((hidden * gain[...].astype(F32)).astype(BF16))
        square = jnp.sum(hidden * hidden, axis=1, keepdims=True)
        tail = split_row(jnp.broadcast_to(square, (TOK, TOK)).T[0:1])
        for b in range(8):
            to[b, TOK:] = tail
    left = jnp.concatenate(left, axis=0)
    for b, cols in blocks(place, grow):
        both = dot(left, cols[...]).astype(BF16)
        keep[b, :TOK] = both[:TOK]
        send[b, :TOK] = both[TOK:]


def pair_in_kernel(keep, recv, out):
    tail = split_row(join_row(keep[0, TOK:]) + join_row(recv[0, TOK:]))
    for b in range(8):
        out[b, :TOK] = (keep[b, :TOK].astype(F32) + recv[b, :TOK].astype(F32)).astype(BF16)
        out[b, TOK:] = tail


def mid_kernel(got, out, inv_ref):
    total = got[0, :TOK].astype(F32)
    row = join_row(got[0, TOK:])
    for b in range(1, 8):
        total += got[b, :TOK].astype(F32)
        row += join_row(got[b, TOK:])
    inv = lax.rsqrt(jnp.broadcast_to(row, (TOK, TOK)).T / D2 + EPS)
    inv_ref[...] = inv
    out[...] = (total * inv[:, 0:1]).astype(BF16)


def stat_kernel(back, turned, small_in, out):
    stat = jnp.sum(back[...].astype(F32) * small_in[...].astype(F32), axis=1, keepdims=True)
    tail = split_row(jnp.broadcast_to(stat, (TOK, TOK)).T[0:1])
    for b in range(8):
        out[b, :TOK] = turned[...]
        out[b, TOK:] = tail


def out_kernel(place, got, other, proj, out):
    c = place[0]
    total = jnp.zeros((TOK, COLS), F32)
    for b in range(8):
        total += dot(got[b], proj[2 * b + c])
        total += dot(other[b], proj[2 * b + 1 - c])
    out[...] = total.astype(BF16)


def grad_kernel(place, got, other, *refs):
    grow, (part, sent, stat_ref) = refs[:8], refs[8:]
    c = place[0]
    total = jnp.zeros((2 * TOK, ROWS), F32)
    for b, cols in blocks(place, grow):
        pair = jnp.concatenate([got[b, :TOK], other[b, :TOK]], axis=0)
        total += dot_nt(pair, cols[...])
    part[c] = total[:TOK]
    part[1 - c] = total[TOK:]
    sent[c] = total[:TOK].astype(BF16)
    sent[1 - c] = total[TOK:].astype(BF16)
    stat = jnp.zeros((1, TOK), F32)
    for b in range(8):
        stat += join_row(got[b, TOK:]) + join_row(other[b, TOK:])
    stat_ref[...] = jnp.broadcast_to(stat, (TOK, TOK)).T


def left_kernel(place, part, peer, hidden_ref, inv_c, inv_o, stat_own, stat_peer, gain_ref, og_ref, out):
    c = place[0]
    xl = place[2]
    gain = gain_ref[...].astype(F32)
    hidden_grads, normeds, ogs = [], [], []
    for t, inv_ref in ((c, inv_c), (1 - c, inv_o)):
        inv = inv_ref[:, 0:1]
        stat = jnp.where(t == xl, stat_own[:, 0:1], stat_peer[:, 0:1])
        mean = stat / inv / D2
        hidden = hidden_ref[t]
        og = og_ref[t].astype(F32)
        scaled = (part[t] + peer[t].astype(F32)) * gain
        hidden_grads.append(og + inv * scaled - hidden * inv * inv * inv * mean)
        normeds.append(hidden * inv * gain)
        ogs.append(og)
    out[...] = jnp.concatenate(hidden_grads + normeds + ogs, axis=0).T.astype(BF16)


def last_kernel(steps, place, left_ref, emb_m, emb_o, got, other, late, late_o, *outs):
    z = place[1]
    left = left_ref[...]
    half = ROWS // 2
    for at, d in enumerate(steps):
        b = lax.rem(z + d, 8)
        right = jnp.concatenate(
            [
                emb_m[b],
                emb_o[b],
                got[b, :TOK],
                other[b, :TOK],
                late[b],
                late_o[b],
            ],
            axis=0,
        )
        total = dot(left, right).astype(BF16)
        outs[2 * at][...] = total[:half]
        outs[2 * at + 1][...] = total[half:]


def end_kernel(x0, x1, u0, d0, u1, d1, out):
    half = ROWS // 2
    out[:half] = x0[...].astype(F32) + u0[...].astype(F32) + d0[...].astype(F32)
    out[half:] = x1[...].astype(F32) + u1[...].astype(F32) + d1[...].astype(F32)


def turn(x):
    return lax.ppermute(x, ("xl", "c"), [(0, 0), (1, 2), (2, 1), (3, 3)])


def up(v):
    return lax.ppermute(v, "z", [(i, (i + 1) % 8) for i in range(8)])


def down(v):
    return lax.ppermute(v, "z", [(i, (i - 1) % 8) for i in range(8)])


def shards(token_ids, embed, proj, grow_op, norm_gain, out_grad):
    c = lax.axis_index("c")
    z = lax.axis_index("z")
    xl = lax.axis_index("xl")
    place = jnp.stack([c, z, xl]).astype(jnp.int32)
    gain = norm_gain.reshape(1, ROWS)
    proj = proj.reshape(16, COLS, COLS)
    block = sds((8, TOK, COLS))
    work = 2 * TOK * ROWS * 4096

    with jax.named_scope("embedding"):
        ids = lax.all_to_all(
            jnp.broadcast_to(token_ids.reshape(1, 1, TOK), (16, 1, TOK)), OP, 0, 0, tiled=False
        )
        ups, downs = [up(grow_op)], [down(grow_op)]
        ids, ups[0], downs[0] = lax.optimization_barrier((ids, ups[0], downs[0]))
        ups.append(up(ups[0]))
        downs.append(down(downs[0]))
        ids = ids.reshape(16, TOK)
        vocab = embed.shape[0]
        first = (z * 2 + xl) * vocab
        own = token_ids.reshape(1, TOK)

        def one(k, held=(), send=lambda held: (held, ())):
            at = jnp.stack([first, k]).astype(jnp.int32)
            rows, most = call(
                look_kernel,
                [sds((16, SLOTS, COLS)), sds((8, TOK), F32)],
                at,
                ids,
                embed,
                flops=2 * 16 * SLOTS * vocab * COLS,
            )
            rows, held = lax.optimization_barrier((rows, held))
            rows = lax.all_to_all(rows, OP, 0, 0, tiled=False)
            held, og_peer = send(held)
            rows, held, og_peer = lax.optimization_barrier((rows, held, og_peer))
            part = call(
                functools.partial(place_kernel, vocab),
                sds((TOK, COLS)),
                at,
                own,
                rows,
                flops=2 * 16 * SLOTS * TOK * COLS,
            )
            return part, most[0, 0], held, og_peer

        half = ROWS // 2
        found, most, (ups3, downs3), og_peer = one(
            jnp.int32(0),
            (ups[1], downs[1]),
            lambda held: ((up(held[0]), down(held[1])), swap(out_grad, "xl")),
        )
        ups.append(ups3)
        downs.append(downs3)
        far = jnp.concatenate([up(ups3[:half]), down(downs3[half:])], axis=0)
        found = lax.while_loop(
            lambda state: (state[0] * SLOTS).astype(F32) < most,
            lambda state: (state[0] + 1, state[1] + one(state[0])[0]),
            (jnp.int32(1), found),
        )
        emb_part = turn(found[1])

    with jax.named_scope("operator"):
        grow = [grow_op, *downs, far, *ups[::-1]]
        og = jnp.stack([jnp.where(xl == 0, out_grad, og_peer), jnp.where(xl == 0, og_peer, out_grad)])
        og, emb_part = lax.optimization_barrier((og, emb_part))
        keep, send = call(back_kernel, [block, block], place, og, *grow, flops=work)
        back = call(pair_kernel, block, keep, swap(send, "c"))

    with jax.named_scope("first"):
        emb = exchange(jnp.broadcast_to(emb_part[None], (8, TOK, COLS)))
        emb, back = lax.optimization_barrier((emb, back))
        back = exchange(back)
        emb_other = swap(emb, "c")

    with jax.named_scope("hidden"):
        pair = sds((2, TOK, ROWS), F32)
        pair_sent = sds((2, TOK, ROWS))
        part, sent = call(
            hidden_kernel, [pair, pair_sent], place, emb, emb_other, *grow, flops=work
        )
        back = call(sum_kernel, sds((TOK, COLS)), back)
        peer, back = lax.optimization_barrier((swap(sent, "xl"), back))
        longer = sds((8, TOK + TAIL, COLS))
        hidden, keep, send = call(
            in_kernel, [pair, longer, longer], place, part, peer, gain, *grow, flops=work
        )
        small = call(pair_in_kernel, longer, keep, swap(send, "c"))

    with jax.named_scope("back"):
        back = turn(back)
        keep, send = call(
            proj_kernel, [block, block], place, back, proj, flops=2 * TOK * COLS * 4096
        )
        back = call(pair_kernel, block, keep, swap(send, "c"))

    with jax.named_scope("second"):
        small = exchange(small)
        small, back = lax.optimization_barrier((small, back))
        back = exchange(back)
        small, inv = call(mid_kernel, [sds((TOK, COLS)), sds((TOK, TOK), F32)], small)
        small, inv_other = lax.optimization_barrier((turn(small), swap(inv, "c")))

    with jax.named_scope("third"):
        back = call(sum_kernel, sds((TOK, COLS)), back)
        back = call(stat_kernel, longer, back, turn(back), small)
        small = exchange(jnp.broadcast_to(small[None], (8, TOK, COLS)))
        small, back = lax.optimization_barrier((small, back))
        got = exchange(back)
        small_other = swap(small, "c")
        out = turn(
            call(
                out_kernel,
                sds((TOK, COLS)),
                place,
                small,
                small_other,
                proj,
                flops=2 * TOK * COLS * 4096,
            )
        )
        got, out = lax.optimization_barrier((got, out))
        other = swap(got, "c")
        part, sent, stat = call(
            grad_kernel,
            [pair, pair_sent, sds((TOK, TOK), F32)],
            place,
            got,
            other,
            *grow,
            flops=work,
        )
        peer, stat_peer = swap(sent, "xl"), swap(stat, "xl")

    with jax.named_scope("fourth"):
        late = exchange(jnp.broadcast_to(out[None], (8, TOK, COLS)))
        late, peer, stat_peer = lax.optimization_barrier((late, peer, stat_peer))
        late_other = swap(late, "c")
        left = call(
            left_kernel,
            sds((ROWS, 6 * TOK)),
            place,
            part,
            peer,
            hidden,
            inv,
            inv_other,
            stat,
            stat_peer,
            gain,
            og,
        )
        x = {}
        for steps in ((4, 3, 5), (2, 6, 1, 7, 0)):
            parts = call(
                functools.partial(last_kernel, steps),
                [sds((ROWS // 2, COLS))] * (2 * len(steps)),
                place,
                left,
                emb,
                emb_other,
                got,
                other,
                late,
                late_other,
                flops=3 * work * len(steps) // 8,
            )
            for at, d in enumerate(steps):
                x[d] = parts[2 * at : 2 * at + 2]

    def add(a, b):
        return (a.astype(F32) + b.astype(F32)).astype(BF16)

    with jax.named_scope("scatter"):
        u0 = up(x[4][0])
        d1 = down(x[4][1])
        u1 = up(x[3][1])
        d0 = down(x[5][0])
        u0 = up(add(u0, x[3][0]))
        d1 = down(add(d1, x[5][1]))
        u1 = up(add(u1, x[2][1]))
        d0 = down(add(d0, x[6][0]))
        u0 = up(add(u0, x[2][0]))
        d1 = down(add(d1, x[6][1]))
        u1 = up(add(u1, x[1][1]))
        d0 = down(add(d0, x[7][0]))
        u0 = up(add(u0, x[1][0]))
        d1 = down(add(d1, x[7][1]))
        return call(end_kernel, sds((ROWS, COLS), F32), *x[0], u0, d0, u1, d1)


def solution(mesh):
    fine = Mesh(mesh.devices.reshape(8, 2, 4, 2, 2), ("z", "xl", "y", "xh", "c"))
    in_specs = (P(OP), P(OP, TP), P(None, TP), P(TP, OP), P(TP), P(OP, TP))
    return jax.shard_map(shards, mesh=fine, in_specs=in_specs, out_specs=P(TP, OP), check_vma=False)
```

```python
import functools

import jax
import jax.numpy as jnp
import numpy as np
from jax import lax
from jax.experimental import pallas as pl
from jax.experimental.pallas import tpu as pltpu
from jax.sharding import Mesh, PartitionSpec as P

D2 = 6656
EPS = 1e-05
TOK = 128
ROWS = 416
COLS = 256
TAIL = 16
SLOTS = 48
OP = ("z", "xl")
TP = ("y", "xh", "c")
YX = ("y", "xh")
F32 = jnp.float32
BF16 = jnp.bfloat16
NT = (((1,), (1,)), ((), ()))


def call(kernel, out_shape, *args, flops=0):
    smem = pl.BlockSpec(memory_space=pltpu.SMEM)
    vmem = pl.BlockSpec(memory_space=pltpu.VMEM)
    single = not isinstance(out_shape, (list, tuple))
    outs = [out_shape] if single else list(out_shape)
    nbytes = sum(int(np.prod(a.shape)) * a.dtype.itemsize for a in list(args) + outs)
    return pl.pallas_call(
        kernel,
        out_shape=out_shape,
        in_specs=[smem if a.dtype == jnp.int32 and a.ndim == 1 else vmem for a in args],
        out_specs=vmem if single else [vmem] * len(outs),
        compiler_params=pltpu.CompilerParams(vmem_limit_bytes=48 * 1024 * 1024),
        cost_estimate=pl.CostEstimate(flops=flops, bytes_accessed=nbytes, transcendentals=0),
    )(*args)


def sds(shape, dtype=BF16):
    return jax.ShapeDtypeStruct(shape, dtype)


def dot(a, b):
    return jnp.dot(a, b, preferred_element_type=F32)


def dot_nt(a, b):
    return lax.dot_general(a, b, NT, preferred_element_type=F32)


def swap(x, axis):
    return lax.ppermute(x, axis, [(0, 1), (1, 0)])


def exchange(x):
    return lax.all_to_all(x, YX, 0, 0, tiled=False)


def ranks(inside, base):
    before = lax.broadcasted_iota(jnp.int32, (TOK, TOK), 0)
    after = lax.broadcasted_iota(jnp.int32, (TOK, TOK), 1)
    marks = jnp.where(inside, 1.0, 0.0).astype(BF16)
    rank = dot(marks, jnp.where(before < after, 1.0, 0.0).astype(BF16))
    return jnp.where(inside, rank - base, -1.0)


def look_kernel(at, ids_ref, table_ref, out_ref, most_ref):
    vocab = table_ref.shape[0]
    most = jnp.zeros((16, 1), F32)
    for v in range(16):
        here = (ids_ref[...] >= v * vocab) & (ids_ref[...] < (v + 1) * vocab)
        most = jnp.maximum(most, jnp.sum(jnp.where(here, 1.0, 0.0), axis=1, keepdims=True))
    most_ref[...] = jnp.broadcast_to(jnp.max(most, axis=0, keepdims=True), (8, TOK))
    ids = ids_ref[...] - at[0]
    key = ranks((ids >= 0) & (ids < vocab), (at[1] * SLOTS).astype(F32))
    ids = ids.astype(F32) + 1.0
    slot = lax.broadcasted_iota(jnp.int32, (SLOTS, TOK), 0).astype(F32)
    lanes = lax.broadcasted_iota(jnp.int32, (4 * SLOTS, vocab), 1).astype(F32)
    table = table_ref[...]
    for g in range(4):
        rows = []
        for o in range(4 * g, 4 * g + 4):
            hit = jnp.where(slot == key[o : o + 1], ids[o : o + 1], 0.0)
            rows.append(jnp.sum(hit, axis=1, keepdims=True) - 1.0)
        hot = jnp.where(lanes == jnp.concatenate(rows, axis=0), 1.0, 0.0).astype(BF16)
        found = dot(hot, table).astype(BF16)
        for o in range(4):
            out_ref[4 * g + o] = found[o * SLOTS : (o + 1) * SLOTS]


def place_kernel(vocab, at, ids_ref, rows_ref, out_ref):
    ids = jnp.broadcast_to(ids_ref[...], (16, TOK))
    first = lax.broadcasted_iota(jnp.int32, (16, TOK), 0) * vocab
    key = ranks((ids >= first) & (ids < first + vocab), (at[1] * SLOTS).astype(F32))
    slot = lax.broadcasted_iota(jnp.int32, (SLOTS, TOK), 0).astype(F32)
    hits = [jnp.where(slot == key[v : v + 1], 1.0, 0.0) for v in range(16)]
    hits = jnp.concatenate(hits, axis=0).T.astype(BF16)
    rows = jnp.concatenate([rows_ref[v] for v in range(16)], axis=0)
    out_ref[...] = dot(hits, rows).astype(BF16)


def split_row(row):
    hi = row.astype(BF16)
    lo = (row - hi.astype(F32)).astype(BF16)
    return jnp.broadcast_to(jnp.concatenate([hi, lo], axis=1), (TAIL, COLS))


def join_row(tail):
    both = tail.astype(F32)[0:1]
    return both[:, :TOK] + both[:, TOK:]


def blocks(place, grow):
    for d in range(8):
        yield lax.rem(place[1] + d, 8), grow[d]


def back_kernel(place, og, *refs):
    grow, (keep, send) = refs[:8], refs[8:]
    c = place[0]
    left = jnp.concatenate([og[c], og[1 - c]], axis=0)
    for b, cols in blocks(place, grow):
        part = dot(left, cols[...]).astype(BF16)
        keep[b] = part[:TOK]
        send[b] = part[TOK:]


def first_kernel(emb, keep, recv, out):
    for b in range(8):
        out[b, :TOK] = emb[...]
        out[b, TOK:] = (keep[b].astype(F32) + recv[b].astype(F32)).astype(BF16)


def sum_kernel(got, out):
    total = got[0, TOK:].astype(F32)
    for b in range(1, 8):
        total += got[b, TOK:].astype(F32)
    out[...] = total.astype(BF16)


def hidden_kernel(place, got, other, *refs):
    grow, (part, sent) = refs[:8], refs[8:]
    c = place[0]
    total = jnp.zeros((2 * TOK, ROWS), F32)
    for b, cols in blocks(place, grow):
        total += dot_nt(jnp.concatenate([got[b, :TOK], other[b]], axis=0), cols[...])
    part[c] = total[:TOK]
    part[1 - c] = total[TOK:]
    sent[c] = total[:TOK].astype(BF16)
    sent[1 - c] = total[TOK:].astype(BF16)


def proj_kernel(place, back, proj, keep, send):
    c = place[0]
    for b in range(8):
        keep[b] = dot_nt(back[...], proj[2 * b + c]).astype(BF16)
        send[b] = dot_nt(back[...], proj[2 * b + 1 - c]).astype(BF16)


def in_kernel(place, part, peer, gain, proj_keep, proj_send, *refs):
    grow, (hidden_ref, keep, send) = refs[:8], refs[8:]
    c = place[0]
    left = []
    for t, to, proj in ((c, keep, proj_keep), (1 - c, send, proj_send)):
        hidden = part[t] + peer[t].astype(F32)
        hidden_ref[t] = hidden
        left.append((hidden * gain[...].astype(F32)).astype(BF16))
        square = jnp.sum(hidden * hidden, axis=1, keepdims=True)
        tail = split_row(jnp.broadcast_to(square, (TOK, TOK)).T[0:1])
        for b in range(8):
            to[b, TOK : 2 * TOK] = proj[b]
            to[b, 2 * TOK :] = tail
    left = jnp.concatenate(left, axis=0)
    for b, cols in blocks(place, grow):
        both = dot(left, cols[...]).astype(BF16)
        keep[b, :TOK] = both[:TOK]
        send[b, :TOK] = both[TOK:]


def second_kernel(keep, recv, out):
    tail = split_row(join_row(keep[0, 2 * TOK :]) + join_row(recv[0, 2 * TOK :]))
    for b in range(8):
        mine = keep[b, : 2 * TOK].astype(F32)
        out[b, : 2 * TOK] = (mine + recv[b, : 2 * TOK].astype(F32)).astype(BF16)
        out[b, 2 * TOK :] = tail


def mid_kernel(got, out, inv_ref):
    both = got[0, : 2 * TOK].astype(F32)
    row = join_row(got[0, 2 * TOK :])
    for b in range(1, 8):
        both += got[b, : 2 * TOK].astype(F32)
        row += join_row(got[b, 2 * TOK :])
    inv = lax.rsqrt(jnp.broadcast_to(row, (TOK, TOK)).T / D2 + EPS)
    inv_ref[...] = inv
    out[:TOK] = (both[:TOK] * inv[:, 0:1]).astype(BF16)
    out[TOK:] = both[TOK:].astype(BF16)


def third_kernel(before, after, out):
    stat = jnp.sum(before[TOK:].astype(F32) * after[:TOK].astype(F32), axis=1, keepdims=True)
    tail = split_row(jnp.broadcast_to(stat, (TOK, TOK)).T[0:1])
    for b in range(8):
        out[b, : 2 * TOK] = after[...]
        out[b, 2 * TOK :] = tail


def out_kernel(place, got, other, proj, out, stat_ref):
    c = place[0]
    total = jnp.zeros((TOK, COLS), F32)
    stat = jnp.zeros((1, TOK), F32)
    for b in range(8):
        total += dot(got[b, :TOK], proj[2 * b + c])
        total += dot(other[b, :TOK], proj[2 * b + 1 - c])
        stat += join_row(got[b, 2 * TOK :]) + join_row(other[b, 2 * TOK :])
    out[...] = total.astype(BF16)
    stat_ref[...] = jnp.broadcast_to(stat, (TOK, TOK)).T


def grad_kernel(place, got, other, *refs):
    grow, (part, sent) = refs[:8], refs[8:]
    c = place[0]
    total = jnp.zeros((2 * TOK, ROWS), F32)
    for b, cols in blocks(place, grow):
        pair = jnp.concatenate([got[b, TOK : 2 * TOK], other[b, TOK : 2 * TOK]], axis=0)
        total += dot_nt(pair, cols[...])
    part[c] = total[:TOK]
    part[1 - c] = total[TOK:]
    sent[c] = total[:TOK].astype(BF16)
    sent[1 - c] = total[TOK:].astype(BF16)


def left_kernel(place, part, peer, hidden_ref, inv_c, inv_o, stat_own, stat_peer, gain_ref, og_ref, out):
    c = place[0]
    xl = place[2]
    gain = gain_ref[...].astype(F32)
    hidden_grads, normeds, ogs = [], [], []
    for t, inv_ref in ((c, inv_c), (1 - c, inv_o)):
        inv = inv_ref[:, 0:1]
        stat = jnp.where(t == xl, stat_own[:, 0:1], stat_peer[:, 0:1])
        mean = stat / inv / D2
        hidden = hidden_ref[t]
        og = og_ref[t].astype(F32)
        scaled = (part[t] + peer[t].astype(F32)) * gain
        hidden_grads.append(og + inv * scaled - hidden * inv * inv * inv * mean)
        normeds.append(hidden * inv * gain)
        ogs.append(og)
    out[...] = jnp.concatenate(hidden_grads + normeds + ogs, axis=0).T.astype(BF16)


def last_kernel(steps, place, left_ref, emb_m, emb_o, got, other, late, late_o, *outs):
    z = place[1]
    left = left_ref[...]
    half = ROWS // 2
    for at, d in enumerate(steps):
        b = lax.rem(z + d, 8)
        right = jnp.concatenate(
            [
                emb_m[b, :TOK],
                emb_o[b],
                got[b, TOK : 2 * TOK],
                other[b, TOK : 2 * TOK],
                late[b],
                late_o[b],
            ],
            axis=0,
        )
        total = dot(left, right).astype(BF16)
        outs[2 * at][...] = total[:half]
        outs[2 * at + 1][...] = total[half:]


def end_kernel(x0, x1, u0, d0, u1, d1, out):
    half = ROWS // 2
    out[:half] = x0[...].astype(F32) + u0[...].astype(F32) + d0[...].astype(F32)
    out[half:] = x1[...].astype(F32) + u1[...].astype(F32) + d1[...].astype(F32)


def turn(x):
    return lax.ppermute(x, ("xl", "c"), [(0, 0), (1, 2), (2, 1), (3, 3)])


def up(v):
    return lax.ppermute(v, "z", [(i, (i + 1) % 8) for i in range(8)])


def down(v):
    return lax.ppermute(v, "z", [(i, (i - 1) % 8) for i in range(8)])


def shards(token_ids, embed, proj, grow_op, norm_gain, out_grad):
    c = lax.axis_index("c")
    z = lax.axis_index("z")
    xl = lax.axis_index("xl")
    place = jnp.stack([c, z, xl]).astype(jnp.int32)
    gain = norm_gain.reshape(1, ROWS)
    proj = proj.reshape(16, COLS, COLS)
    block = sds((8, TOK, COLS))
    work = 2 * TOK * ROWS * 4096

    with jax.named_scope("embedding"):
        embed = turn(embed)
        ids = lax.all_to_all(
            jnp.broadcast_to(token_ids.reshape(1, 1, TOK), (16, 1, TOK)), OP, 0, 0, tiled=False
        )
        ups, downs = [up(grow_op)], [down(grow_op)]
        ids, ups[0], downs[0] = lax.optimization_barrier((ids, ups[0], downs[0]))
        ups.append(up(ups[0]))
        downs.append(down(downs[0]))
        ids = ids.reshape(16, TOK)
        vocab = embed.shape[0]
        first = (z * 2 + c) * vocab
        own = lax.dynamic_slice_in_dim(ids, z * 2 + c, 1, axis=0)

        def one(k, held=(), send=lambda held: (held, ())):
            at = jnp.stack([first, k]).astype(jnp.int32)
            rows, most = call(
                look_kernel,
                [sds((16, SLOTS, COLS)), sds((8, TOK), F32)],
                at,
                ids,
                embed,
                flops=2 * 16 * SLOTS * vocab * COLS,
            )
            rows, held = lax.optimization_barrier((rows, held))
            rows = lax.all_to_all(rows, ("z", "c"), 0, 0, tiled=False)
            held, og_peer = send(held)
            rows, og_peer = lax.optimization_barrier((rows, og_peer))
            part = call(
                functools.partial(place_kernel, vocab),
                sds((TOK, COLS)),
                at,
                own,
                rows,
                flops=2 * 16 * SLOTS * TOK * COLS,
            )
            return part, most[0, 0], held, og_peer

        half = ROWS // 2
        found, most, (ups3, downs3), og_peer = one(
            jnp.int32(0),
            (ups[1], downs[1]),
            lambda held: ((up(held[0]), down(held[1])), swap(out_grad, "xl")),
        )
        ups.append(ups3)
        downs.append(downs3)
        far = jnp.concatenate([up(ups3[:half]), down(downs3[half:])], axis=0)
        found = lax.while_loop(
            lambda state: (state[0] * SLOTS).astype(F32) < most,
            lambda state: (state[0] + 1, state[1] + one(state[0])[0]),
            (jnp.int32(1), found),
        )
        emb_part = found[1]

    with jax.named_scope("operator"):
        grow = [grow_op, *downs, far, *ups[::-1]]
        og = jnp.stack([jnp.where(xl == 0, out_grad, og_peer), jnp.where(xl == 0, og_peer, out_grad)])
        og, emb_part = lax.optimization_barrier((og, emb_part))
        keep, send = call(back_kernel, [block, block], place, og, *grow, flops=work)
        recv = swap(send, "c")

    with jax.named_scope("first"):
        emb = exchange(call(first_kernel, sds((8, 2 * TOK, COLS)), emb_part, keep, recv))
        emb_other = swap(emb[:, :TOK], "c")
        back = call(sum_kernel, sds((TOK, COLS)), emb)
        emb, back = lax.optimization_barrier((emb, back))
        back = turn(back)

    with jax.named_scope("hidden"):
        pair = sds((2, TOK, ROWS), F32)
        pair_sent = sds((2, TOK, ROWS))
        part, sent = call(
            hidden_kernel, [pair, pair_sent], place, emb, emb_other, *grow, flops=work
        )
        peer = swap(sent, "xl")
        proj_keep, proj_send = call(
            proj_kernel, [block, block], place, back, proj, flops=2 * TOK * COLS * 4096
        )
        longer = sds((8, 2 * TOK + TAIL, COLS))
        hidden, keep, send = call(
            in_kernel,
            [pair, longer, longer],
            place,
            part,
            peer,
            gain,
            proj_keep,
            proj_send,
            *grow,
            flops=work,
        )

    with jax.named_scope("second"):
        got = exchange(call(second_kernel, longer, keep, swap(send, "c")))
        before, inv = call(mid_kernel, [sds((2 * TOK, COLS)), sds((TOK, TOK), F32)], got)
        after, inv_other = lax.optimization_barrier((turn(before), swap(inv, "c")))

    with jax.named_scope("third"):
        got = exchange(call(third_kernel, sds((8, 2 * TOK + TAIL, COLS)), before, after))
        other = swap(got, "c")
        out, stat = call(
            out_kernel,
            [sds((TOK, COLS)), sds((TOK, TOK), F32)],
            place,
            got,
            other,
            proj,
            flops=2 * TOK * COLS * 4096,
        )
        got_back, out, stat = lax.optimization_barrier((got, out, stat))
        out, stat_peer = lax.optimization_barrier((turn(out), swap(stat, "xl")))
        part, sent = call(
            grad_kernel, [pair, pair_sent], place, got_back, other, *grow, flops=work
        )
        out, part, sent = lax.optimization_barrier((out, part, sent))
        peer = swap(sent, "xl")

    with jax.named_scope("fourth"):
        late = exchange(jnp.broadcast_to(out[None], (8, TOK, COLS)))
        late, peer = lax.optimization_barrier((late, peer))
        late_other = swap(late, "c")
        left = call(
            left_kernel,
            sds((ROWS, 6 * TOK)),
            place,
            part,
            peer,
            hidden,
            inv,
            inv_other,
            stat,
            stat_peer,
            gain,
            og,
        )
        x = {}
        for steps in ((4, 3, 5), (2, 6, 1, 7, 0)):
            parts = call(
                functools.partial(last_kernel, steps),
                [sds((ROWS // 2, COLS))] * (2 * len(steps)),
                place,
                left,
                emb,
                emb_other,
                got,
                other,
                late,
                late_other,
                flops=3 * work * len(steps) // 8,
            )
            for at, d in enumerate(steps):
                x[d] = parts[2 * at : 2 * at + 2]

    def add(a, b):
        return (a.astype(F32) + b.astype(F32)).astype(BF16)

    with jax.named_scope("scatter"):
        u0 = up(x[4][0])
        d1 = down(x[4][1])
        u1 = up(x[3][1])
        d0 = down(x[5][0])
        u0 = up(add(u0, x[3][0]))
        d1 = down(add(d1, x[5][1]))
        u1 = up(add(u1, x[2][1]))
        d0 = down(add(d0, x[6][0]))
        u0 = up(add(u0, x[2][0]))
        d1 = down(add(d1, x[6][1]))
        u1 = up(add(u1, x[1][1]))
        d0 = down(add(d0, x[7][0]))
        u0 = up(add(u0, x[1][0]))
        d1 = down(add(d1, x[7][1]))
        return call(end_kernel, sds((ROWS, COLS), F32), *x[0], u0, d0, u1, d1)


def solution(mesh):
    fine = Mesh(mesh.devices.reshape(8, 2, 4, 2, 2), ("z", "xl", "y", "xh", "c"))
    in_specs = (P(OP), P(OP, TP), P(None, TP), P(TP, OP), P(TP), P(OP, TP))
    return jax.shard_map(shards, mesh=fine, in_specs=in_specs, out_specs=P(TP, OP), check_vma=False)
```

```python
import functools

import jax
import jax.numpy as jnp
import numpy as np
from jax import lax
from jax.experimental import pallas as pl
from jax.experimental.pallas import tpu as pltpu
from jax.sharding import Mesh, PartitionSpec as P

D2 = 6656
EPS = 1e-05
TOK = 128
ROWS = 416
COLS = 256
TAIL = 16
SLOTS = 48
OP = ("z", "xl")
TP = ("y", "xh", "c")
YX = ("y", "xh")
F32 = jnp.float32
BF16 = jnp.bfloat16
NT = (((1,), (1,)), ((), ()))


def call(kernel, out_shape, *args, flops=0):
    smem = pl.BlockSpec(memory_space=pltpu.SMEM)
    vmem = pl.BlockSpec(memory_space=pltpu.VMEM)
    single = not isinstance(out_shape, (list, tuple))
    outs = [out_shape] if single else list(out_shape)
    nbytes = sum(int(np.prod(a.shape)) * a.dtype.itemsize for a in list(args) + outs)
    return pl.pallas_call(
        kernel,
        out_shape=out_shape,
        in_specs=[smem if a.dtype == jnp.int32 and a.ndim == 1 else vmem for a in args],
        out_specs=vmem if single else [vmem] * len(outs),
        compiler_params=pltpu.CompilerParams(vmem_limit_bytes=20 * 1024 * 1024),
        cost_estimate=pl.CostEstimate(flops=flops, bytes_accessed=nbytes, transcendentals=0),
    )(*args)


def sds(shape, dtype=BF16):
    return jax.ShapeDtypeStruct(shape, dtype)


def dot(a, b):
    return jnp.dot(a, b, preferred_element_type=F32)


def dot_nt(a, b):
    return lax.dot_general(a, b, NT, preferred_element_type=F32)


def swap(x, axis):
    return lax.ppermute(x, axis, [(0, 1), (1, 0)])


def exchange(x):
    return lax.all_to_all(x, YX, 0, 0, tiled=False)


def ranks(inside, base):
    before = lax.broadcasted_iota(jnp.int32, (TOK, TOK), 0)
    after = lax.broadcasted_iota(jnp.int32, (TOK, TOK), 1)
    marks = jnp.where(inside, 1.0, 0.0).astype(BF16)
    rank = dot(marks, jnp.where(before < after, 1.0, 0.0).astype(BF16))
    return jnp.where(inside, rank - base, -1.0)


def look_kernel(at, ids_ref, table_ref, out_ref, most_ref):
    vocab = table_ref.shape[0]
    most = jnp.zeros((16, 1), F32)
    for v in range(16):
        here = (ids_ref[...] >= v * vocab) & (ids_ref[...] < (v + 1) * vocab)
        most = jnp.maximum(most, jnp.sum(jnp.where(here, 1.0, 0.0), axis=1, keepdims=True))
    most_ref[...] = jnp.broadcast_to(jnp.max(most, axis=0, keepdims=True), (8, TOK))
    ids = ids_ref[...] - at[0]
    key = ranks((ids >= 0) & (ids < vocab), (at[1] * SLOTS).astype(F32))
    ids = ids.astype(F32) + 1.0
    slot = lax.broadcasted_iota(jnp.int32, (SLOTS, TOK), 0).astype(F32)
    lanes = lax.broadcasted_iota(jnp.int32, (4 * SLOTS, vocab), 1).astype(F32)
    table = table_ref[...]
    for g in range(4):
        rows = []
        for o in range(4 * g, 4 * g + 4):
            hit = jnp.where(slot == key[o : o + 1], ids[o : o + 1], 0.0)
            rows.append(jnp.sum(hit, axis=1, keepdims=True) - 1.0)
        hot = jnp.where(lanes == jnp.concatenate(rows, axis=0), 1.0, 0.0).astype(BF16)
        found = dot(hot, table).astype(BF16)
        for o in range(4):
            out_ref[4 * g + o] = found[o * SLOTS : (o + 1) * SLOTS]


def place_kernel(vocab, at, ids_ref, rows_ref, out_ref):
    ids = jnp.broadcast_to(ids_ref[...], (16, TOK))
    first = lax.broadcasted_iota(jnp.int32, (16, TOK), 0) * vocab
    key = ranks((ids >= first) & (ids < first + vocab), (at[1] * SLOTS).astype(F32))
    slot = lax.broadcasted_iota(jnp.int32, (SLOTS, TOK), 0).astype(F32)
    hits = [jnp.where(slot == key[v : v + 1], 1.0, 0.0) for v in range(16)]
    hits = jnp.concatenate(hits, axis=0).T.astype(BF16)
    rows = jnp.concatenate([rows_ref[v] for v in range(16)], axis=0)
    out_ref[...] = dot(hits, rows).astype(BF16)


def split_row(row):
    hi = row.astype(BF16)
    lo = (row - hi.astype(F32)).astype(BF16)
    return jnp.broadcast_to(jnp.concatenate([hi, lo], axis=1), (TAIL, COLS))


def join_row(tail):
    both = tail.astype(F32)[0:1]
    return both[:, :TOK] + both[:, TOK:]


def blocks(place, grow):
    for d in range(8):
        yield lax.rem(place[1] + d, 8), grow[d]


def back_kernel(place, og, *refs):
    grow, (keep, send) = refs[:8], refs[8:]
    c = place[0]
    left = jnp.concatenate([og[c], og[1 - c]], axis=0)
    for b, cols in blocks(place, grow):
        part = dot(left, cols[...]).astype(BF16)
        keep[b] = part[:TOK]
        send[b] = part[TOK:]


def pair_kernel(keep, recv, out):
    for b in range(8):
        out[b] = (keep[b].astype(F32) + recv[b].astype(F32)).astype(BF16)


def sum_kernel(got, out):
    total = got[0].astype(F32)
    for b in range(1, 8):
        total += got[b].astype(F32)
    out[...] = total.astype(BF16)


def hidden_kernel(place, got, other, *refs):
    grow, (part, sent) = refs[:8], refs[8:]
    c = place[0]
    total = jnp.zeros((2 * TOK, ROWS), F32)
    for b, cols in blocks(place, grow):
        total += dot_nt(jnp.concatenate([got[b], other[b]], axis=0), cols[...])
    part[c] = total[:TOK]
    part[1 - c] = total[TOK:]
    sent[c] = total[:TOK].astype(BF16)
    sent[1 - c] = total[TOK:].astype(BF16)


def proj_kernel(place, back, proj, keep, send):
    c = place[0]
    for b in range(8):
        keep[b] = dot_nt(back[...], proj[2 * b + c]).astype(BF16)
        send[b] = dot_nt(back[...], proj[2 * b + 1 - c]).astype(BF16)


def in_kernel(place, part, peer, gain, *refs):
    grow, (hidden_ref, keep, send) = refs[:8], refs[8:]
    c = place[0]
    left = []
    for t, to in ((c, keep), (1 - c, send)):
        hidden = part[t] + peer[t].astype(F32)
        hidden_ref[t] = hidden
        left.append((hidden * gain[...].astype(F32)).astype(BF16))
        square = jnp.sum(hidden * hidden, axis=1, keepdims=True)
        tail = split_row(jnp.broadcast_to(square, (TOK, TOK)).T[0:1])
        for b in range(8):
            to[b, TOK:] = tail
    left = jnp.concatenate(left, axis=0)
    for b, cols in blocks(place, grow):
        both = dot(left, cols[...]).astype(BF16)
        keep[b, :TOK] = both[:TOK]
        send[b, :TOK] = both[TOK:]


def second_kernel(keep, recv, proj_keep, proj_recv, out):
    tail = split_row(join_row(keep[0, TOK:]) + join_row(recv[0, TOK:]))
    for b in range(8):
        out[b, :TOK] = (keep[b, :TOK].astype(F32) + recv[b, :TOK].astype(F32)).astype(BF16)
        out[b, TOK : 2 * TOK] = (proj_keep[b].astype(F32) + proj_recv[b].astype(F32)).astype(BF16)
        out[b, 2 * TOK :] = tail


def mid_kernel(got, out, inv_ref):
    both = got[0, : 2 * TOK].astype(F32)
    row = join_row(got[0, 2 * TOK :])
    for b in range(1, 8):
        both += got[b, : 2 * TOK].astype(F32)
        row += join_row(got[b, 2 * TOK :])
    inv = lax.rsqrt(jnp.broadcast_to(row, (TOK, TOK)).T / D2 + EPS)
    inv_ref[...] = inv
    out[:TOK] = (both[:TOK] * inv[:, 0:1]).astype(BF16)
    out[TOK:] = both[TOK:].astype(BF16)


def third_kernel(before, after, out):
    stat = jnp.sum(before[TOK:].astype(F32) * after[:TOK].astype(F32), axis=1, keepdims=True)
    tail = split_row(jnp.broadcast_to(stat, (TOK, TOK)).T[0:1])
    for b in range(8):
        out[b, : 2 * TOK] = after[...]
        out[b, 2 * TOK :] = tail


def out_kernel(place, got, other, proj, out):
    c = place[0]
    total = jnp.zeros((TOK, COLS), F32)
    for b in range(8):
        total += dot(got[b, :TOK], proj[2 * b + c])
        total += dot(other[b, :TOK], proj[2 * b + 1 - c])
    out[...] = total.astype(BF16)


def grad_kernel(place, got, other, *refs):
    grow, (part, sent) = refs[:8], refs[8:]
    c = place[0]
    total = jnp.zeros((2 * TOK, ROWS), F32)
    for b, cols in blocks(place, grow):
        pair = jnp.concatenate([got[b, TOK : 2 * TOK], other[b, TOK : 2 * TOK]], axis=0)
        total += dot_nt(pair, cols[...])
    stat = jnp.zeros((1, TOK), F32)
    for b in range(8):
        stat += join_row(got[b, 2 * TOK :]) + join_row(other[b, 2 * TOK :])
    tail = jnp.concatenate([split_row(stat), jnp.zeros((TAIL, ROWS - COLS), BF16)], axis=1)
    for t, rows in ((c, total[:TOK]), (1 - c, total[TOK:])):
        part[t] = rows
        sent[t, :TOK] = rows.astype(BF16)
        sent[t, TOK:] = tail


def left_kernel(place, part, peer, hidden_ref, inv_c, inv_o, sent, gain_ref, og_ref, out):
    c = place[0]
    xl = place[2]
    gain = gain_ref[...].astype(F32)
    hidden_grads, normeds, ogs = [], [], []
    for t, inv_ref in ((c, inv_c), (1 - c, inv_o)):
        inv = inv_ref[:, 0:1]
        row = jnp.where(t == xl, join_row(sent[0, TOK:, :COLS]), join_row(peer[0, TOK:, :COLS]))
        mean = jnp.broadcast_to(row, (TOK, TOK)).T[:, 0:1] / inv / D2
        hidden = hidden_ref[t]
        og = og_ref[t].astype(F32)
        scaled = (part[t] + peer[t, :TOK].astype(F32)) * gain
        hidden_grads.append(og + inv * scaled - hidden * inv * inv * inv * mean)
        normeds.append(hidden * inv * gain)
        ogs.append(og)
    out[...] = jnp.concatenate(hidden_grads + normeds + ogs, axis=0).T.astype(BF16)


def last_kernel(steps, place, left_ref, emb_m, emb_o, got, other, late, late_o, *outs):
    z = place[1]
    left = left_ref[...]
    half = ROWS // 2
    for at, d in enumerate(steps):
        b = lax.rem(z + d, 8)
        right = jnp.concatenate(
            [
                emb_m[b],
                emb_o[b],
                got[b, TOK : 2 * TOK],
                other[b, TOK : 2 * TOK],
                late[b],
                late_o[b],
            ],
            axis=0,
        )
        total = dot(left, right).astype(BF16)
        outs[2 * at][...] = total[:half]
        outs[2 * at + 1][...] = total[half:]


def end_kernel(x0, x1, u0, d0, u1, d1, out):
    half = ROWS // 2
    out[:half] = x0[...].astype(F32) + u0[...].astype(F32) + d0[...].astype(F32)
    out[half:] = x1[...].astype(F32) + u1[...].astype(F32) + d1[...].astype(F32)


def turn(x):
    return lax.ppermute(x, ("xl", "c"), [(0, 0), (1, 2), (2, 1), (3, 3)])


def up(v):
    return lax.ppermute(v, "z", [(i, (i + 1) % 8) for i in range(8)])


def down(v):
    return lax.ppermute(v, "z", [(i, (i - 1) % 8) for i in range(8)])


def shards(token_ids, embed, proj, grow_op, norm_gain, out_grad):
    c = lax.axis_index("c")
    z = lax.axis_index("z")
    xl = lax.axis_index("xl")
    place = jnp.stack([c, z, xl]).astype(jnp.int32)
    gain = norm_gain.reshape(1, ROWS)
    proj = proj.reshape(16, COLS, COLS)
    block = sds((8, TOK, COLS))
    work = 2 * TOK * ROWS * 4096

    with jax.named_scope("embedding"):
        ids = lax.all_to_all(
            jnp.broadcast_to(token_ids.reshape(1, 1, TOK), (16, 1, TOK)), OP, 0, 0, tiled=False
        )
        ups, downs = [up(grow_op)], [down(grow_op)]
        og_peer = swap(out_grad, "xl")
        ids, ups[0], downs[0], og_peer = lax.optimization_barrier((ids, ups[0], downs[0], og_peer))
        ids = ids.reshape(16, TOK)
        vocab = embed.shape[0]
        first = (z * 2 + xl) * vocab
        own = token_ids.reshape(1, TOK)

        def one(k, held=()):
            at = jnp.stack([first, k]).astype(jnp.int32)
            rows, most = call(
                look_kernel,
                [sds((16, SLOTS, COLS)), sds((8, TOK), F32)],
                at,
                ids,
                embed,
                flops=2 * 16 * SLOTS * vocab * COLS,
            )
            rows, held = lax.optimization_barrier((rows, held))
            rows = lax.all_to_all(rows, OP, 0, 0, tiled=False)
            part = call(
                functools.partial(place_kernel, vocab),
                sds((TOK, COLS)),
                at,
                own,
                rows,
                flops=2 * 16 * SLOTS * TOK * COLS,
            )
            return part, most[0, 0], held

        half = ROWS // 2
        found, most, held = one(jnp.int32(0), (ups[0], downs[0]))
        ups, downs = [held[0]], [held[1]]
        for _ in range(2):
            ups.append(up(ups[-1]))
            downs.append(down(downs[-1]))
        found = lax.while_loop(
            lambda state: (state[0] * SLOTS).astype(F32) < most,
            lambda state: (state[0] + 1, state[1] + one(state[0])[0]),
            (jnp.int32(1), found),
        )
        emb_part = turn(found[1])
        far = jnp.concatenate([up(ups[2][:half]), down(downs[2][half:])], axis=0)

    with jax.named_scope("operator"):
        grow = [grow_op, *downs, far, *ups[::-1]]
        og = jnp.stack([jnp.where(xl == 0, out_grad, og_peer), jnp.where(xl == 0, og_peer, out_grad)])

    with jax.named_scope("first"):
        emb = exchange(jnp.broadcast_to(emb_part[None], (8, TOK, COLS)))
        og, emb = lax.optimization_barrier((og, emb))
        emb_other = swap(emb, "c")
        keep, send = call(back_kernel, [block, block], place, og, *grow, flops=work)
        back = exchange(call(pair_kernel, block, keep, swap(send, "c")))

    with jax.named_scope("hidden"):
        pair = sds((2, TOK, ROWS), F32)
        pair_sent = sds((2, TOK, ROWS))
        part, sent = call(
            hidden_kernel, [pair, pair_sent], place, emb, emb_other, *grow, flops=work
        )
        back = call(sum_kernel, sds((TOK, COLS)), back)
        peer, back = lax.optimization_barrier((swap(sent, "xl"), back))
        back = turn(back)
        longer = sds((8, TOK + TAIL, COLS))
        hidden, keep, send = call(
            in_kernel, [pair, longer, longer], place, part, peer, gain, *grow, flops=work
        )
        recv = swap(send, "c")
        proj_keep, send = call(
            proj_kernel, [block, block], place, back, proj, flops=2 * TOK * COLS * 4096
        )
        proj_recv = swap(send, "c")

    with jax.named_scope("second"):
        got = exchange(
            call(
                second_kernel,
                sds((8, 2 * TOK + TAIL, COLS)),
                keep,
                recv,
                proj_keep,
                proj_recv,
            )
        )
        before, inv = call(mid_kernel, [sds((2 * TOK, COLS)), sds((TOK, TOK), F32)], got)
        after, inv_other = lax.optimization_barrier((turn(before), swap(inv, "c")))

    with jax.named_scope("third"):
        got = exchange(call(third_kernel, sds((8, 2 * TOK + TAIL, COLS)), before, after))
        other = swap(got, "c")
        part, sent = call(
            grad_kernel, [pair, sds((2, TOK + TAIL, ROWS))], place, got, other, *grow, flops=work
        )
        got_in, sent = lax.optimization_barrier((got, sent))
        peer = swap(sent, "xl")
        out = call(
            out_kernel,
            sds((TOK, COLS)),
            place,
            got_in,
            other,
            proj,
            flops=2 * TOK * COLS * 4096,
        )
        out, peer = lax.optimization_barrier((turn(out), peer))

    with jax.named_scope("fourth"):
        late = exchange(jnp.broadcast_to(out[None], (8, TOK, COLS)))
        late_other = swap(late, "c")
        left = call(
            left_kernel,
            sds((ROWS, 6 * TOK)),
            place,
            part,
            peer,
            hidden,
            inv,
            inv_other,
            sent,
            gain,
            og,
        )
        x = {}
        for steps in ((4, 3, 5), (2, 6, 1, 7, 0)):
            parts = call(
                functools.partial(last_kernel, steps),
                [sds((ROWS // 2, COLS))] * (2 * len(steps)),
                place,
                left,
                emb,
                emb_other,
                got,
                other,
                late,
                late_other,
                flops=3 * work * len(steps) // 8,
            )
            for at, d in enumerate(steps):
                x[d] = parts[2 * at : 2 * at + 2]

    def add(a, b):
        return (a.astype(F32) + b.astype(F32)).astype(BF16)

    with jax.named_scope("scatter"):
        u0 = up(x[4][0])
        d1 = down(x[4][1])
        u1 = up(x[3][1])
        d0 = down(x[5][0])
        u0 = up(add(u0, x[3][0]))
        d1 = down(add(d1, x[5][1]))
        u1 = up(add(u1, x[2][1]))
        d0 = down(add(d0, x[6][0]))
        u0 = up(add(u0, x[2][0]))
        d1 = down(add(d1, x[6][1]))
        u1 = up(add(u1, x[1][1]))
        d0 = down(add(d0, x[7][0]))
        u0 = up(add(u0, x[1][0]))
        d1 = down(add(d1, x[7][1]))
        return call(end_kernel, sds((ROWS, COLS), F32), *x[0], u0, d0, u1, d1)


def solution(mesh):
    fine = Mesh(mesh.devices.reshape(8, 2, 4, 2, 2), ("z", "xl", "y", "xh", "c"))
    in_specs = (P(OP), P(OP, TP), P(None, TP), P(TP, OP), P(TP), P(OP, TP))
    return jax.shard_map(shards, mesh=fine, in_specs=in_specs, out_specs=P(TP, OP), check_vma=False)
```

```python
import functools

import jax
import jax.numpy as jnp
import numpy as np
from jax import lax
from jax.experimental import pallas as pl
from jax.experimental.pallas import tpu as pltpu
from jax.sharding import Mesh, PartitionSpec as P

D2 = 6656
EPS = 1e-05
TOK = 128
ROWS = 416
COLS = 256
TAIL = 16
SLOTS = 48
OP = ("z", "xl")
TP = ("y", "xh", "c")
YX = ("y", "xh")
F32 = jnp.float32
BF16 = jnp.bfloat16
NT = (((1,), (1,)), ((), ()))


def call(kernel, out_shape, *args, flops=0):
    smem = pl.BlockSpec(memory_space=pltpu.SMEM)
    vmem = pl.BlockSpec(memory_space=pltpu.VMEM)
    single = not isinstance(out_shape, (list, tuple))
    outs = [out_shape] if single else list(out_shape)
    nbytes = sum(int(np.prod(a.shape)) * a.dtype.itemsize for a in list(args) + outs)
    return pl.pallas_call(
        kernel,
        out_shape=out_shape,
        in_specs=[smem if a.dtype == jnp.int32 and a.ndim == 1 else vmem for a in args],
        out_specs=vmem if single else [vmem] * len(outs),
        compiler_params=pltpu.CompilerParams(vmem_limit_bytes=20 * 1024 * 1024),
        cost_estimate=pl.CostEstimate(flops=flops, bytes_accessed=nbytes, transcendentals=0),
    )(*args)


def sds(shape, dtype=BF16):
    return jax.ShapeDtypeStruct(shape, dtype)


def dot(a, b):
    return jnp.dot(a, b, preferred_element_type=F32)


def dot_nt(a, b):
    return lax.dot_general(a, b, NT, preferred_element_type=F32)


def swap(x, axis):
    return lax.ppermute(x, axis, [(0, 1), (1, 0)])


def exchange(x):
    return lax.all_to_all(x, YX, 0, 0, tiled=False)


def ranks(inside, base):
    before = lax.broadcasted_iota(jnp.int32, (TOK, TOK), 0)
    after = lax.broadcasted_iota(jnp.int32, (TOK, TOK), 1)
    marks = jnp.where(inside, 1.0, 0.0).astype(BF16)
    rank = dot(marks, jnp.where(before < after, 1.0, 0.0).astype(BF16))
    return jnp.where(inside, rank - base, -1.0)


def look_kernel(at, ids_ref, table_ref, out_ref, most_ref):
    vocab = table_ref.shape[0]
    most = jnp.zeros((16, 1), F32)
    for v in range(16):
        here = (ids_ref[...] >= v * vocab) & (ids_ref[...] < (v + 1) * vocab)
        most = jnp.maximum(most, jnp.sum(jnp.where(here, 1.0, 0.0), axis=1, keepdims=True))
    most_ref[...] = jnp.broadcast_to(jnp.max(most, axis=0, keepdims=True), (8, TOK))
    ids = ids_ref[...] - at[0]
    key = ranks((ids >= 0) & (ids < vocab), (at[1] * SLOTS).astype(F32))
    ids = ids.astype(F32) + 1.0
    slot = lax.broadcasted_iota(jnp.int32, (SLOTS, TOK), 0).astype(F32)
    lanes = lax.broadcasted_iota(jnp.int32, (4 * SLOTS, vocab), 1).astype(F32)
    table = table_ref[...]
    for g in range(4):
        rows = []
        for o in range(4 * g, 4 * g + 4):
            hit = jnp.where(slot == key[o : o + 1], ids[o : o + 1], 0.0)
            rows.append(jnp.sum(hit, axis=1, keepdims=True) - 1.0)
        hot = jnp.where(lanes == jnp.concatenate(rows, axis=0), 1.0, 0.0).astype(BF16)
        found = dot(hot, table).astype(BF16)
        for o in range(4):
            out_ref[4 * g + o] = found[o * SLOTS : (o + 1) * SLOTS]


def place_kernel(vocab, at, ids_ref, rows_ref, out_ref):
    ids = jnp.broadcast_to(ids_ref[...], (16, TOK))
    first = lax.broadcasted_iota(jnp.int32, (16, TOK), 0) * vocab
    key = ranks((ids >= first) & (ids < first + vocab), (at[1] * SLOTS).astype(F32))
    slot = lax.broadcasted_iota(jnp.int32, (SLOTS, TOK), 0).astype(F32)
    hits = [jnp.where(slot == key[v : v + 1], 1.0, 0.0) for v in range(16)]
    hits = jnp.concatenate(hits, axis=0).T.astype(BF16)
    rows = jnp.concatenate([rows_ref[v] for v in range(16)], axis=0)
    out_ref[...] = dot(hits, rows).astype(BF16)


def split_row(row):
    hi = row.astype(BF16)
    lo = (row - hi.astype(F32)).astype(BF16)
    return jnp.broadcast_to(jnp.concatenate([hi, lo], axis=1), (TAIL, COLS))


def join_row(tail):
    both = tail.astype(F32)[0:1]
    return both[:, :TOK] + both[:, TOK:]


def blocks(place, grow):
    for d in range(8):
        yield lax.rem(place[1] + d, 8), grow[d]


def hidden_kernel(place, got, other, *refs):
    grow, (part, sent) = refs[:8], refs[8:]
    c = place[0]
    total = jnp.zeros((2 * TOK, ROWS), F32)
    for b, cols in blocks(place, grow):
        total += dot_nt(jnp.concatenate([got[b], other[b]], axis=0), cols[...])
    part[c] = total[:TOK]
    part[1 - c] = total[TOK:]
    sent[c] = total[:TOK].astype(BF16)
    sent[1 - c] = total[TOK:].astype(BF16)


def proj_kernel(place, back, proj, keep, send):
    c = place[0]
    for b in range(8):
        keep[b] = dot_nt(back[...], proj[2 * b + c]).astype(BF16)
        send[b] = dot_nt(back[...], proj[2 * b + 1 - c]).astype(BF16)


def in_kernel(place, part, peer, gain, og, *refs):
    grow, (hidden_ref, keep, send) = refs[:8], refs[8:]
    c = place[0]
    left = []
    for t, to in ((c, keep), (1 - c, send)):
        hidden = part[t] + peer[t].astype(F32)
        hidden_ref[t] = hidden
        left += [(hidden * gain[...].astype(F32)).astype(BF16), og[t]]
        square = jnp.sum(hidden * hidden, axis=1, keepdims=True)
        tail = split_row(jnp.broadcast_to(square, (TOK, TOK)).T[0:1])
        for b in range(8):
            to[b, 2 * TOK :] = tail
    left = jnp.concatenate(left, axis=0)
    for b, cols in blocks(place, grow):
        both = dot(left, cols[...]).astype(BF16)
        keep[b, : 2 * TOK] = both[: 2 * TOK]
        send[b, : 2 * TOK] = both[2 * TOK :]


def second_kernel(keep, recv, out):
    tail = split_row(join_row(keep[0, 2 * TOK :]) + join_row(recv[0, 2 * TOK :]))
    for b in range(8):
        mine = keep[b, : 2 * TOK].astype(F32)
        out[b, : 2 * TOK] = (mine + recv[b, : 2 * TOK].astype(F32)).astype(BF16)
        out[b, 2 * TOK :] = tail


def mid_kernel(got, out, inv_ref):
    both = got[0, : 2 * TOK].astype(F32)
    row = join_row(got[0, 2 * TOK :])
    for b in range(1, 8):
        both += got[b, : 2 * TOK].astype(F32)
        row += join_row(got[b, 2 * TOK :])
    inv = lax.rsqrt(jnp.broadcast_to(row, (TOK, TOK)).T / D2 + EPS)
    inv_ref[...] = inv
    out[:TOK] = (both[:TOK] * inv[:, 0:1]).astype(BF16)
    out[TOK:] = both[TOK:].astype(BF16)


def proj_kernel(place, turned, proj, keep, send):
    c = place[0]
    back = turned[TOK:]
    for b in range(8):
        keep[b] = dot_nt(back, proj[2 * b + c]).astype(BF16)
        send[b] = dot_nt(back, proj[2 * b + 1 - c]).astype(BF16)


def third_kernel(turned, keep, recv, out):
    for b in range(8):
        out[b, :TOK] = turned[:TOK]
        out[b, TOK:] = (keep[b].astype(F32) + recv[b].astype(F32)).astype(BF16)


def out_kernel(place, turned, got, other, proj, out, stat_ref):
    c = place[0]
    total = jnp.zeros((TOK, COLS), F32)
    back = jnp.zeros((TOK, COLS), F32)
    for b in range(8):
        total += dot(got[b, :TOK], proj[2 * b + c])
        total += dot(other[b], proj[2 * b + 1 - c])
        back += got[b, TOK:].astype(F32)
    back = back.astype(BF16)
    out[:TOK] = total.astype(BF16)
    out[TOK:] = back
    stat = jnp.sum(back.astype(F32) * turned[:TOK].astype(F32), axis=1, keepdims=True)
    stat_ref[...] = split_row(jnp.broadcast_to(stat, (TOK, TOK)).T[0:1])


def fourth_kernel(turned, stat, out):
    for b in range(8):
        out[b, : 2 * TOK] = turned[...]
        out[b, 2 * TOK :] = stat[...]


def grad_kernel(place, got, other, *refs):
    grow, (part, sent) = refs[:8], refs[8:]
    c = place[0]
    total = jnp.zeros((2 * TOK, ROWS), F32)
    for b, cols in blocks(place, grow):
        pair = jnp.concatenate([got[b, TOK : 2 * TOK], other[b, :TOK]], axis=0)
        total += dot_nt(pair, cols[...])
    stat = jnp.zeros((1, TOK), F32)
    for b in range(8):
        stat += join_row(got[b, 2 * TOK :]) + join_row(other[b, TOK:])
    tail = jnp.concatenate([split_row(stat), jnp.zeros((TAIL, ROWS - COLS), BF16)], axis=1)
    for t, rows in ((c, total[:TOK]), (1 - c, total[TOK:])):
        part[t] = rows
        sent[t, :TOK] = rows.astype(BF16)
        sent[t, TOK:] = tail


def left_kernel(place, part, peer, hidden_ref, inv_c, inv_o, sent, gain_ref, og_ref, out):
    c = place[0]
    xl = place[2]
    gain = gain_ref[...].astype(F32)
    hidden_grads, normeds, ogs = [], [], []
    for t, inv_ref in ((c, inv_c), (1 - c, inv_o)):
        inv = inv_ref[:, 0:1]
        row = jnp.where(t == xl, join_row(sent[0, TOK:, :COLS]), join_row(peer[0, TOK:, :COLS]))
        mean = jnp.broadcast_to(row, (TOK, TOK)).T[:, 0:1] / inv / D2
        hidden = hidden_ref[t]
        og = og_ref[t].astype(F32)
        scaled = (part[t] + peer[t, :TOK].astype(F32)) * gain
        hidden_grads.append(og + inv * scaled - hidden * inv * inv * inv * mean)
        normeds.append(hidden * inv * gain)
        ogs.append(og)
    out[...] = jnp.concatenate(hidden_grads + normeds + ogs, axis=0).T.astype(BF16)


def last_kernel(steps, place, left_ref, emb_m, emb_o, late, back_o, out_o, *outs):
    z = place[1]
    left = left_ref[...]
    half = ROWS // 2
    for at, d in enumerate(steps):
        b = lax.rem(z + d, 8)
        right = jnp.concatenate(
            [
                emb_m[b],
                emb_o[b],
                late[b, TOK : 2 * TOK],
                back_o[b, :TOK],
                late[b, :TOK],
                out_o[b],
            ],
            axis=0,
        )
        total = dot(left, right).astype(BF16)
        outs[2 * at][...] = total[:half]
        outs[2 * at + 1][...] = total[half:]


def end_kernel(x0, x1, u0, d0, u1, d1, out):
    half = ROWS // 2
    out[:half] = x0[...].astype(F32) + u0[...].astype(F32) + d0[...].astype(F32)
    out[half:] = x1[...].astype(F32) + u1[...].astype(F32) + d1[...].astype(F32)


def turn(x):
    return lax.ppermute(x, ("xl", "c"), [(0, 0), (1, 2), (2, 1), (3, 3)])


def up(v):
    return lax.ppermute(v, "z", [(i, (i + 1) % 8) for i in range(8)])


def down(v):
    return lax.ppermute(v, "z", [(i, (i - 1) % 8) for i in range(8)])


def shards(token_ids, embed, proj, grow_op, norm_gain, out_grad):
    c = lax.axis_index("c")
    z = lax.axis_index("z")
    xl = lax.axis_index("xl")
    place = jnp.stack([c, z, xl]).astype(jnp.int32)
    gain = norm_gain.reshape(1, ROWS)
    proj = proj.reshape(16, COLS, COLS)
    block = sds((8, TOK, COLS))
    work = 2 * TOK * ROWS * 4096

    with jax.named_scope("embedding"):
        ids = lax.all_to_all(
            jnp.broadcast_to(token_ids.reshape(1, 1, TOK), (16, 1, TOK)), OP, 0, 0, tiled=False
        )
        ups, downs = [up(grow_op)], [down(grow_op)]
        ids, ups[0], downs[0] = lax.optimization_barrier((ids, ups[0], downs[0]))
        ids = ids.reshape(16, TOK)
        vocab = embed.shape[0]
        first = (z * 2 + xl) * vocab
        own = token_ids.reshape(1, TOK)

        def one(k, held=()):
            at = jnp.stack([first, k]).astype(jnp.int32)
            rows, most = call(
                look_kernel,
                [sds((16, SLOTS, COLS)), sds((8, TOK), F32)],
                at,
                ids,
                embed,
                flops=2 * 16 * SLOTS * vocab * COLS,
            )
            rows, held = lax.optimization_barrier((rows, held))
            rows = lax.all_to_all(rows, OP, 0, 0, tiled=False)
            if held:
                step = (up(held[0]), down(held[1]), swap(held[2], "xl"))
                rows, held = lax.optimization_barrier((rows, step))
            part = call(
                functools.partial(place_kernel, vocab),
                sds((TOK, COLS)),
                at,
                own,
                rows,
                flops=2 * 16 * SLOTS * TOK * COLS,
            )
            return part, most[0, 0], held

        half = ROWS // 2
        near = ups[0], downs[0]
        found, most, held = one(jnp.int32(0), (ups[0], downs[0], out_grad))
        ups, downs, og_peer = [held[0]], [held[1]], held[2]
        ups.append(up(ups[0]))
        downs.append(down(downs[0]))
        found = lax.while_loop(
            lambda state: (state[0] * SLOTS).astype(F32) < most,
            lambda state: (state[0] + 1, state[1] + one(state[0])[0]),
            (jnp.int32(1), found),
        )
        emb_part, ups[1], downs[1] = lax.optimization_barrier((turn(found[1]), ups[1], downs[1]))
        far = [up(ups[1][:half]), down(downs[1][half:])]

    with jax.named_scope("operator"):
        og = jnp.stack([jnp.where(xl == 0, out_grad, og_peer), jnp.where(xl == 0, og_peer, out_grad)])

    with jax.named_scope("first"):
        emb = exchange(jnp.broadcast_to(emb_part[None], (8, TOK, COLS)))
        emb, far = lax.optimization_barrier((emb, far))
        first_up, first_down = near
        grow = [grow_op, first_down, *downs, jnp.concatenate(far, axis=0), *ups[::-1], first_up]
        emb_other = swap(emb, "c")

    with jax.named_scope("hidden"):
        pair = sds((2, TOK, ROWS), F32)
        part, sent = call(
            hidden_kernel,
            [pair, sds((2, TOK, ROWS))],
            place,
            emb,
            emb_other,
            *grow,
            flops=work,
        )
        longer = sds((8, 2 * TOK + TAIL, COLS))
        hidden, keep, send = call(
            in_kernel,
            [pair, longer, longer],
            place,
            part,
            swap(sent, "xl"),
            gain,
            og,
            *grow,
            flops=2 * work,
        )

    with jax.named_scope("second"):
        got = exchange(call(second_kernel, longer, keep, swap(send, "c")))
        before, inv = call(mid_kernel, [sds((2 * TOK, COLS)), sds((TOK, TOK), F32)], got)
        turned, inv_other = lax.optimization_barrier((turn(before), swap(inv, "c")))

    with jax.named_scope("third"):
        keep, send = call(
            proj_kernel, [block, block], place, turned, proj, flops=2 * TOK * COLS * 4096
        )
        got = exchange(
            call(third_kernel, sds((8, 2 * TOK, COLS)), turned, keep, swap(send, "c"))
        )
        out, stat = call(
            out_kernel,
            [sds((2 * TOK, COLS)), sds((TAIL, COLS))],
            place,
            turned,
            got,
            swap(got[:, :TOK], "c"),
            proj,
            flops=2 * TOK * COLS * 4096,
        )

    with jax.named_scope("fourth"):
        late = exchange(call(fourth_kernel, longer, turn(out), stat))
        back_other = swap(late[:, TOK:], "c")
        part, sent = call(
            grad_kernel,
            [pair, sds((2, TOK + TAIL, ROWS))],
            place,
            late,
            back_other,
            *grow,
            flops=work,
        )
        late, sent = lax.optimization_barrier((late, sent))
        out_other = swap(late[:, :TOK], "c")
        peer = swap(sent, "xl")
        left = call(
            left_kernel,
            sds((ROWS, 6 * TOK)),
            place,
            part,
            peer,
            hidden,
            inv,
            inv_other,
            sent,
            gain,
            og,
        )
        x = {}
        for steps in ((4, 3, 5), (2, 6, 1, 7, 0)):
            parts = call(
                functools.partial(last_kernel, steps),
                [sds((ROWS // 2, COLS))] * (2 * len(steps)),
                place,
                left,
                emb,
                emb_other,
                late,
                back_other,
                out_other,
                flops=3 * work * len(steps) // 8,
            )
            for at, d in enumerate(steps):
                x[d] = parts[2 * at : 2 * at + 2]

    def add(a, b):
        return (a.astype(F32) + b.astype(F32)).astype(BF16)

    with jax.named_scope("scatter"):
        u0 = up(x[4][0])
        d1 = down(x[4][1])
        u1 = up(x[3][1])
        d0 = down(x[5][0])
        u0 = up(add(u0, x[3][0]))
        d1 = down(add(d1, x[5][1]))
        u1 = up(add(u1, x[2][1]))
        d0 = down(add(d0, x[6][0]))
        u0 = up(add(u0, x[2][0]))
        d1 = down(add(d1, x[6][1]))
        u1 = up(add(u1, x[1][1]))
        d0 = down(add(d0, x[7][0]))
        u0 = up(add(u0, x[1][0]))
        d1 = down(add(d1, x[7][1]))
        return call(end_kernel, sds((ROWS, COLS), F32), *x[0], u0, d0, u1, d1)


def solution(mesh):
    fine = Mesh(mesh.devices.reshape(8, 2, 4, 2, 2), ("z", "xl", "y", "xh", "c"))
    in_specs = (P(OP), P(OP, TP), P(None, TP), P(TP, OP), P(TP), P(OP, TP))
    return jax.shard_map(shards, mesh=fine, in_specs=in_specs, out_specs=P(TP, OP), check_vma=False)
```

```python
import functools

import jax
import jax.numpy as jnp
import numpy as np
from jax import lax
from jax.experimental import pallas as pl
from jax.experimental.pallas import tpu as pltpu
from jax.sharding import Mesh, PartitionSpec as P

D2 = 6656
EPS = 1e-05
TOK = 128
ROWS = 416
COLS = 256
TAIL = 16
SLOTS = 48
OP = ("z", "xl")
TP = ("y", "xh", "c")
YX = ("y", "xh")
F32 = jnp.float32
BF16 = jnp.bfloat16
NT = (((1,), (1,)), ((), ()))


def call(kernel, out_shape, *args, flops=0):
    smem = pl.BlockSpec(memory_space=pltpu.SMEM)
    vmem = pl.BlockSpec(memory_space=pltpu.VMEM)
    single = not isinstance(out_shape, (list, tuple))
    outs = [out_shape] if single else list(out_shape)
    nbytes = sum(int(np.prod(a.shape)) * a.dtype.itemsize for a in list(args) + outs)
    return pl.pallas_call(
        kernel,
        out_shape=out_shape,
        in_specs=[smem if a.dtype == jnp.int32 and a.ndim == 1 else vmem for a in args],
        out_specs=vmem if single else [vmem] * len(outs),
        compiler_params=pltpu.CompilerParams(vmem_limit_bytes=20 * 1024 * 1024),
        cost_estimate=pl.CostEstimate(flops=flops, bytes_accessed=nbytes, transcendentals=0),
    )(*args)


def sds(shape, dtype=BF16):
    return jax.ShapeDtypeStruct(shape, dtype)


def dot(a, b):
    return jnp.dot(a, b, preferred_element_type=F32)


def dot_nt(a, b):
    return lax.dot_general(a, b, NT, preferred_element_type=F32)


def swap(x, axis):
    return lax.ppermute(x, axis, [(0, 1), (1, 0)])


def exchange(x):
    return lax.all_to_all(x, YX, 0, 0, tiled=False)


def ranks(inside, base):
    before = lax.broadcasted_iota(jnp.int32, (TOK, TOK), 0)
    after = lax.broadcasted_iota(jnp.int32, (TOK, TOK), 1)
    marks = jnp.where(inside, 1.0, 0.0).astype(BF16)
    rank = dot(marks, jnp.where(before < after, 1.0, 0.0).astype(BF16))
    return jnp.where(inside, rank - base, -1.0)


def look_kernel(at, ids_ref, table_ref, out_ref, most_ref):
    vocab = table_ref.shape[0]
    most = jnp.zeros((16, 1), F32)
    for v in range(16):
        here = (ids_ref[...] >= v * vocab) & (ids_ref[...] < (v + 1) * vocab)
        most = jnp.maximum(most, jnp.sum(jnp.where(here, 1.0, 0.0), axis=1, keepdims=True))
    most_ref[...] = jnp.broadcast_to(jnp.max(most, axis=0, keepdims=True), (8, TOK))
    ids = ids_ref[...] - at[0]
    key = ranks((ids >= 0) & (ids < vocab), (at[1] * SLOTS).astype(F32))
    ids = ids.astype(F32) + 1.0
    slot = lax.broadcasted_iota(jnp.int32, (SLOTS, TOK), 0).astype(F32)
    lanes = lax.broadcasted_iota(jnp.int32, (4 * SLOTS, vocab), 1).astype(F32)
    table = table_ref[...]
    for g in range(4):
        rows = []
        for o in range(4 * g, 4 * g + 4):
            hit = jnp.where(slot == key[o : o + 1], ids[o : o + 1], 0.0)
            rows.append(jnp.sum(hit, axis=1, keepdims=True) - 1.0)
        hot = jnp.where(lanes == jnp.concatenate(rows, axis=0), 1.0, 0.0).astype(BF16)
        found = dot(hot, table).astype(BF16)
        for o in range(4):
            out_ref[4 * g + o] = found[o * SLOTS : (o + 1) * SLOTS]


def place_kernel(vocab, at, ids_ref, rows_ref, out_ref):
    ids = jnp.broadcast_to(ids_ref[...], (16, TOK))
    first = lax.broadcasted_iota(jnp.int32, (16, TOK), 0) * vocab
    key = ranks((ids >= first) & (ids < first + vocab), (at[1] * SLOTS).astype(F32))
    slot = lax.broadcasted_iota(jnp.int32, (SLOTS, TOK), 0).astype(F32)
    hits = [jnp.where(slot == key[v : v + 1], 1.0, 0.0) for v in range(16)]
    hits = jnp.concatenate(hits, axis=0).T.astype(BF16)
    rows = jnp.concatenate([rows_ref[v] for v in range(16)], axis=0)
    out_ref[...] = dot(hits, rows).astype(BF16)


def split_row(row):
    hi = row.astype(BF16)
    lo = (row - hi.astype(F32)).astype(BF16)
    return jnp.broadcast_to(jnp.concatenate([hi, lo], axis=1), (TAIL, COLS))


def join_row(tail):
    both = tail.astype(F32)[0:1]
    return both[:, :TOK] + both[:, TOK:]


def blocks(place, grow):
    for d in range(8):
        yield lax.rem(place[1] + d, 8), grow[d]


def hidden_kernel(place, got, other, *refs):
    grow, (part, sent) = refs[:8], refs[8:]
    c = place[0]
    total = jnp.zeros((ROWS, 2 * TOK), F32)
    for b, cols in blocks(place, grow):
        total += dot_nt(cols[...], jnp.concatenate([got[b], other[b]], axis=0))
    for t, rows in ((c, total[:, :TOK]), (1 - c, total[:, TOK:])):
        part[t] = rows
        sent[t] = rows.astype(BF16)


def in_kernel(place, part, peer, gain, og, *refs):
    grow, (hidden_ref, keep, send) = refs[:8], refs[8:]
    c = place[0]
    left = []
    for t, to in ((c, keep), (1 - c, send)):
        hidden = part[t] + peer[t].astype(F32)
        hidden_ref[t] = hidden
        left += [(hidden * gain[...].astype(F32)).T.astype(BF16), og[t]]
        tail = split_row(jnp.sum(hidden * hidden, axis=0, keepdims=True))
        for b in range(8):
            to[b, 2 * TOK :] = tail
    left = jnp.concatenate(left, axis=0)
    for b, cols in blocks(place, grow):
        both = dot(left, cols[...]).astype(BF16)
        keep[b, : 2 * TOK] = both[: 2 * TOK]
        send[b, : 2 * TOK] = both[2 * TOK :]


def second_kernel(keep, recv, out):
    tail = split_row(join_row(keep[0, 2 * TOK :]) + join_row(recv[0, 2 * TOK :]))
    for b in range(8):
        mine = keep[b, : 2 * TOK].astype(F32)
        out[b, : 2 * TOK] = (mine + recv[b, : 2 * TOK].astype(F32)).astype(BF16)
        out[b, 2 * TOK :] = tail


def mid_kernel(got, out, inv_ref):
    both = got[0, : 2 * TOK].astype(F32)
    row = join_row(got[0, 2 * TOK :])
    for b in range(1, 8):
        both += got[b, : 2 * TOK].astype(F32)
        row += join_row(got[b, 2 * TOK :])
    inv = lax.rsqrt(jnp.broadcast_to(row, (TOK, TOK)) / D2 + EPS)
    inv_ref[...] = inv[0:8]
    out[:TOK] = (both[:TOK] * inv.T[:, 0:1]).astype(BF16)
    out[TOK:] = both[TOK:].astype(BF16)


def proj_kernel(place, turned, proj, keep, send):
    c = place[0]
    back = turned[TOK:]
    for b in range(8):
        keep[b] = dot_nt(back, proj[2 * b + c]).astype(BF16)
        send[b] = dot_nt(back, proj[2 * b + 1 - c]).astype(BF16)


def third_kernel(turned, keep, recv, out):
    for b in range(8):
        out[b, :TOK] = turned[:TOK]
        out[b, TOK:] = (keep[b].astype(F32) + recv[b].astype(F32)).astype(BF16)


def out_kernel(place, turned, got, other, proj, out, stat_ref):
    c = place[0]
    total = jnp.zeros((TOK, COLS), F32)
    back = jnp.zeros((TOK, COLS), F32)
    for b in range(8):
        total += dot(got[b, :TOK], proj[2 * b + c])
        total += dot(other[b], proj[2 * b + 1 - c])
        back += got[b, TOK:].astype(F32)
    back = back.astype(BF16)
    out[:TOK] = total.astype(BF16)
    out[TOK:] = back
    stat = jnp.sum(back.astype(F32) * turned[:TOK].astype(F32), axis=1, keepdims=True)
    stat_ref[...] = split_row(jnp.broadcast_to(stat, (TOK, TOK)).T[0:1])


def fourth_kernel(turned, stat, out):
    for b in range(8):
        out[b, : 2 * TOK] = turned[...]
        out[b, 2 * TOK :] = stat[...]


def grad_kernel(place, got, other, *refs):
    grow, (part, sent) = refs[:8], refs[8:]
    c = place[0]
    total = jnp.zeros((ROWS, 2 * TOK), F32)
    for b, cols in blocks(place, grow):
        pair = jnp.concatenate([got[b, TOK : 2 * TOK], other[b, :TOK]], axis=0)
        total += dot_nt(cols[...], pair)
    stat = jnp.zeros((1, TOK), F32)
    for b in range(8):
        stat += join_row(got[b, 2 * TOK :]) + join_row(other[b, TOK:])
    both = split_row(stat)
    tail = jnp.concatenate([both[:8, :TOK].astype(F32), both[:8, TOK:].astype(F32)], axis=0)
    for t, rows in ((c, total[:, :TOK]), (1 - c, total[:, TOK:])):
        part[t] = rows
        sent[t, :ROWS] = rows.astype(BF16)
        sent[t, ROWS:] = tail.astype(BF16)


def left_kernel(place, part, peer, hidden_ref, inv_c, inv_o, sent, gain_ref, og_ref, out):
    c = place[0]
    xl = place[2]
    gain = gain_ref[...].astype(F32)
    hidden_grads, normeds, ogs = [], [], []
    for t, inv_ref in ((c, inv_c), (1 - c, inv_o)):
        inv = inv_ref[0:1]
        tail = jnp.where(t == xl, sent[0, ROWS:].astype(F32), peer[0, ROWS:].astype(F32))
        mean = (tail[0:1] + tail[8:9]) / inv / D2
        hidden = hidden_ref[t]
        og = og_ref[t].astype(F32).T
        scaled = (part[t] + peer[t, :ROWS].astype(F32)) * gain
        hidden_grads.append(og + inv * scaled - hidden * inv * inv * inv * mean)
        normeds.append(hidden * inv * gain)
        ogs.append(og)
    out[...] = jnp.concatenate(hidden_grads + normeds + ogs, axis=1).astype(BF16)


def last_kernel(steps, place, left_ref, emb_m, emb_o, late, back_o, out_o, *outs):
    z = place[1]
    left = left_ref[...]
    half = ROWS // 2
    for at, d in enumerate(steps):
        b = lax.rem(z + d, 8)
        right = jnp.concatenate(
            [
                emb_m[b],
                emb_o[b],
                late[b, TOK : 2 * TOK],
                back_o[b, :TOK],
                late[b, :TOK],
                out_o[b],
            ],
            axis=0,
        )
        total = dot(left, right).astype(BF16)
        outs[2 * at][...] = total[:half]
        outs[2 * at + 1][...] = total[half:]


def end_kernel(x0, x1, u0, d0, u1, d1, out):
    half = ROWS // 2
    out[:half] = x0[...].astype(F32) + u0[...].astype(F32) + d0[...].astype(F32)
    out[half:] = x1[...].astype(F32) + u1[...].astype(F32) + d1[...].astype(F32)


def turn(x):
    return lax.ppermute(x, ("xl", "c"), [(0, 0), (1, 2), (2, 1), (3, 3)])


def up(v):
    return lax.ppermute(v, "z", [(i, (i + 1) % 8) for i in range(8)])


def down(v):
    return lax.ppermute(v, "z", [(i, (i - 1) % 8) for i in range(8)])


def shards(token_ids, embed, proj, grow_op, norm_gain, out_grad):
    c = lax.axis_index("c")
    z = lax.axis_index("z")
    xl = lax.axis_index("xl")
    place = jnp.stack([c, z, xl]).astype(jnp.int32)
    gain = norm_gain.reshape(ROWS, 1)
    proj = proj.reshape(16, COLS, COLS)
    block = sds((8, TOK, COLS))
    work = 2 * TOK * ROWS * 4096

    with jax.named_scope("embedding"):
        ids = lax.all_to_all(
            jnp.broadcast_to(token_ids.reshape(1, 1, TOK), (16, 1, TOK)), OP, 0, 0, tiled=False
        )
        near = up(grow_op), down(grow_op)
        ids, near = lax.optimization_barrier((ids, near))
        ups, downs = [up(near[0])], [down(near[1])]
        ids = ids.reshape(16, TOK)
        vocab = embed.shape[0]
        first = (z * 2 + xl) * vocab
        own = token_ids.reshape(1, TOK)

        def one(k, held=None):
            at = jnp.stack([first, k]).astype(jnp.int32)
            rows, most = call(
                look_kernel,
                [sds((16, SLOTS, COLS)), sds((8, TOK), F32)],
                at,
                ids,
                embed,
                flops=2 * 16 * SLOTS * vocab * COLS,
            )
            rows, held = lax.optimization_barrier((rows, held))
            rows = lax.all_to_all(rows, OP, 0, 0, tiled=False)
            if held:
                rows, held = lax.optimization_barrier((rows, (*held[:2], swap(held[2], "xl"))))
            part = call(
                functools.partial(place_kernel, vocab),
                sds((TOK, COLS)),
                at,
                own,
                rows,
                flops=2 * 16 * SLOTS * TOK * COLS,
            )
            return part, most[0, 0], held

        half = ROWS // 2
        found, most, held = one(jnp.int32(0), (ups[0], downs[0], out_grad))
        ups, downs, og_peer = [held[0]], [held[1]], held[2]
        ups.append(up(ups[0]))
        downs.append(down(downs[0]))
        found = lax.while_loop(
            lambda state: (state[0] * SLOTS).astype(F32) < most,
            lambda state: (state[0] + 1, state[1] + one(state[0])[0]),
            (jnp.int32(1), found),
        )
        emb_part, ups[1], downs[1] = lax.optimization_barrier((turn(found[1]), ups[1], downs[1]))
        far = [up(ups[1][:half]), down(downs[1][half:])]

    with jax.named_scope("operator"):
        og = jnp.stack([jnp.where(xl == 0, out_grad, og_peer), jnp.where(xl == 0, og_peer, out_grad)])

    with jax.named_scope("first"):
        emb = exchange(jnp.broadcast_to(emb_part[None], (8, TOK, COLS)))
        emb, far = lax.optimization_barrier((emb, far))
        first_up, first_down = near
        grow = [grow_op, first_down, *downs, jnp.concatenate(far, axis=0), *ups[::-1], first_up]
        emb_other = swap(emb, "c")

    with jax.named_scope("hidden"):
        pair = sds((2, ROWS, TOK), F32)
        part, sent = call(
            hidden_kernel,
            [pair, sds((2, ROWS, TOK))],
            place,
            emb,
            emb_other,
            *grow,
            flops=work,
        )
        longer = sds((8, 2 * TOK + TAIL, COLS))
        hidden, keep, send = call(
            in_kernel,
            [pair, longer, longer],
            place,
            part,
            swap(sent, "xl"),
            gain,
            og,
            *grow,
            flops=2 * work,
        )

    with jax.named_scope("second"):
        got = exchange(call(second_kernel, longer, keep, swap(send, "c")))
        before, inv = call(mid_kernel, [sds((2 * TOK, COLS)), sds((8, TOK), F32)], got)
        turned, inv_other = lax.optimization_barrier((turn(before), swap(inv, "c")))

    with jax.named_scope("third"):
        keep, send = call(
            proj_kernel, [block, block], place, turned, proj, flops=2 * TOK * COLS * 4096
        )
        got = exchange(
            call(third_kernel, sds((8, 2 * TOK, COLS)), turned, keep, swap(send, "c"))
        )
        out, stat = call(
            out_kernel,
            [sds((2 * TOK, COLS)), sds((TAIL, COLS))],
            place,
            turned,
            got,
            swap(got[:, :TOK], "c"),
            proj,
            flops=2 * TOK * COLS * 4096,
        )

    with jax.named_scope("fourth"):
        late = exchange(call(fourth_kernel, longer, turn(out), stat))
        back_other = swap(late[:, TOK:], "c")
        part, sent = call(
            grad_kernel,
            [pair, sds((2, ROWS + TAIL, TOK))],
            place,
            late,
            back_other,
            *grow,
            flops=work,
        )
        late, sent = lax.optimization_barrier((late, sent))
        out_other = swap(late[:, :TOK], "c")
        peer = swap(sent, "xl")
        left = call(
            left_kernel,
            sds((ROWS, 6 * TOK)),
            place,
            part,
            peer,
            hidden,
            inv,
            inv_other,
            sent,
            gain,
            og,
        )
        x = {}
        for steps in ((4, 3, 5), (2, 6, 1, 7, 0)):
            parts = call(
                functools.partial(last_kernel, steps),
                [sds((ROWS // 2, COLS))] * (2 * len(steps)),
                place,
                left,
                emb,
                emb_other,
                late,
                back_other,
                out_other,
                flops=3 * work * len(steps) // 8,
            )
            for at, d in enumerate(steps):
                x[d] = parts[2 * at : 2 * at + 2]

    def add(a, b):
        return (a.astype(F32) + b.astype(F32)).astype(BF16)

    with jax.named_scope("scatter"):
        u0 = up(x[4][0])
        d1 = down(x[4][1])
        u1 = up(x[3][1])
        d0 = down(x[5][0])
        u0 = up(add(u0, x[3][0]))
        d1 = down(add(d1, x[5][1]))
        u1 = up(add(u1, x[2][1]))
        d0 = down(add(d0, x[6][0]))
        u0 = up(add(u0, x[2][0]))
        d1 = down(add(d1, x[6][1]))
        u1 = up(add(u1, x[1][1]))
        d0 = down(add(d0, x[7][0]))
        u0 = up(add(u0, x[1][0]))
        d1 = down(add(d1, x[7][1]))
        return call(end_kernel, sds((ROWS, COLS), F32), *x[0], u0, d0, u1, d1)


def solution(mesh):
    fine = Mesh(mesh.devices.reshape(8, 2, 4, 2, 2), ("z", "xl", "y", "xh", "c"))
    in_specs = (P(OP), P(OP, TP), P(None, TP), P(TP, OP), P(TP), P(OP, TP))
    return jax.shard_map(shards, mesh=fine, in_specs=in_specs, out_specs=P(TP, OP), check_vma=False)
```

```python
import functools

import jax
import jax.numpy as jnp
import numpy as np
from jax import lax
from jax.experimental import pallas as pl
from jax.experimental.pallas import tpu as pltpu
from jax.sharding import Mesh, PartitionSpec as P

D2 = 6656
EPS = 1e-05
TOK = 128
ROWS = 416
COLS = 256
TAIL = 16
SLOTS = 48
OP = ("z", "xl")
TP = ("y", "xh", "c")
YX = ("y", "xh")
F32 = jnp.float32
BF16 = jnp.bfloat16
NT = (((1,), (1,)), ((), ()))


def call(kernel, out_shape, *args, flops=0):
    smem = pl.BlockSpec(memory_space=pltpu.SMEM)
    vmem = pl.BlockSpec(memory_space=pltpu.VMEM)
    single = not isinstance(out_shape, (list, tuple))
    outs = [out_shape] if single else list(out_shape)
    nbytes = sum(int(np.prod(a.shape)) * a.dtype.itemsize for a in list(args) + outs)
    return pl.pallas_call(
        kernel,
        out_shape=out_shape,
        in_specs=[smem if a.dtype == jnp.int32 and a.ndim == 1 else vmem for a in args],
        out_specs=vmem if single else [vmem] * len(outs),
        compiler_params=pltpu.CompilerParams(vmem_limit_bytes=20 * 1024 * 1024),
        cost_estimate=pl.CostEstimate(flops=flops, bytes_accessed=nbytes, transcendentals=0),
    )(*args)


def sds(shape, dtype=BF16):
    return jax.ShapeDtypeStruct(shape, dtype)


def dot(a, b):
    return jnp.dot(a, b, preferred_element_type=F32)


def dot_nt(a, b):
    return lax.dot_general(a, b, NT, preferred_element_type=F32)


def swap(x, axis):
    return lax.ppermute(x, axis, [(0, 1), (1, 0)])


def exchange(x):
    return lax.all_to_all(x, YX, 0, 0, tiled=False)


def ranks(inside, base):
    before = lax.broadcasted_iota(jnp.int32, (TOK, TOK), 0)
    after = lax.broadcasted_iota(jnp.int32, (TOK, TOK), 1)
    marks = jnp.where(inside, 1.0, 0.0).astype(BF16)
    rank = dot(marks, jnp.where(before < after, 1.0, 0.0).astype(BF16))
    return jnp.where(inside, rank - base, -1.0)


def look_kernel(at, ids_ref, table_ref, out_ref, most_ref):
    vocab = table_ref.shape[0]
    most = jnp.zeros((16, 1), F32)
    for v in range(16):
        here = (ids_ref[...] >= v * vocab) & (ids_ref[...] < (v + 1) * vocab)
        most = jnp.maximum(most, jnp.sum(jnp.where(here, 1.0, 0.0), axis=1, keepdims=True))
    most_ref[...] = jnp.broadcast_to(jnp.max(most, axis=0, keepdims=True), (8, TOK))
    ids = ids_ref[...] - at[0]
    key = ranks((ids >= 0) & (ids < vocab), (at[1] * SLOTS).astype(F32))
    ids = ids.astype(F32) + 1.0
    slot = lax.broadcasted_iota(jnp.int32, (SLOTS, TOK), 0).astype(F32)
    lanes = lax.broadcasted_iota(jnp.int32, (4 * SLOTS, vocab), 1).astype(F32)
    table = table_ref[...]
    for g in range(4):
        rows = []
        for o in range(4 * g, 4 * g + 4):
            hit = jnp.where(slot == key[o : o + 1], ids[o : o + 1], 0.0)
            rows.append(jnp.sum(hit, axis=1, keepdims=True) - 1.0)
        hot = jnp.where(lanes == jnp.concatenate(rows, axis=0), 1.0, 0.0).astype(BF16)
        found = dot(hot, table).astype(BF16)
        for o in range(4):
            out_ref[4 * g + o] = found[o * SLOTS : (o + 1) * SLOTS]


def place_kernel(vocab, at, ids_ref, rows_ref, out_ref):
    ids = jnp.broadcast_to(ids_ref[...], (16, TOK))
    first = lax.broadcasted_iota(jnp.int32, (16, TOK), 0) * vocab
    key = ranks((ids >= first) & (ids < first + vocab), (at[1] * SLOTS).astype(F32))
    slot = lax.broadcasted_iota(jnp.int32, (SLOTS, TOK), 0).astype(F32)
    hits = [jnp.where(slot == key[v : v + 1], 1.0, 0.0) for v in range(16)]
    hits = jnp.concatenate(hits, axis=0).T.astype(BF16)
    rows = jnp.concatenate([rows_ref[v] for v in range(16)], axis=0)
    out_ref[...] = dot(hits, rows).astype(BF16)


def split_row(row):
    hi = row.astype(BF16)
    lo = (row - hi.astype(F32)).astype(BF16)
    return jnp.broadcast_to(jnp.concatenate([hi, lo], axis=1), (TAIL, COLS))


def join_row(tail):
    both = tail.astype(F32)[0:1]
    return both[:, :TOK] + both[:, TOK:]


def blocks(place, grow):
    for d in range(8):
        yield lax.rem(place[1] + d, 8), grow[d]


def spread_kernel(rows, out):
    for b in range(8):
        out[b] = rows[...]


def hidden_kernel(place, got, other, *refs):
    grow, (part, sent) = refs[:8], refs[8:]
    c = place[0]
    total = jnp.zeros((ROWS, 2 * TOK), F32)
    for b, cols in blocks(place, grow):
        total += dot_nt(cols[...], jnp.concatenate([got[b], other[b]], axis=0))
    for t, rows in ((c, total[:, :TOK]), (1 - c, total[:, TOK:])):
        part[t] = rows
        sent[t] = rows.astype(BF16)


def in_kernel(place, part, peer, gain, og, *refs):
    grow, (hidden_ref, keep, send) = refs[:8], refs[8:]
    c = place[0]
    left = []
    for t, to in ((c, keep), (1 - c, send)):
        hidden = part[t] + peer[t].astype(F32)
        hidden_ref[t] = hidden
        left += [(hidden * gain[...].astype(F32)).T.astype(BF16), og[t]]
        tail = split_row(jnp.sum(hidden * hidden, axis=0, keepdims=True))
        for b in range(8):
            to[b, 2 * TOK :] = tail
    left = jnp.concatenate(left, axis=0)
    for b, cols in blocks(place, grow):
        both = dot(left, cols[...]).astype(BF16)
        keep[b, : 2 * TOK] = both[: 2 * TOK]
        send[b, : 2 * TOK] = both[2 * TOK :]


def second_kernel(keep, recv, out):
    tail = split_row(join_row(keep[0, 2 * TOK :]) + join_row(recv[0, 2 * TOK :]))
    for b in range(8):
        mine = keep[b, : 2 * TOK].astype(F32)
        out[b, : 2 * TOK] = (mine + recv[b, : 2 * TOK].astype(F32)).astype(BF16)
        out[b, 2 * TOK :] = tail


def mid_kernel(got, out, inv_ref):
    both = got[0, : 2 * TOK].astype(F32)
    row = join_row(got[0, 2 * TOK :])
    for b in range(1, 8):
        both += got[b, : 2 * TOK].astype(F32)
        row += join_row(got[b, 2 * TOK :])
    inv = lax.rsqrt(jnp.broadcast_to(row, (TOK, TOK)) / D2 + EPS)
    inv_ref[...] = inv[0:8]
    out[:TOK] = (both[:TOK] * inv.T[:, 0:1]).astype(BF16)
    out[TOK:] = both[TOK:].astype(BF16)


def proj_kernel(place, turned, proj, keep, send):
    c = place[0]
    back = turned[TOK:]
    for b in range(8):
        keep[b] = dot_nt(back, proj[2 * b + c]).astype(BF16)
        send[b] = dot_nt(back, proj[2 * b + 1 - c]).astype(BF16)


def third_kernel(turned, keep, recv, out):
    for b in range(8):
        out[b, :TOK] = turned[:TOK]
        out[b, TOK:] = (keep[b].astype(F32) + recv[b].astype(F32)).astype(BF16)


def out_kernel(place, turned, got, other, proj, out, stat_ref):
    c = place[0]
    total = jnp.zeros((TOK, COLS), F32)
    back = jnp.zeros((TOK, COLS), F32)
    for b in range(8):
        total += dot(got[b, :TOK], proj[2 * b + c])
        total += dot(other[b], proj[2 * b + 1 - c])
        back += got[b, TOK:].astype(F32)
    back = back.astype(BF16)
    out[:TOK] = total.astype(BF16)
    out[TOK:] = back
    stat = jnp.sum(back.astype(F32) * turned[:TOK].astype(F32), axis=1, keepdims=True)
    stat_ref[...] = split_row(jnp.broadcast_to(stat, (TOK, TOK)).T[0:1])


def fourth_kernel(turned, stat, out):
    for b in range(8):
        out[b, : 2 * TOK] = turned[...]
        out[b, 2 * TOK :] = stat[...]


def grad_kernel(place, got, other, *refs):
    grow, (part, sent) = refs[:8], refs[8:]
    c = place[0]
    total = jnp.zeros((ROWS, 2 * TOK), F32)
    for b, cols in blocks(place, grow):
        pair = jnp.concatenate([got[b, TOK : 2 * TOK], other[b, :TOK]], axis=0)
        total += dot_nt(cols[...], pair)
    stat = jnp.zeros((1, TOK), F32)
    for b in range(8):
        stat += join_row(got[b, 2 * TOK :]) + join_row(other[b, TOK:])
    both = split_row(stat)
    tail = jnp.concatenate([both[:8, :TOK].astype(F32), both[:8, TOK:].astype(F32)], axis=0)
    for t, rows in ((c, total[:, :TOK]), (1 - c, total[:, TOK:])):
        part[t] = rows
        sent[t, :ROWS] = rows.astype(BF16)
        sent[t, ROWS:] = tail.astype(BF16)


def left_kernel(place, part, peer, hidden_ref, inv_c, inv_o, sent, gain_ref, og_ref, out):
    c = place[0]
    xl = place[2]
    gain = gain_ref[...].astype(F32)
    hidden_grads, normeds, ogs = [], [], []
    for t, inv_ref in ((c, inv_c), (1 - c, inv_o)):
        inv = inv_ref[0:1]
        tail = jnp.where(t == xl, sent[0, ROWS:].astype(F32), peer[0, ROWS:].astype(F32))
        mean = (tail[0:1] + tail[8:9]) / inv / D2
        hidden = hidden_ref[t]
        og = og_ref[t].astype(F32).T
        scaled = (part[t] + peer[t, :ROWS].astype(F32)) * gain
        hidden_grads.append(og + inv * scaled - hidden * inv * inv * inv * mean)
        normeds.append(hidden * inv * gain)
        ogs.append(og)
    out[...] = jnp.concatenate(hidden_grads + normeds + ogs, axis=1).astype(BF16)


def last_kernel(steps, place, left_ref, emb_m, emb_o, late, back_o, out_o, *outs):
    z = place[1]
    left = left_ref[...]
    half = ROWS // 2
    for at, d in enumerate(steps):
        b = lax.rem(z + d, 8)
        right = jnp.concatenate(
            [
                emb_m[b],
                emb_o[b],
                late[b, TOK : 2 * TOK],
                back_o[b, :TOK],
                late[b, :TOK],
                out_o[b],
            ],
            axis=0,
        )
        total = dot(left, right).astype(BF16)
        if d == 4:
            outs[at][...] = total[:half]
            outs[-1][...] = total[half:]
        else:
            outs[at][...] = total


def end_kernel(mine, above, below, out):
    out[...] = mine[...].astype(F32) + above[...].astype(F32) + below[...].astype(F32)


def join_kernel(half, mine, near, far, out):
    start = half * (ROWS // 2)
    out[...] = (mine[...].astype(F32) + near[...].astype(F32)).astype(BF16)
    rows = pl.ds(start, ROWS // 2)
    total = mine[rows].astype(F32) + near[rows].astype(F32) + far[...].astype(F32)
    out[rows] = total.astype(BF16)


def turn(x):
    return lax.ppermute(x, ("xl", "c"), [(0, 0), (1, 2), (2, 1), (3, 3)])


def up(v):
    return lax.ppermute(v, "z", [(i, (i + 1) % 8) for i in range(8)])


def down(v):
    return lax.ppermute(v, "z", [(i, (i - 1) % 8) for i in range(8)])


def shards(token_ids, embed, proj, grow_op, norm_gain, out_grad):
    c = lax.axis_index("c")
    z = lax.axis_index("z")
    xl = lax.axis_index("xl")
    place = jnp.stack([c, z, xl]).astype(jnp.int32)
    gain = norm_gain.reshape(ROWS, 1)
    proj = proj.reshape(16, COLS, COLS)
    block = sds((8, TOK, COLS))
    work = 2 * TOK * ROWS * 4096

    with jax.named_scope("embedding"):
        ids = lax.all_to_all(
            jnp.broadcast_to(token_ids.reshape(1, 1, TOK), (16, 1, TOK)), OP, 0, 0, tiled=False
        )
        near = up(grow_op), down(grow_op)
        ids, near = lax.optimization_barrier((ids, near))
        ups, downs = [up(near[0])], [down(near[1])]
        ids = ids.reshape(16, TOK)
        vocab = embed.shape[0]
        first = (z * 2 + xl) * vocab
        own = token_ids.reshape(1, TOK)

        def one(k, held=None):
            at = jnp.stack([first, k]).astype(jnp.int32)
            rows, most = call(
                look_kernel,
                [sds((16, SLOTS, COLS)), sds((8, TOK), F32)],
                at,
                ids,
                embed,
                flops=2 * 16 * SLOTS * vocab * COLS,
            )
            rows, held = lax.optimization_barrier((rows, held))
            rows = lax.all_to_all(rows, OP, 0, 0, tiled=False)
            if held:
                step = up(held[0]), down(held[1]), swap(held[2], "xl")
                rows, step = lax.optimization_barrier((rows, step))
                held = (*held[:2], *step)
            part = call(
                functools.partial(place_kernel, vocab),
                sds((TOK, COLS)),
                at,
                own,
                rows,
                flops=2 * 16 * SLOTS * TOK * COLS,
            )
            return part, most[0, 0], held

        half = ROWS // 2
        found, most, held = one(jnp.int32(0), (ups[0], downs[0], out_grad))
        ups, downs, og_peer = [held[0], held[2]], [held[1], held[3]], held[4]
        found = lax.while_loop(
            lambda state: (state[0] * SLOTS).astype(F32) < most,
            lambda state: (state[0] + 1, state[1] + one(state[0])[0]),
            (jnp.int32(1), found),
        )
        emb_part = turn(found[1])
        far = [up(ups[1][:half]), down(downs[1][half:])]

    with jax.named_scope("operator"):
        og = jnp.stack([jnp.where(xl == 0, out_grad, og_peer), jnp.where(xl == 0, og_peer, out_grad)])

    with jax.named_scope("first"):
        emb = exchange(call(spread_kernel, block, emb_part))
        emb, far = lax.optimization_barrier((emb, far))
        first_up, first_down = near
        grow = [grow_op, first_down, *downs, jnp.concatenate(far, axis=0), *ups[::-1], first_up]
        emb_other = swap(emb, "c")

    with jax.named_scope("hidden"):
        pair = sds((2, ROWS, TOK), F32)
        part, sent = call(
            hidden_kernel,
            [pair, sds((2, ROWS, TOK))],
            place,
            emb,
            emb_other,
            *grow,
            flops=work,
        )
        longer = sds((8, 2 * TOK + TAIL, COLS))
        hidden, keep, send = call(
            in_kernel,
            [pair, longer, longer],
            place,
            part,
            swap(sent, "xl"),
            gain,
            og,
            *grow,
            flops=2 * work,
        )

    with jax.named_scope("second"):
        got = exchange(call(second_kernel, longer, keep, swap(send, "c")))
        before, inv = call(mid_kernel, [sds((2 * TOK, COLS)), sds((8, TOK), F32)], got)
        turned, inv_other = lax.optimization_barrier((turn(before), swap(inv, "c")))

    with jax.named_scope("third"):
        keep, send = call(
            proj_kernel, [block, block], place, turned, proj, flops=2 * TOK * COLS * 4096
        )
        got = exchange(
            call(third_kernel, sds((8, 2 * TOK, COLS)), turned, keep, swap(send, "c"))
        )
        out, stat = call(
            out_kernel,
            [sds((2 * TOK, COLS)), sds((TAIL, COLS))],
            place,
            turned,
            got,
            swap(got[:, :TOK], "c"),
            proj,
            flops=2 * TOK * COLS * 4096,
        )

    with jax.named_scope("fourth"):
        late = exchange(call(fourth_kernel, longer, turn(out), stat))
        back_other = swap(late[:, TOK:], "c")
        part, sent = call(
            grad_kernel,
            [pair, sds((2, ROWS + TAIL, TOK))],
            place,
            late,
            back_other,
            *grow,
            flops=work,
        )
        late, sent = lax.optimization_barrier((late, sent))
        out_other = swap(late[:, :TOK], "c")
        peer = swap(sent, "xl")
        left = call(
            left_kernel,
            sds((ROWS, 6 * TOK)),
            place,
            part,
            peer,
            hidden,
            inv,
            inv_other,
            sent,
            gain,
            og,
        )
        x = {}
        for steps in ((4, 3, 5), (2, 6, 1, 7, 0)):
            parts = call(
                functools.partial(last_kernel, steps),
                [sds((ROWS // 2, COLS) if d == 4 else (ROWS, COLS)) for d in steps]
                + [sds((ROWS // 2, COLS))] * (4 in steps),
                place,
                left,
                emb,
                emb_other,
                late,
                back_other,
                out_other,
                flops=3 * work * len(steps) // 8,
            )
            x.update(zip(steps, parts))
            if 4 in steps:
                x[8] = parts[-1]

    def add(a, b):
        return (a.astype(F32) + b.astype(F32)).astype(BF16)

    with jax.named_scope("scatter"):
        up_far = lax.ppermute(x[4], "z", [(i, (i + 2) % 8) for i in range(8)])
        down_far = lax.ppermute(x[8], "z", [(i, (i - 2) % 8) for i in range(8)])
        above, below = up(x[3]), down(x[5])
        near = above, below, up_far, down_far
        above, below, up_far, down_far = lax.optimization_barrier(near)
        tile = sds((ROWS, COLS))
        above = up(call(functools.partial(join_kernel, 0), tile, x[2], above, up_far))
        below = down(call(functools.partial(join_kernel, 1), tile, x[6], below, down_far))
        above, below = up(add(above, x[1])), down(add(below, x[7]))
        return call(end_kernel, sds((ROWS, COLS), F32), x[0], above, below)


def solution(mesh):
    fine = Mesh(mesh.devices.reshape(8, 2, 4, 2, 2), ("z", "xl", "y", "xh", "c"))
    in_specs = (P(OP), P(OP, TP), P(None, TP), P(TP, OP), P(TP), P(OP, TP))
    return jax.shard_map(shards, mesh=fine, in_specs=in_specs, out_specs=P(TP, OP), check_vma=False)
```

```python
import functools

import jax
import jax.numpy as jnp
import numpy as np
from jax import lax
from jax.experimental import pallas as pl
from jax.experimental.pallas import tpu as pltpu
from jax.sharding import Mesh, PartitionSpec as P

D2 = 6656
EPS = 1e-05
TOK = 128
ROWS = 416
COLS = 256
TAIL = 16
SLOTS = 48
OP = ("z", "xl")
TP = ("y", "xh", "c")
YX = ("y", "xh")
F32 = jnp.float32
BF16 = jnp.bfloat16
NT = (((1,), (1,)), ((), ()))


def call(kernel, out_shape, *args, flops=0):
    smem = pl.BlockSpec(memory_space=pltpu.SMEM)
    vmem = pl.BlockSpec(memory_space=pltpu.VMEM)
    single = not isinstance(out_shape, (list, tuple))
    outs = [out_shape] if single else list(out_shape)
    nbytes = sum(int(np.prod(a.shape)) * a.dtype.itemsize for a in list(args) + outs)
    return pl.pallas_call(
        kernel,
        out_shape=out_shape,
        in_specs=[smem if a.dtype == jnp.int32 and a.ndim == 1 else vmem for a in args],
        out_specs=vmem if single else [vmem] * len(outs),
        compiler_params=pltpu.CompilerParams(vmem_limit_bytes=20 * 1024 * 1024),
        cost_estimate=pl.CostEstimate(flops=flops, bytes_accessed=nbytes, transcendentals=0),
    )(*args)


def sds(shape, dtype=BF16):
    return jax.ShapeDtypeStruct(shape, dtype)


def dot(a, b):
    return jnp.dot(a, b, preferred_element_type=F32)


def dot_nt(a, b):
    return lax.dot_general(a, b, NT, preferred_element_type=F32)


def swap(x, axis):
    return lax.ppermute(x, axis, [(0, 1), (1, 0)])


def exchange(x):
    return lax.all_to_all(x, YX, 0, 0, tiled=False)


def ranks(inside, base):
    before = lax.broadcasted_iota(jnp.int32, (TOK, TOK), 0)
    after = lax.broadcasted_iota(jnp.int32, (TOK, TOK), 1)
    marks = jnp.where(inside, 1.0, 0.0).astype(BF16)
    rank = dot(marks, jnp.where(before < after, 1.0, 0.0).astype(BF16))
    return jnp.where(inside, rank - base, -1.0)


def look_kernel(at, ids_ref, table_ref, out_ref, most_ref):
    vocab = table_ref.shape[0]
    most = jnp.zeros((16, 1), F32)
    for v in range(16):
        here = (ids_ref[...] >= v * vocab) & (ids_ref[...] < (v + 1) * vocab)
        most = jnp.maximum(most, jnp.sum(jnp.where(here, 1.0, 0.0), axis=1, keepdims=True))
    most_ref[...] = jnp.broadcast_to(jnp.max(most, axis=0, keepdims=True), (8, TOK))
    ids = ids_ref[...] - at[0]
    key = ranks((ids >= 0) & (ids < vocab), (at[1] * SLOTS).astype(F32))
    ids = ids.astype(F32) + 1.0
    slot = lax.broadcasted_iota(jnp.int32, (SLOTS, TOK), 0).astype(F32)
    lanes = lax.broadcasted_iota(jnp.int32, (4 * SLOTS, TOK), 1).astype(F32)
    table = table_ref[...]
    for g in range(4):
        rows = []
        for o in range(4 * g, 4 * g + 4):
            hit = jnp.where(slot == key[o : o + 1], ids[o : o + 1], 0.0)
            rows.append(jnp.sum(hit, axis=1, keepdims=True) - 1.0)
        rows = jnp.broadcast_to(jnp.concatenate(rows, axis=0), (4 * SLOTS, TOK))
        group = jnp.floor(rows / TOK)
        low = jnp.where(lanes == rows - group * TOK, 1.0, 0.0).astype(BF16)
        group = group.astype(BF16)
        none = jnp.zeros_like(low)
        hot = [jnp.where(group == jnp.asarray(i, BF16), low, none) for i in range(-(-vocab // TOK))]
        hot = jnp.concatenate(hot, axis=1)[:, :vocab]
        found = dot(hot, table).astype(BF16)
        for o in range(4):
            out_ref[4 * g + o] = found[o * SLOTS : (o + 1) * SLOTS]


def place_kernel(vocab, at, ids_ref, rows_ref, out_ref):
    ids = jnp.broadcast_to(ids_ref[...], (16, TOK))
    first = lax.broadcasted_iota(jnp.int32, (16, TOK), 0) * vocab
    key = ranks((ids >= first) & (ids < first + vocab), (at[1] * SLOTS).astype(F32))
    slot = lax.broadcasted_iota(jnp.int32, (SLOTS, TOK), 0).astype(F32)
    hits = [jnp.where(slot == key[v : v + 1], 1.0, 0.0) for v in range(16)]
    hits = jnp.concatenate(hits, axis=0).T.astype(BF16)
    rows = jnp.concatenate([rows_ref[v] for v in range(16)], axis=0)
    out_ref[...] = dot(hits, rows).astype(BF16)


def split_row(row):
    hi = row.astype(BF16)
    lo = (row - hi.astype(F32)).astype(BF16)
    return jnp.broadcast_to(jnp.concatenate([hi, lo], axis=1), (TAIL, COLS))


def join_row(tail):
    both = tail.astype(F32)[0:1]
    return both[:, :TOK] + both[:, TOK:]


def blocks(place, grow):
    for d in range(8):
        yield lax.rem(place[1] + d, 8), grow[d]


def spread_kernel(rows, out):
    for b in range(8):
        out[b] = rows[...]


def hidden_kernel(place, got, other, *refs):
    grow, (part, sent) = refs[:8], refs[8:]
    c = place[0]
    total = jnp.zeros((ROWS, 2 * TOK), F32)
    for b, cols in blocks(place, grow):
        total += dot_nt(cols[...], jnp.concatenate([got[b], other[b]], axis=0))
    for t, rows in ((c, total[:, :TOK]), (1 - c, total[:, TOK:])):
        part[t] = rows
        sent[t] = rows.astype(BF16)


def in_kernel(place, part, peer, gain, og, *refs):
    grow, (hidden_ref, keep, send) = refs[:8], refs[8:]
    c = place[0]
    left = []
    for t, to in ((c, keep), (1 - c, send)):
        hidden = part[t] + peer[t].astype(F32)
        hidden_ref[t] = hidden
        left += [(hidden * gain[...].astype(F32)).T.astype(BF16), og[t]]
        tail = split_row(jnp.sum(hidden * hidden, axis=0, keepdims=True))
        for b in range(8):
            to[b, 2 * TOK :] = tail
    left = jnp.concatenate(left, axis=0)
    for b, cols in blocks(place, grow):
        both = dot(left, cols[...]).astype(BF16)
        keep[b, : 2 * TOK] = both[: 2 * TOK]
        send[b, : 2 * TOK] = both[2 * TOK :]


def second_kernel(keep, recv, out):
    tail = split_row(join_row(keep[0, 2 * TOK :]) + join_row(recv[0, 2 * TOK :]))
    for b in range(8):
        mine = keep[b, : 2 * TOK].astype(F32)
        out[b, : 2 * TOK] = (mine + recv[b, : 2 * TOK].astype(F32)).astype(BF16)
        out[b, 2 * TOK :] = tail


def mid_kernel(got, out, inv_ref):
    both = got[0, : 2 * TOK].astype(F32)
    row = join_row(got[0, 2 * TOK :])
    for b in range(1, 8):
        both += got[b, : 2 * TOK].astype(F32)
        row += join_row(got[b, 2 * TOK :])
    inv = lax.rsqrt(jnp.broadcast_to(row, (TOK, TOK)) / D2 + EPS)
    inv_ref[...] = inv[0:8]
    out[:TOK] = (both[:TOK] * inv.T[:, 0:1]).astype(BF16)
    out[TOK:] = both[TOK:].astype(BF16)


def proj_kernel(place, turned, proj, keep, send):
    c = place[0]
    back = turned[TOK:]
    for b in range(8):
        keep[b] = dot_nt(back, proj[2 * b + c]).astype(BF16)
        send[b] = dot_nt(back, proj[2 * b + 1 - c]).astype(BF16)


def third_kernel(turned, keep, recv, out):
    for b in range(8):
        out[b, :TOK] = turned[:TOK]
        out[b, TOK:] = (keep[b].astype(F32) + recv[b].astype(F32)).astype(BF16)


def out_kernel(place, turned, got, other, proj, out, stat_ref):
    c = place[0]
    total = jnp.zeros((TOK, COLS), F32)
    back = jnp.zeros((TOK, COLS), F32)
    for b in range(8):
        total += dot(got[b, :TOK], proj[2 * b + c])
        total += dot(other[b], proj[2 * b + 1 - c])
        back += got[b, TOK:].astype(F32)
    back = back.astype(BF16)
    out[:TOK] = total.astype(BF16)
    out[TOK:] = back
    stat = jnp.sum(back.astype(F32) * turned[:TOK].astype(F32), axis=1, keepdims=True)
    stat_ref[...] = split_row(jnp.broadcast_to(stat, (TOK, TOK)).T[0:1])


def fourth_kernel(turned, stat, out):
    for b in range(8):
        out[b, : 2 * TOK] = turned[...]
        out[b, 2 * TOK :] = stat[...]


def grad_kernel(place, got, other, *refs):
    grow, (part, sent) = refs[:8], refs[8:]
    c = place[0]
    total = jnp.zeros((ROWS, 2 * TOK), F32)
    for b, cols in blocks(place, grow):
        pair = jnp.concatenate([got[b, TOK : 2 * TOK], other[b, :TOK]], axis=0)
        total += dot_nt(cols[...], pair)
    stat = jnp.zeros((1, TOK), F32)
    for b in range(8):
        stat += join_row(got[b, 2 * TOK :]) + join_row(other[b, TOK:])
    both = split_row(stat)
    tail = jnp.concatenate([both[:8, :TOK].astype(F32), both[:8, TOK:].astype(F32)], axis=0)
    for t, rows in ((c, total[:, :TOK]), (1 - c, total[:, TOK:])):
        part[t] = rows
        sent[t, :ROWS] = rows.astype(BF16)
        sent[t, ROWS:] = tail.astype(BF16)


def left_kernel(place, part, peer, hidden_ref, inv_c, inv_o, sent, gain_ref, og_ref, out):
    c = place[0]
    xl = place[2]
    gain = gain_ref[...].astype(F32)
    hidden_grads, normeds, ogs = [], [], []
    for t, inv_ref in ((c, inv_c), (1 - c, inv_o)):
        inv = inv_ref[0:1]
        tail = jnp.where(t == xl, sent[0, ROWS:].astype(F32), peer[0, ROWS:].astype(F32))
        mean = (tail[0:1] + tail[8:9]) / inv / D2
        hidden = hidden_ref[t]
        og = og_ref[t].astype(F32).T
        scaled = (part[t] + peer[t, :ROWS].astype(F32)) * gain
        hidden_grads.append(og + inv * scaled - hidden * inv * inv * inv * mean)
        normeds.append(hidden * inv * gain)
        ogs.append(og)
    out[...] = jnp.concatenate(hidden_grads + normeds + ogs, axis=1).astype(BF16)


def last_kernel(steps, place, left_ref, emb_m, emb_o, late, back_o, out_o, *outs):
    z = place[1]
    left = left_ref[...]
    half = ROWS // 2
    for at, d in enumerate(steps):
        b = lax.rem(z + d, 8)
        right = jnp.concatenate(
            [
                emb_m[b],
                emb_o[b],
                late[b, TOK : 2 * TOK],
                back_o[b, :TOK],
                late[b, :TOK],
                out_o[b],
            ],
            axis=0,
        )
        total = dot(left, right).astype(BF16)
        if d == 4:
            outs[at][...] = total[:half]
            outs[-1][...] = total[half:]
        else:
            outs[at][...] = total


def end_kernel(mine, above, below, out):
    out[...] = mine[...].astype(F32) + above[...].astype(F32) + below[...].astype(F32)


def join_kernel(half, mine, near, far, out):
    start = half * (ROWS // 2)
    out[...] = (mine[...].astype(F32) + near[...].astype(F32)).astype(BF16)
    rows = pl.ds(start, ROWS // 2)
    total = mine[rows].astype(F32) + near[rows].astype(F32) + far[...].astype(F32)
    out[rows] = total.astype(BF16)


def turn(x):
    return lax.ppermute(x, ("xl", "c"), [(0, 0), (1, 2), (2, 1), (3, 3)])


def up(v):
    return lax.ppermute(v, "z", [(i, (i + 1) % 8) for i in range(8)])


def down(v):
    return lax.ppermute(v, "z", [(i, (i - 1) % 8) for i in range(8)])


def shards(token_ids, embed, proj, grow_op, norm_gain, out_grad):
    c = lax.axis_index("c")
    z = lax.axis_index("z")
    xl = lax.axis_index("xl")
    place = jnp.stack([c, z, xl]).astype(jnp.int32)
    gain = norm_gain.reshape(ROWS, 1)
    proj = proj.reshape(16, COLS, COLS)
    block = sds((8, TOK, COLS))
    work = 2 * TOK * ROWS * 4096

    with jax.named_scope("embedding"):
        ids = lax.all_to_all(
            jnp.broadcast_to(token_ids.reshape(1, 1, TOK), (16, 1, TOK)), OP, 0, 0, tiled=False
        )
        near = up(grow_op), down(grow_op)
        ids, near = lax.optimization_barrier((ids, near))
        ups, downs = [up(near[0])], [down(near[1])]
        ids = ids.reshape(16, TOK)
        vocab = embed.shape[0]
        first = (z * 2 + xl) * vocab
        own = token_ids.reshape(1, TOK)

        def one(k, held=None):
            at = jnp.stack([first, k]).astype(jnp.int32)
            rows, most = call(
                look_kernel,
                [sds((16, SLOTS, COLS)), sds((8, TOK), F32)],
                at,
                ids,
                embed,
                flops=2 * 16 * SLOTS * vocab * COLS,
            )
            rows, held = lax.optimization_barrier((rows, held))
            rows = lax.all_to_all(rows, OP, 0, 0, tiled=False)
            if held:
                step = up(held[0]), down(held[1]), swap(held[2], "xl")
                rows, step = lax.optimization_barrier((rows, step))
                held = (*held[:2], *step)
            part = call(
                functools.partial(place_kernel, vocab),
                sds((TOK, COLS)),
                at,
                own,
                rows,
                flops=2 * 16 * SLOTS * TOK * COLS,
            )
            return part, most[0, 0], held

        half = ROWS // 2
        found, most, held = one(jnp.int32(0), (ups[0], downs[0], out_grad))
        ups, downs, og_peer = [held[0], held[2]], [held[1], held[3]], held[4]
        found = lax.while_loop(
            lambda state: (state[0] * SLOTS).astype(F32) < most,
            lambda state: (state[0] + 1, state[1] + one(state[0])[0]),
            (jnp.int32(1), found),
        )
        emb_part = turn(found[1])
        far = [up(ups[1][:half]), down(downs[1][half:])]

    with jax.named_scope("operator"):
        og = jnp.stack([jnp.where(xl == 0, out_grad, og_peer), jnp.where(xl == 0, og_peer, out_grad)])

    with jax.named_scope("first"):
        emb = exchange(call(spread_kernel, block, emb_part))
        emb, far = lax.optimization_barrier((emb, far))
        first_up, first_down = near
        grow = [grow_op, first_down, *downs, jnp.concatenate(far, axis=0), *ups[::-1], first_up]
        emb_other = swap(emb, "c")

    with jax.named_scope("hidden"):
        pair = sds((2, ROWS, TOK), F32)
        part, sent = call(
            hidden_kernel,
            [pair, sds((2, ROWS, TOK))],
            place,
            emb,
            emb_other,
            *grow,
            flops=work,
        )
        longer = sds((8, 2 * TOK + TAIL, COLS))
        hidden, keep, send = call(
            in_kernel,
            [pair, longer, longer],
            place,
            part,
            swap(sent, "xl"),
            gain,
            og,
            *grow,
            flops=2 * work,
        )

    with jax.named_scope("second"):
        got = exchange(call(second_kernel, longer, keep, swap(send, "c")))
        before, inv = call(mid_kernel, [sds((2 * TOK, COLS)), sds((8, TOK), F32)], got)
        turned = turn(before)

    with jax.named_scope("third"):
        keep, send = call(
            proj_kernel, [block, block], place, turned, proj, flops=2 * TOK * COLS * 4096
        )
        got = exchange(
            call(third_kernel, sds((8, 2 * TOK, COLS)), turned, keep, swap(send, "c"))
        )
        out, stat = call(
            out_kernel,
            [sds((2 * TOK, COLS)), sds((TAIL, COLS))],
            place,
            turned,
            got,
            swap(got[:, :TOK], "c"),
            proj,
            flops=2 * TOK * COLS * 4096,
        )

    with jax.named_scope("fourth"):
        late = exchange(call(fourth_kernel, longer, turn(out), stat))
        back_other = swap(late[:, TOK:], "c")
        part, sent = call(
            grad_kernel,
            [pair, sds((2, ROWS + TAIL, TOK))],
            place,
            late,
            back_other,
            *grow,
            flops=work,
        )
        late, sent, inv_late = lax.optimization_barrier((late, sent, inv))
        inv_other = swap(inv_late, "c")
        out_other = swap(late[:, :TOK], "c")
        peer = swap(sent, "xl")
        left = call(
            left_kernel,
            sds((ROWS, 6 * TOK)),
            place,
            part,
            peer,
            hidden,
            inv,
            inv_other,
            sent,
            gain,
            og,
        )
        x = {}
        for steps in ((4,), (3, 5), (2, 6, 1, 7, 0)):
            parts = call(
                functools.partial(last_kernel, steps),
                [sds((ROWS // 2, COLS) if d == 4 else (ROWS, COLS)) for d in steps]
                + [sds((ROWS // 2, COLS))] * (4 in steps),
                place,
                left,
                emb,
                emb_other,
                late,
                back_other,
                out_other,
                flops=3 * work * len(steps) // 8,
            )
            left, parts = lax.optimization_barrier((left, parts))
            x.update(zip(steps, parts))
            if 4 in steps:
                x[8] = parts[-1]

    def add(a, b):
        return (a.astype(F32) + b.astype(F32)).astype(BF16)

    with jax.named_scope("scatter"):
        up_far = lax.ppermute(x[4], "z", [(i, (i + 2) % 8) for i in range(8)])
        down_far = lax.ppermute(x[8], "z", [(i, (i - 2) % 8) for i in range(8)])
        above, below = up(x[3]), down(x[5])
        near = above, below, up_far, down_far
        above, below, up_far, down_far = lax.optimization_barrier(near)
        tile = sds((ROWS, COLS))
        above = up(call(functools.partial(join_kernel, 0), tile, x[2], above, up_far))
        below = down(call(functools.partial(join_kernel, 1), tile, x[6], below, down_far))
        above, below = up(add(above, x[1])), down(add(below, x[7]))
        return call(end_kernel, sds((ROWS, COLS), F32), x[0], above, below)


def solution(mesh):
    fine = Mesh(mesh.devices.reshape(8, 2, 4, 2, 2), ("z", "xl", "y", "xh", "c"))
    in_specs = (P(OP), P(OP, TP), P(None, TP), P(TP, OP), P(TP), P(OP, TP))
    return jax.shard_map(shards, mesh=fine, in_specs=in_specs, out_specs=P(TP, OP), check_vma=False)
```

```python
import functools

import jax
import jax.numpy as jnp
import numpy as np
from jax import lax
from jax.experimental import pallas as pl
from jax.experimental.pallas import tpu as pltpu
from jax.sharding import Mesh, PartitionSpec as P

D2 = 6656
EPS = 1e-05
TOK = 128
ROWS = 416
COLS = 256
TAIL = 16
SLOTS = 48
OP = ("z", "xl")
TP = ("y", "xh", "c")
YX = ("y", "xh")
F32 = jnp.float32
BF16 = jnp.bfloat16
NT = (((1,), (1,)), ((), ()))


def call(kernel, out_shape, *args, flops=0):
    smem = pl.BlockSpec(memory_space=pltpu.SMEM)
    vmem = pl.BlockSpec(memory_space=pltpu.VMEM)
    single = not isinstance(out_shape, (list, tuple))
    outs = [out_shape] if single else list(out_shape)
    nbytes = sum(int(np.prod(a.shape)) * a.dtype.itemsize for a in list(args) + outs)
    return pl.pallas_call(
        kernel,
        out_shape=out_shape,
        in_specs=[smem if a.dtype == jnp.int32 and a.ndim == 1 else vmem for a in args],
        out_specs=vmem if single else [vmem] * len(outs),
        compiler_params=pltpu.CompilerParams(vmem_limit_bytes=20 * 1024 * 1024),
        cost_estimate=pl.CostEstimate(flops=flops, bytes_accessed=nbytes, transcendentals=0),
    )(*args)


def sds(shape, dtype=BF16):
    return jax.ShapeDtypeStruct(shape, dtype)


def dot(a, b):
    return jnp.dot(a, b, preferred_element_type=F32)


def dot_nt(a, b):
    return lax.dot_general(a, b, NT, preferred_element_type=F32)


def swap(x, axis):
    return lax.ppermute(x, axis, [(0, 1), (1, 0)])


def exchange(x):
    return lax.all_to_all(x, YX, 0, 0, tiled=False)


def ranks(inside, base):
    before = lax.broadcasted_iota(jnp.int32, (TOK, TOK), 0)
    after = lax.broadcasted_iota(jnp.int32, (TOK, TOK), 1)
    marks = jnp.where(inside, 1.0, 0.0).astype(BF16)
    rank = dot(marks, jnp.where(before < after, 1.0, 0.0).astype(BF16))
    return jnp.where(inside, rank - base, -1.0)


def look_kernel(at, ids_ref, table_ref, out_ref, most_ref):
    vocab = table_ref.shape[0]
    most = jnp.zeros((16, 1), F32)
    for v in range(16):
        here = (ids_ref[...] >= v * vocab) & (ids_ref[...] < (v + 1) * vocab)
        most = jnp.maximum(most, jnp.sum(jnp.where(here, 1.0, 0.0), axis=1, keepdims=True))
    most_ref[...] = jnp.broadcast_to(jnp.max(most, axis=0, keepdims=True), (8, TOK))
    ids = ids_ref[...] - at[0]
    key = ranks((ids >= 0) & (ids < vocab), (at[1] * SLOTS).astype(F32))
    ids = ids.astype(F32) + 1.0
    slot = lax.broadcasted_iota(jnp.int32, (SLOTS, TOK), 0).astype(F32)
    lanes = lax.broadcasted_iota(jnp.int32, (4 * SLOTS, vocab), 1).astype(F32)
    table = table_ref[...]
    for g in range(4):
        rows = []
        for o in range(4 * g, 4 * g + 4):
            hit = jnp.where(slot == key[o : o + 1], ids[o : o + 1], 0.0)
            rows.append(jnp.sum(hit, axis=1, keepdims=True) - 1.0)
        hot = jnp.where(lanes == jnp.concatenate(rows, axis=0), 1.0, 0.0).astype(BF16)
        found = dot(hot, table).astype(BF16)
        for o in range(4):
            out_ref[4 * g + o] = found[o * SLOTS : (o + 1) * SLOTS]


def place_kernel(vocab, at, ids_ref, rows_ref, out_ref):
    ids = jnp.broadcast_to(ids_ref[...], (16, TOK))
    first = lax.broadcasted_iota(jnp.int32, (16, TOK), 0) * vocab
    key = ranks((ids >= first) & (ids < first + vocab), (at[1] * SLOTS).astype(F32))
    slot = lax.broadcasted_iota(jnp.int32, (SLOTS, TOK), 0).astype(F32)
    hits = [jnp.where(slot == key[v : v + 1], 1.0, 0.0) for v in range(16)]
    hits = jnp.concatenate(hits, axis=0).T.astype(BF16)
    rows = jnp.concatenate([rows_ref[v] for v in range(16)], axis=0)
    out_ref[...] = dot(hits, rows).astype(BF16)


def split_row(row):
    hi = row.astype(BF16)
    lo = (row - hi.astype(F32)).astype(BF16)
    return jnp.broadcast_to(jnp.concatenate([hi, lo], axis=1), (TAIL, COLS))


def join_row(tail):
    both = tail.astype(F32)[0:1]
    return both[:, :TOK] + both[:, TOK:]


def blocks(place, grow):
    for d in range(8):
        yield lax.rem(place[1] + d, 8), grow[d]


def spread_kernel(rows, out):
    for b in range(8):
        out[b] = rows[...]


def hidden_kernel(place, got, other, *refs):
    grow, (part, sent) = refs[:8], refs[8:]
    c = place[0]
    total = jnp.zeros((ROWS, 2 * TOK), F32)
    for b, cols in blocks(place, grow):
        total += dot_nt(cols[...], jnp.concatenate([got[b], other[b]], axis=0))
    for t, rows in ((c, total[:, :TOK]), (1 - c, total[:, TOK:])):
        part[t] = rows
        sent[t] = rows.astype(BF16)


def in_kernel(place, part, peer, gain, og, *refs):
    grow, (hidden_ref, keep, send) = refs[:8], refs[8:]
    c = place[0]
    left = []
    for t, to in ((c, keep), (1 - c, send)):
        hidden = part[t] + peer[t].astype(F32)
        hidden_ref[t] = hidden
        left += [(hidden * gain[...].astype(F32)).T.astype(BF16), og[t]]
        tail = split_row(jnp.sum(hidden * hidden, axis=0, keepdims=True))
        for b in range(8):
            to[b, 2 * TOK :] = tail
    left = jnp.concatenate(left, axis=0)
    for b, cols in blocks(place, grow):
        both = dot(left, cols[...]).astype(BF16)
        keep[b, : 2 * TOK] = both[: 2 * TOK]
        send[b, : 2 * TOK] = both[2 * TOK :]


def second_kernel(keep, recv, out):
    tail = split_row(join_row(keep[0, 2 * TOK :]) + join_row(recv[0, 2 * TOK :]))
    for b in range(8):
        mine = keep[b, : 2 * TOK].astype(F32)
        out[b, : 2 * TOK] = (mine + recv[b, : 2 * TOK].astype(F32)).astype(BF16)
        out[b, 2 * TOK :] = tail


def mid_kernel(got, out, inv_ref):
    both = got[0, : 2 * TOK].astype(F32)
    row = join_row(got[0, 2 * TOK :])
    for b in range(1, 8):
        both += got[b, : 2 * TOK].astype(F32)
        row += join_row(got[b, 2 * TOK :])
    inv = lax.rsqrt(jnp.broadcast_to(row, (TOK, TOK)) / D2 + EPS)
    inv_ref[...] = inv[0:8]
    out[:TOK] = (both[:TOK] * inv.T[:, 0:1]).astype(BF16)
    out[TOK:] = both[TOK:].astype(BF16)


def proj_kernel(place, turned, proj, keep, send):
    c = place[0]
    back = turned[TOK:]
    for b in range(8):
        keep[b] = dot_nt(back, proj[2 * b + c]).astype(BF16)
        send[b] = dot_nt(back, proj[2 * b + 1 - c]).astype(BF16)


def third_kernel(turned, keep, recv, out):
    for b in range(8):
        out[b, :TOK] = turned[:TOK]
        out[b, TOK:] = (keep[b].astype(F32) + recv[b].astype(F32)).astype(BF16)


def out_kernel(place, turned, got, other, proj, out, stat_ref):
    c = place[0]
    total = jnp.zeros((TOK, COLS), F32)
    back = jnp.zeros((TOK, COLS), F32)
    for b in range(8):
        total += dot(got[b, :TOK], proj[2 * b + c])
        total += dot(other[b], proj[2 * b + 1 - c])
        back += got[b, TOK:].astype(F32)
    back = back.astype(BF16)
    out[:TOK] = total.astype(BF16)
    out[TOK:] = back
    stat = jnp.sum(back.astype(F32) * turned[:TOK].astype(F32), axis=1, keepdims=True)
    stat_ref[...] = split_row(jnp.broadcast_to(stat, (TOK, TOK)).T[0:1])


def fourth_kernel(turned, stat, out):
    for b in range(8):
        out[b, : 2 * TOK] = turned[...]
        out[b, 2 * TOK :] = stat[...]


def grad_kernel(place, got, other, *refs):
    grow, (part, sent) = refs[:8], refs[8:]
    c = place[0]
    total = jnp.zeros((ROWS, 2 * TOK), F32)
    for b, cols in blocks(place, grow):
        pair = jnp.concatenate([got[b, TOK : 2 * TOK], other[b, :TOK]], axis=0)
        total += dot_nt(cols[...], pair)
    stat = jnp.zeros((1, TOK), F32)
    for b in range(8):
        stat += join_row(got[b, 2 * TOK :]) + join_row(other[b, TOK:])
    both = split_row(stat)
    tail = jnp.concatenate([both[:8, :TOK].astype(F32), both[:8, TOK:].astype(F32)], axis=0)
    for t, rows in ((c, total[:, :TOK]), (1 - c, total[:, TOK:])):
        part[t] = rows
        sent[t, :ROWS] = rows.astype(BF16)
        sent[t, ROWS:] = tail.astype(BF16)


def left_kernel(place, part, peer, hidden_ref, inv_c, inv_o, sent, gain_ref, og_ref, out):
    c = place[0]
    xl = place[2]
    gain = gain_ref[...].astype(F32)
    hidden_grads, normeds, ogs = [], [], []
    for t, inv_ref in ((c, inv_c), (1 - c, inv_o)):
        inv = inv_ref[0:1]
        tail = jnp.where(t == xl, sent[0, ROWS:].astype(F32), peer[0, ROWS:].astype(F32))
        mean = (tail[0:1] + tail[8:9]) / inv / D2
        hidden = hidden_ref[t]
        og = og_ref[t].astype(F32).T
        scaled = (part[t] + peer[t, :ROWS].astype(F32)) * gain
        hidden_grads.append(og + inv * scaled - hidden * inv * inv * inv * mean)
        normeds.append(hidden * inv * gain)
        ogs.append(og)
    out[...] = jnp.concatenate(hidden_grads + normeds + ogs, axis=1).astype(BF16)


def last_kernel(steps, place, left_ref, emb_m, emb_o, late, back_o, out_o, *outs):
    z = place[1]
    left = left_ref[...]
    half = ROWS // 2
    for at, d in enumerate(steps):
        b = lax.rem(z + d, 8)
        right = jnp.concatenate(
            [
                emb_m[b],
                emb_o[b],
                late[b, TOK : 2 * TOK],
                back_o[b, :TOK],
                late[b, :TOK],
                out_o[b],
            ],
            axis=0,
        )
        total = dot(left, right).astype(BF16)
        if d == 4:
            outs[at][...] = total[:half]
            outs[-1][...] = total[half:]
        else:
            outs[at][...] = total


def end_kernel(mine, above, below, out):
    out[...] = mine[...].astype(F32) + above[...].astype(F32) + below[...].astype(F32)


def join_kernel(half, mine, near, far, out):
    start = half * (ROWS // 2)
    out[...] = (mine[...].astype(F32) + near[...].astype(F32)).astype(BF16)
    rows = pl.ds(start, ROWS // 2)
    total = mine[rows].astype(F32) + near[rows].astype(F32) + far[...].astype(F32)
    out[rows] = total.astype(BF16)


def turn(x):
    return lax.ppermute(x, ("xl", "c"), [(0, 0), (1, 2), (2, 1), (3, 3)])


def up(v):
    return lax.ppermute(v, "z", [(i, (i + 1) % 8) for i in range(8)])


def down(v):
    return lax.ppermute(v, "z", [(i, (i - 1) % 8) for i in range(8)])


def shards(token_ids, embed, proj, grow_op, norm_gain, out_grad):
    c = lax.axis_index("c")
    z = lax.axis_index("z")
    xl = lax.axis_index("xl")
    place = jnp.stack([c, z, xl]).astype(jnp.int32)
    gain = norm_gain.reshape(ROWS, 1)
    proj = proj.reshape(16, COLS, COLS)
    block = sds((8, TOK, COLS))
    work = 2 * TOK * ROWS * 4096

    with jax.named_scope("embedding"):
        embed = turn(embed)
        ids = lax.all_to_all(
            jnp.broadcast_to(token_ids.reshape(1, 1, TOK), (16, 1, TOK)), OP, 0, 0, tiled=False
        )
        near = up(grow_op), down(grow_op)
        ids, near = lax.optimization_barrier((ids, near))
        ups, downs = [up(near[0])], [down(near[1])]
        ids = ids.reshape(16, TOK)
        vocab = embed.shape[0]
        first = (z * 2 + c) * vocab
        own = lax.dynamic_slice_in_dim(ids, z * 2 + c, 1, axis=0)

        def one(k, held=None):
            at = jnp.stack([first, k]).astype(jnp.int32)
            rows, most = call(
                look_kernel,
                [sds((16, SLOTS, COLS)), sds((8, TOK), F32)],
                at,
                ids,
                embed,
                flops=2 * 16 * SLOTS * vocab * COLS,
            )
            rows, held = lax.optimization_barrier((rows, held))
            rows = lax.all_to_all(rows, ("z", "c"), 0, 0, tiled=False)
            if held:
                step = up(held[0]), down(held[1]), swap(held[2], "xl")
                rows, step = lax.optimization_barrier((rows, step))
                held = (*held[:2], *step)
            part = call(
                functools.partial(place_kernel, vocab),
                sds((TOK, COLS)),
                at,
                own,
                rows,
                flops=2 * 16 * SLOTS * TOK * COLS,
            )
            return part, most[0, 0], held

        half = ROWS // 2
        found, most, held = one(jnp.int32(0), (ups[0], downs[0], out_grad))
        ups, downs, og_peer = [held[0], held[2]], [held[1], held[3]], held[4]
        found = lax.while_loop(
            lambda state: (state[0] * SLOTS).astype(F32) < most,
            lambda state: (state[0] + 1, state[1] + one(state[0])[0]),
            (jnp.int32(1), found),
        )
        emb_part = found[1]
        far = [up(ups[1][:half]), down(downs[1][half:])]

    with jax.named_scope("operator"):
        og = jnp.stack([jnp.where(xl == 0, out_grad, og_peer), jnp.where(xl == 0, og_peer, out_grad)])

    with jax.named_scope("first"):
        emb = exchange(call(spread_kernel, block, emb_part))
        emb, far = lax.optimization_barrier((emb, far))
        first_up, first_down = near
        grow = [grow_op, first_down, *downs, jnp.concatenate(far, axis=0), *ups[::-1], first_up]
        emb_other = swap(emb, "c")

    with jax.named_scope("hidden"):
        pair = sds((2, ROWS, TOK), F32)
        part, sent = call(
            hidden_kernel,
            [pair, sds((2, ROWS, TOK))],
            place,
            emb,
            emb_other,
            *grow,
            flops=work,
        )
        longer = sds((8, 2 * TOK + TAIL, COLS))
        hidden, keep, send = call(
            in_kernel,
            [pair, longer, longer],
            place,
            part,
            swap(sent, "xl"),
            gain,
            og,
            *grow,
            flops=2 * work,
        )

    with jax.named_scope("second"):
        got = exchange(call(second_kernel, longer, keep, swap(send, "c")))
        before, inv = call(mid_kernel, [sds((2 * TOK, COLS)), sds((8, TOK), F32)], got)
        turned = turn(before)

    with jax.named_scope("third"):
        keep, send = call(
            proj_kernel, [block, block], place, turned, proj, flops=2 * TOK * COLS * 4096
        )
        got = exchange(
            call(third_kernel, sds((8, 2 * TOK, COLS)), turned, keep, swap(send, "c"))
        )
        out, stat = call(
            out_kernel,
            [sds((2 * TOK, COLS)), sds((TAIL, COLS))],
            place,
            turned,
            got,
            swap(got[:, :TOK], "c"),
            proj,
            flops=2 * TOK * COLS * 4096,
        )

    with jax.named_scope("fourth"):
        late = exchange(call(fourth_kernel, longer, turn(out), stat))
        back_other = swap(late[:, TOK:], "c")
        part, sent = call(
            grad_kernel,
            [pair, sds((2, ROWS + TAIL, TOK))],
            place,
            late,
            back_other,
            *grow,
            flops=work,
        )
        late, sent, inv_late = lax.optimization_barrier((late, sent, inv))
        inv_other = swap(inv_late, "c")
        out_other = swap(late[:, :TOK], "c")
        peer = swap(sent, "xl")
        left = call(
            left_kernel,
            sds((ROWS, 6 * TOK)),
            place,
            part,
            peer,
            hidden,
            inv,
            inv_other,
            sent,
            gain,
            og,
        )
        x = {}
        for steps in ((4, 3, 5), (2, 6, 1, 7, 0)):
            parts = call(
                functools.partial(last_kernel, steps),
                [sds((ROWS // 2, COLS) if d == 4 else (ROWS, COLS)) for d in steps]
                + [sds((ROWS // 2, COLS))] * (4 in steps),
                place,
                left,
                emb,
                emb_other,
                late,
                back_other,
                out_other,
                flops=3 * work * len(steps) // 8,
            )
            x.update(zip(steps, parts))
            if 4 in steps:
                x[8] = parts[-1]

    def add(a, b):
        return (a.astype(F32) + b.astype(F32)).astype(BF16)

    with jax.named_scope("scatter"):
        up_far = lax.ppermute(x[4], "z", [(i, (i + 2) % 8) for i in range(8)])
        down_far = lax.ppermute(x[8], "z", [(i, (i - 2) % 8) for i in range(8)])
        above, below = up(x[3]), down(x[5])
        near = above, below, up_far, down_far
        above, below, up_far, down_far = lax.optimization_barrier(near)
        tile = sds((ROWS, COLS))
        above = up(call(functools.partial(join_kernel, 0), tile, x[2], above, up_far))
        below = down(call(functools.partial(join_kernel, 1), tile, x[6], below, down_far))
        above, below = up(add(above, x[1])), down(add(below, x[7]))
        return call(end_kernel, sds((ROWS, COLS), F32), x[0], above, below)


def solution(mesh):
    fine = Mesh(mesh.devices.reshape(8, 2, 4, 2, 2), ("z", "xl", "y", "xh", "c"))
    in_specs = (P(OP), P(OP, TP), P(None, TP), P(TP, OP), P(TP), P(OP, TP))
    return jax.shard_map(shards, mesh=fine, in_specs=in_specs, out_specs=P(TP, OP), check_vma=False)
```

```python
import functools

import jax
import jax.numpy as jnp
import numpy as np
from jax import lax
from jax.experimental import pallas as pl
from jax.experimental.pallas import tpu as pltpu
from jax.sharding import Mesh, PartitionSpec as P

D2 = 6656
EPS = 1e-05
TOK = 128
ROWS = 416
COLS = 256
TAIL = 16
SLOTS = 48
OP = ("z", "xl")
TP = ("y", "xh", "c")
YX = ("y", "xh")
F32 = jnp.float32
BF16 = jnp.bfloat16
NT = (((1,), (1,)), ((), ()))


def call(kernel, out_shape, *args, flops=0):
    smem = pl.BlockSpec(memory_space=pltpu.SMEM)
    vmem = pl.BlockSpec(memory_space=pltpu.VMEM)
    single = not isinstance(out_shape, (list, tuple))
    outs = [out_shape] if single else list(out_shape)
    nbytes = sum(int(np.prod(a.shape)) * a.dtype.itemsize for a in list(args) + outs)
    return pl.pallas_call(
        kernel,
        out_shape=out_shape,
        in_specs=[smem if a.dtype == jnp.int32 and a.ndim == 1 else vmem for a in args],
        out_specs=vmem if single else [vmem] * len(outs),
        compiler_params=pltpu.CompilerParams(vmem_limit_bytes=20 * 1024 * 1024),
        cost_estimate=pl.CostEstimate(flops=flops, bytes_accessed=nbytes, transcendentals=0),
    )(*args)


def sds(shape, dtype=BF16):
    return jax.ShapeDtypeStruct(shape, dtype)


def dot(a, b):
    return jnp.dot(a, b, preferred_element_type=F32)


def dot_nt(a, b):
    return lax.dot_general(a, b, NT, preferred_element_type=F32)


def swap(x, axis):
    return lax.ppermute(x, axis, [(0, 1), (1, 0)])


def exchange(x):
    return lax.all_to_all(x, YX, 0, 0, tiled=False)


def ranks(inside, base):
    before = lax.broadcasted_iota(jnp.int32, (TOK, TOK), 0)
    after = lax.broadcasted_iota(jnp.int32, (TOK, TOK), 1)
    marks = jnp.where(inside, 1.0, 0.0).astype(BF16)
    rank = dot(marks, jnp.where(before < after, 1.0, 0.0).astype(BF16))
    return jnp.where(inside, rank - base, -1.0)


def look_kernel(at, ids_ref, table_ref, out_ref, most_ref):
    vocab = table_ref.shape[0]
    most = jnp.zeros((16, 1), F32)
    for v in range(16):
        here = (ids_ref[...] >= v * vocab) & (ids_ref[...] < (v + 1) * vocab)
        most = jnp.maximum(most, jnp.sum(jnp.where(here, 1.0, 0.0), axis=1, keepdims=True))
    most_ref[...] = jnp.broadcast_to(jnp.max(most, axis=0, keepdims=True), (8, TOK))
    ids = ids_ref[...] - at[0]
    key = ranks((ids >= 0) & (ids < vocab), (at[1] * SLOTS).astype(F32))
    ids = ids.astype(F32) + 1.0
    slot = lax.broadcasted_iota(jnp.int32, (SLOTS, TOK), 0).astype(F32)
    lanes = lax.broadcasted_iota(jnp.int32, (4 * SLOTS, vocab), 1).astype(F32)
    table = table_ref[...]
    for g in range(4):
        rows = []
        for o in range(4 * g, 4 * g + 4):
            hit = jnp.where(slot == key[o : o + 1], ids[o : o + 1], 0.0)
            rows.append(jnp.sum(hit, axis=1, keepdims=True) - 1.0)
        hot = jnp.where(lanes == jnp.concatenate(rows, axis=0), 1.0, 0.0).astype(BF16)
        found = dot(hot, table).astype(BF16)
        for o in range(4):
            out_ref[4 * g + o] = found[o * SLOTS : (o + 1) * SLOTS]


def place_kernel(vocab, at, ids_ref, rows_ref, out_ref):
    ids = jnp.broadcast_to(ids_ref[...], (16, TOK))
    first = lax.broadcasted_iota(jnp.int32, (16, TOK), 0) * vocab
    key = ranks((ids >= first) & (ids < first + vocab), (at[1] * SLOTS).astype(F32))
    slot = lax.broadcasted_iota(jnp.int32, (SLOTS, TOK), 0).astype(F32)
    hits = [jnp.where(slot == key[v : v + 1], 1.0, 0.0) for v in range(16)]
    hits = jnp.concatenate(hits, axis=0).T.astype(BF16)
    rows = jnp.concatenate([rows_ref[v] for v in range(16)], axis=0)
    out_ref[...] = dot(hits, rows).astype(BF16)


def split_row(row):
    hi = row.astype(BF16)
    lo = (row - hi.astype(F32)).astype(BF16)
    return jnp.broadcast_to(jnp.concatenate([hi, lo], axis=1), (TAIL, COLS))


def join_row(tail):
    both = tail.astype(F32)[0:1]
    return both[:, :TOK] + both[:, TOK:]


def blocks(place, grow):
    for d in range(8):
        yield lax.rem(place[1] + d, 8), grow[d]


def spread_kernel(rows, out):
    for b in range(8):
        out[b] = rows[...]


def hidden_kernel(place, got, other, *refs):
    grow, (part, sent) = refs[:8], refs[8:]
    c = place[0]
    total = jnp.zeros((ROWS, 2 * TOK), F32)
    for b, cols in blocks(place, grow):
        total += dot_nt(cols[...], jnp.concatenate([got[b], other[b]], axis=0))
    for t, rows in ((c, total[:, :TOK]), (1 - c, total[:, TOK:])):
        part[t] = rows
        sent[t] = rows.astype(BF16)


def in_kernel(place, part, peer, gain, og, *refs):
    grow, (hidden_ref, keep, send) = refs[:8], refs[8:]
    c = place[0]
    left = []
    for t, to in ((c, keep), (1 - c, send)):
        hidden = part[t] + peer[t].astype(F32)
        hidden_ref[t] = hidden
        left += [(hidden * gain[...].astype(F32)).T.astype(BF16), og[t]]
        tail = split_row(jnp.sum(hidden * hidden, axis=0, keepdims=True))
        for b in range(8):
            to[b, 2 * TOK :] = tail
    left = jnp.concatenate(left, axis=0)
    for b, cols in blocks(place, grow):
        both = dot(left, cols[...]).astype(BF16)
        keep[b, : 2 * TOK] = both[: 2 * TOK]
        send[b, : 2 * TOK] = both[2 * TOK :]


def second_kernel(keep, recv, out):
    tail = split_row(join_row(keep[0, 2 * TOK :]) + join_row(recv[0, 2 * TOK :]))
    for b in range(8):
        mine = keep[b, : 2 * TOK].astype(F32)
        out[b, : 2 * TOK] = (mine + recv[b, : 2 * TOK].astype(F32)).astype(BF16)
        out[b, 2 * TOK :] = tail


def mid_kernel(got, out, inv_ref):
    both = got[0, : 2 * TOK].astype(F32)
    row = join_row(got[0, 2 * TOK :])
    for b in range(1, 8):
        both += got[b, : 2 * TOK].astype(F32)
        row += join_row(got[b, 2 * TOK :])
    inv = lax.rsqrt(jnp.broadcast_to(row, (TOK, TOK)) / D2 + EPS)
    inv_ref[...] = inv[0:8]
    out[:TOK] = (both[:TOK] * inv.T[:, 0:1]).astype(BF16)
    out[TOK:] = both[TOK:].astype(BF16)


def proj_kernel(place, turned, proj, keep, send):
    c = place[0]
    back = turned[TOK:]
    for b in range(8):
        keep[b] = dot_nt(back, proj[2 * b + c]).astype(BF16)
        send[b] = dot_nt(back, proj[2 * b + 1 - c]).astype(BF16)


def third_kernel(turned, keep, recv, out):
    for b in range(8):
        out[b, :TOK] = turned[:TOK]
        out[b, TOK:] = (keep[b].astype(F32) + recv[b].astype(F32)).astype(BF16)


def out_kernel(place, turned, got, other, proj, out, stat_ref):
    c = place[0]
    total = jnp.zeros((TOK, COLS), F32)
    back = jnp.zeros((TOK, COLS), F32)
    for b in range(8):
        total += dot(got[b, :TOK], proj[2 * b + c])
        total += dot(other[b], proj[2 * b + 1 - c])
        back += got[b, TOK:].astype(F32)
    back = back.astype(BF16)
    out[:TOK] = total.astype(BF16)
    out[TOK:] = back
    stat = jnp.sum(back.astype(F32) * turned[:TOK].astype(F32), axis=1, keepdims=True)
    stat_ref[...] = split_row(jnp.broadcast_to(stat, (TOK, TOK)).T[0:1])


def fourth_kernel(turned, stat, out):
    for b in range(8):
        out[b, : 2 * TOK] = turned[...]
        out[b, 2 * TOK :] = stat[...]


def grad_kernel(place, got, other, *refs):
    grow, (part, sent) = refs[:8], refs[8:]
    c = place[0]
    total = jnp.zeros((ROWS, 2 * TOK), F32)
    for b, cols in blocks(place, grow):
        pair = jnp.concatenate([got[b, TOK : 2 * TOK], other[b, :TOK]], axis=0)
        total += dot_nt(cols[...], pair)
    stat = jnp.zeros((1, TOK), F32)
    for b in range(8):
        stat += join_row(got[b, 2 * TOK :]) + join_row(other[b, TOK:])
    both = split_row(stat)
    tail = jnp.concatenate([both[:8, :TOK].astype(F32), both[:8, TOK:].astype(F32)], axis=0)
    for t, rows in ((c, total[:, :TOK]), (1 - c, total[:, TOK:])):
        part[t] = rows
        sent[t, :ROWS] = rows.astype(BF16)
        sent[t, ROWS:] = tail.astype(BF16)


def left_kernel(place, part, peer, hidden_ref, inv_c, inv_o, sent, gain_ref, og_ref, out):
    c = place[0]
    xl = place[2]
    gain = gain_ref[...].astype(F32)
    hidden_grads, normeds, ogs = [], [], []
    for t, inv_ref in ((c, inv_c), (1 - c, inv_o)):
        inv = inv_ref[0:1]
        tail = jnp.where(t == xl, sent[0, ROWS:].astype(F32), peer[0, ROWS:].astype(F32))
        mean = (tail[0:1] + tail[8:9]) / inv / D2
        hidden = hidden_ref[t]
        og = og_ref[t].astype(F32).T
        scaled = (part[t] + peer[t, :ROWS].astype(F32)) * gain
        hidden_grads.append(og + inv * scaled - hidden * inv * inv * inv * mean)
        normeds.append(hidden * inv * gain)
        ogs.append(og)
    out[...] = jnp.concatenate(hidden_grads + normeds + ogs, axis=1).astype(BF16)


def last_kernel(steps, place, left_ref, emb_m, emb_o, late, back_o, out_o, *outs):
    z = place[1]
    left = left_ref[...]
    half = ROWS // 2
    for at, d in enumerate(steps):
        b = lax.rem(z + d, 8)
        right = jnp.concatenate(
            [
                emb_m[b],
                emb_o[b],
                late[b, TOK : 2 * TOK],
                back_o[b, :TOK],
                late[b, :TOK],
                out_o[b],
            ],
            axis=0,
        )
        total = dot(left, right).astype(BF16)
        if d == 4:
            outs[at][...] = total[:half]
            outs[-1][...] = total[half:]
        else:
            outs[at][...] = total


def end_kernel(mine, above, below, out):
    out[...] = mine[...].astype(F32) + above[...].astype(F32) + below[...].astype(F32)


def join_kernel(half, mine, near, far, out):
    start = half * (ROWS // 2)
    out[...] = (mine[...].astype(F32) + near[...].astype(F32)).astype(BF16)
    rows = pl.ds(start, ROWS // 2)
    total = mine[rows].astype(F32) + near[rows].astype(F32) + far[...].astype(F32)
    out[rows] = total.astype(BF16)


def turn(x):
    return lax.ppermute(x, ("xl", "c"), [(0, 0), (1, 2), (2, 1), (3, 3)])


def up(v):
    return lax.ppermute(v, "z", [(i, (i + 1) % 8) for i in range(8)])


def down(v):
    return lax.ppermute(v, "z", [(i, (i - 1) % 8) for i in range(8)])


def shards(token_ids, embed, proj, grow_op, norm_gain, out_grad):
    c = lax.axis_index("c")
    z = lax.axis_index("z")
    xl = lax.axis_index("xl")
    place = jnp.stack([c, z, xl]).astype(jnp.int32)
    gain = norm_gain.reshape(ROWS, 1)
    proj = proj.reshape(16, COLS, COLS)
    block = sds((8, TOK, COLS))
    work = 2 * TOK * ROWS * 4096

    with jax.named_scope("embedding"):
        ids = lax.all_to_all(
            jnp.broadcast_to(token_ids.reshape(1, 1, TOK), (16, 1, TOK)), OP, 0, 0, tiled=False
        )
        near = up(grow_op), down(grow_op)
        ids, near = lax.optimization_barrier((ids, near))
        ids = ids.reshape(16, TOK)
        vocab = embed.shape[0]
        first = (z * 2 + xl) * vocab
        own = token_ids.reshape(1, TOK)

        def one(k, held=None):
            at = jnp.stack([first, k]).astype(jnp.int32)
            rows, most = call(
                look_kernel,
                [sds((16, SLOTS, COLS)), sds((8, TOK), F32)],
                at,
                ids,
                embed,
                flops=2 * 16 * SLOTS * vocab * COLS,
            )
            if held:
                second = up(held[0])
                rows, first_down, og, second = lax.optimization_barrier((rows, *held[1:], second))
                held = second, down(first_down)
            rows = lax.all_to_all(rows, OP, 0, 0, tiled=False)
            if held:
                step = up(held[0]), down(held[1]), swap(og, "xl")
                rows, step = lax.optimization_barrier((rows, step))
                held = (*held, *step)
            part = call(
                functools.partial(place_kernel, vocab),
                sds((TOK, COLS)),
                at,
                own,
                rows,
                flops=2 * 16 * SLOTS * TOK * COLS,
            )
            return part, most[0, 0], held

        half = ROWS // 2
        found, most, held = one(jnp.int32(0), (*near, out_grad))
        ups, downs, og_peer = [held[0], held[2]], [held[1], held[3]], held[4]
        found = lax.while_loop(
            lambda state: (state[0] * SLOTS).astype(F32) < most,
            lambda state: (state[0] + 1, state[1] + one(state[0])[0]),
            (jnp.int32(1), found),
        )
        emb_part = turn(found[1])
        far = [up(ups[1][:half]), down(downs[1][half:])]

    with jax.named_scope("operator"):
        og = jnp.stack([jnp.where(xl == 0, out_grad, og_peer), jnp.where(xl == 0, og_peer, out_grad)])

    with jax.named_scope("first"):
        emb = exchange(call(spread_kernel, block, emb_part))
        emb, far = lax.optimization_barrier((emb, far))
        first_up, first_down = near
        grow = [grow_op, first_down, *downs, jnp.concatenate(far, axis=0), *ups[::-1], first_up]
        emb_other = swap(emb, "c")

    with jax.named_scope("hidden"):
        pair = sds((2, ROWS, TOK), F32)
        part, sent = call(
            hidden_kernel,
            [pair, sds((2, ROWS, TOK))],
            place,
            emb,
            emb_other,
            *grow,
            flops=work,
        )
        longer = sds((8, 2 * TOK + TAIL, COLS))
        hidden, keep, send = call(
            in_kernel,
            [pair, longer, longer],
            place,
            part,
            swap(sent, "xl"),
            gain,
            og,
            *grow,
            flops=2 * work,
        )

    with jax.named_scope("second"):
        got = exchange(call(second_kernel, longer, keep, swap(send, "c")))
        before, inv = call(mid_kernel, [sds((2 * TOK, COLS)), sds((8, TOK), F32)], got)
        turned = turn(before)

    with jax.named_scope("third"):
        keep, send = call(
            proj_kernel, [block, block], place, turned, proj, flops=2 * TOK * COLS * 4096
        )
        got = exchange(
            call(third_kernel, sds((8, 2 * TOK, COLS)), turned, keep, swap(send, "c"))
        )
        out, stat = call(
            out_kernel,
            [sds((2 * TOK, COLS)), sds((TAIL, COLS))],
            place,
            turned,
            got,
            swap(got[:, :TOK], "c"),
            proj,
            flops=2 * TOK * COLS * 4096,
        )

    with jax.named_scope("fourth"):
        late = exchange(call(fourth_kernel, longer, turn(out), stat))
        back_other = swap(late[:, TOK:], "c")
        part, sent = call(
            grad_kernel,
            [pair, sds((2, ROWS + TAIL, TOK))],
            place,
            late,
            back_other,
            *grow,
            flops=work,
        )
        late, sent, inv_late = lax.optimization_barrier((late, sent, inv))
        inv_other = swap(inv_late, "c")
        out_other = swap(late[:, :TOK], "c")
        peer = swap(sent, "xl")
        left = call(
            left_kernel,
            sds((ROWS, 6 * TOK)),
            place,
            part,
            peer,
            hidden,
            inv,
            inv_other,
            sent,
            gain,
            og,
        )
        x = {}
        for steps in ((4, 3, 5), (2, 6, 1, 7, 0)):
            parts = call(
                functools.partial(last_kernel, steps),
                [sds((ROWS // 2, COLS) if d == 4 else (ROWS, COLS)) for d in steps]
                + [sds((ROWS // 2, COLS))] * (4 in steps),
                place,
                left,
                emb,
                emb_other,
                late,
                back_other,
                out_other,
                flops=3 * work * len(steps) // 8,
            )
            x.update(zip(steps, parts))
            if 4 in steps:
                x[8] = parts[-1]

    def add(a, b):
        return (a.astype(F32) + b.astype(F32)).astype(BF16)

    with jax.named_scope("scatter"):
        up_far = lax.ppermute(x[4], "z", [(i, (i + 2) % 8) for i in range(8)])
        down_far = lax.ppermute(x[8], "z", [(i, (i - 2) % 8) for i in range(8)])
        above, below = up(x[3]), down(x[5])
        near = above, below, up_far, down_far
        above, below, up_far, down_far = lax.optimization_barrier(near)
        tile = sds((ROWS, COLS))
        above = up(call(functools.partial(join_kernel, 0), tile, x[2], above, up_far))
        below = down(call(functools.partial(join_kernel, 1), tile, x[6], below, down_far))
        above, below = up(add(above, x[1])), down(add(below, x[7]))
        return call(end_kernel, sds((ROWS, COLS), F32), x[0], above, below)


def solution(mesh):
    fine = Mesh(mesh.devices.reshape(8, 2, 4, 2, 2), ("z", "xl", "y", "xh", "c"))
    in_specs = (P(OP), P(OP, TP), P(None, TP), P(TP, OP), P(TP), P(OP, TP))
    return jax.shard_map(shards, mesh=fine, in_specs=in_specs, out_specs=P(TP, OP), check_vma=False)
```

```python
import functools

import jax
import jax.numpy as jnp
import numpy as np
from jax import lax
from jax.experimental import pallas as pl
from jax.experimental.pallas import tpu as pltpu
from jax.sharding import Mesh, PartitionSpec as P

D2 = 6656
EPS = 1e-05
TOK = 128
ROWS = 416
COLS = 256
TAIL = 16
SLOTS = 48
OP = ("z", "xl")
TP = ("y", "xh", "c")
YX = ("y", "xh")
F32 = jnp.float32
BF16 = jnp.bfloat16
NT = (((1,), (1,)), ((), ()))
EARLY = (4, 3, 5)
LATER = (2, 6, 1, 7, 0)


def call(kernel, out_shape, *args, flops=0):
    smem = pl.BlockSpec(memory_space=pltpu.SMEM)
    vmem = pl.BlockSpec(memory_space=pltpu.VMEM)
    single = not isinstance(out_shape, (list, tuple))
    outs = [out_shape] if single else list(out_shape)
    nbytes = sum(int(np.prod(a.shape)) * a.dtype.itemsize for a in list(args) + outs)
    return pl.pallas_call(
        kernel,
        out_shape=out_shape,
        in_specs=[smem if a.dtype == jnp.int32 and a.ndim == 1 else vmem for a in args],
        out_specs=vmem if single else [vmem] * len(outs),
        compiler_params=pltpu.CompilerParams(vmem_limit_bytes=20 * 1024 * 1024),
        cost_estimate=pl.CostEstimate(flops=flops, bytes_accessed=nbytes, transcendentals=0),
    )(*args)


def sds(shape, dtype=BF16):
    return jax.ShapeDtypeStruct(shape, dtype)


def dot(a, b):
    return jnp.dot(a, b, preferred_element_type=F32)


def dot_nt(a, b):
    return lax.dot_general(a, b, NT, preferred_element_type=F32)


def swap(x, axis):
    return lax.ppermute(x, axis, [(0, 1), (1, 0)])


def exchange(x):
    return lax.all_to_all(x, YX, 0, 0, tiled=False)


def ranks(inside, base):
    before = lax.broadcasted_iota(jnp.int32, (TOK, TOK), 0)
    after = lax.broadcasted_iota(jnp.int32, (TOK, TOK), 1)
    marks = jnp.where(inside, 1.0, 0.0).astype(BF16)
    rank = dot(marks, jnp.where(before < after, 1.0, 0.0).astype(BF16))
    return jnp.where(inside, rank - base, -1.0)


def look_kernel(at, ids_ref, table_ref, out_ref, most_ref):
    vocab = table_ref.shape[0]
    most = jnp.zeros((16, 1), F32)
    for v in range(16):
        here = (ids_ref[...] >= v * vocab) & (ids_ref[...] < (v + 1) * vocab)
        most = jnp.maximum(most, jnp.sum(jnp.where(here, 1.0, 0.0), axis=1, keepdims=True))
    most_ref[...] = jnp.broadcast_to(jnp.max(most, axis=0, keepdims=True), (8, TOK))
    ids = ids_ref[...] - at[0]
    key = ranks((ids >= 0) & (ids < vocab), (at[1] * SLOTS).astype(F32))
    ids = ids.astype(F32) + 1.0
    slot = lax.broadcasted_iota(jnp.int32, (SLOTS, TOK), 0).astype(F32)
    lanes = lax.broadcasted_iota(jnp.int32, (4 * SLOTS, vocab), 1).astype(F32)
    table = table_ref[...]
    for g in range(4):
        rows = []
        for o in range(4 * g, 4 * g + 4):
            hit = jnp.where(slot == key[o : o + 1], ids[o : o + 1], 0.0)
            rows.append(jnp.sum(hit, axis=1, keepdims=True) - 1.0)
        hot = jnp.where(lanes == jnp.concatenate(rows, axis=0), 1.0, 0.0).astype(BF16)
        found = dot(hot, table).astype(BF16)
        for o in range(4):
            out_ref[4 * g + o] = found[o * SLOTS : (o + 1) * SLOTS]


def place_kernel(vocab, at, ids_ref, rows_ref, out_ref):
    ids = jnp.broadcast_to(ids_ref[...], (16, TOK))
    first = lax.broadcasted_iota(jnp.int32, (16, TOK), 0) * vocab
    key = ranks((ids >= first) & (ids < first + vocab), (at[1] * SLOTS).astype(F32))
    slot = lax.broadcasted_iota(jnp.int32, (SLOTS, TOK), 0).astype(F32)
    hits = [jnp.where(slot == key[v : v + 1], 1.0, 0.0) for v in range(16)]
    hits = jnp.concatenate(hits, axis=0).T.astype(BF16)
    rows = jnp.concatenate([rows_ref[v] for v in range(16)], axis=0)
    out_ref[...] = dot(hits, rows).astype(BF16)


def split_row(row):
    hi = row.astype(BF16)
    lo = (row - hi.astype(F32)).astype(BF16)
    return jnp.broadcast_to(jnp.concatenate([hi, lo], axis=1), (TAIL, COLS))


def join_row(tail):
    both = tail.astype(F32)[0:1]
    return both[:, :TOK] + both[:, TOK:]


def blocks(place, grow):
    for d in range(8):
        yield lax.rem(place[1] + d, 8), grow[d]


def spread_kernel(rows, out):
    for b in range(8):
        out[b] = rows[...]


def hidden_kernel(place, got, other, *refs):
    grow, (part, sent) = refs[:8], refs[8:]
    c = place[0]
    total = jnp.zeros((ROWS, 2 * TOK), F32)
    for b, cols in blocks(place, grow):
        total += dot_nt(cols[...], jnp.concatenate([got[b], other[b]], axis=0))
    for t, rows in ((c, total[:, :TOK]), (1 - c, total[:, TOK:])):
        part[t] = rows
        sent[t] = rows.astype(BF16)


def in_kernel(place, part, peer, gain, og, *refs):
    grow, (hidden_ref, keep, send) = refs[:8], refs[8:]
    c = place[0]
    left = []
    for t, to in ((c, keep), (1 - c, send)):
        hidden = part[t] + peer[t].astype(F32)
        hidden_ref[t] = hidden
        left += [(hidden * gain[...].astype(F32)).T.astype(BF16), og[t]]
        tail = split_row(jnp.sum(hidden * hidden, axis=0, keepdims=True))
        for b in range(8):
            to[b, 2 * TOK :] = tail
    left = jnp.concatenate(left, axis=0)
    for b, cols in blocks(place, grow):
        both = dot(left, cols[...]).astype(BF16)
        keep[b, : 2 * TOK] = both[: 2 * TOK]
        send[b, : 2 * TOK] = both[2 * TOK :]


def second_kernel(keep, recv, out):
    tail = split_row(join_row(keep[0, 2 * TOK :]) + join_row(recv[0, 2 * TOK :]))
    for b in range(8):
        mine = keep[b, : 2 * TOK].astype(F32)
        out[b, : 2 * TOK] = (mine + recv[b, : 2 * TOK].astype(F32)).astype(BF16)
        out[b, 2 * TOK :] = tail


def mid_kernel(got, out, inv_ref):
    both = got[0, : 2 * TOK].astype(F32)
    row = join_row(got[0, 2 * TOK :])
    for b in range(1, 8):
        both += got[b, : 2 * TOK].astype(F32)
        row += join_row(got[b, 2 * TOK :])
    inv = lax.rsqrt(jnp.broadcast_to(row, (TOK, TOK)) / D2 + EPS)
    inv_ref[...] = inv[0:8]
    out[:TOK] = (both[:TOK] * inv.T[:, 0:1]).astype(BF16)
    out[TOK:] = both[TOK:].astype(BF16)


def proj_kernel(place, turned, proj, keep, send):
    c = place[0]
    back = turned[TOK:]
    for b in range(8):
        keep[b] = dot_nt(back, proj[2 * b + c]).astype(BF16)
        send[b] = dot_nt(back, proj[2 * b + 1 - c]).astype(BF16)


def third_kernel(turned, keep, recv, out):
    for b in range(8):
        out[b, :TOK] = turned[:TOK]
        out[b, TOK:] = (keep[b].astype(F32) + recv[b].astype(F32)).astype(BF16)


def out_kernel(place, turned, got, other, proj, out, stat_ref):
    c = place[0]
    total = jnp.zeros((TOK, COLS), F32)
    back = jnp.zeros((TOK, COLS), F32)
    for b in range(8):
        total += dot(got[b, :TOK], proj[2 * b + c])
        total += dot(other[b], proj[2 * b + 1 - c])
        back += got[b, TOK:].astype(F32)
    back = back.astype(BF16)
    out[:TOK] = total.astype(BF16)
    out[TOK:] = back
    stat = jnp.sum(back.astype(F32) * turned[:TOK].astype(F32), axis=1, keepdims=True)
    stat_ref[...] = split_row(jnp.broadcast_to(stat, (TOK, TOK)).T[0:1])


def fourth_kernel(turned, stat, out):
    for b in range(8):
        out[b, : 2 * TOK] = turned[...]
        out[b, 2 * TOK :] = stat[...]


def grad_kernel(place, got, other, *refs):
    grow, (part, sent) = refs[:8], refs[8:]
    c = place[0]
    total = jnp.zeros((ROWS, 2 * TOK), F32)
    for b, cols in blocks(place, grow):
        pair = jnp.concatenate([got[b, TOK : 2 * TOK], other[b, :TOK]], axis=0)
        total += dot_nt(cols[...], pair)
    stat = jnp.zeros((1, TOK), F32)
    for b in range(8):
        stat += join_row(got[b, 2 * TOK :]) + join_row(other[b, TOK:])
    both = split_row(stat)
    tail = jnp.concatenate([both[:8, :TOK].astype(F32), both[:8, TOK:].astype(F32)], axis=0)
    for t, rows in ((c, total[:, :TOK]), (1 - c, total[:, TOK:])):
        part[t] = rows
        sent[t, :ROWS] = rows.astype(BF16)
        sent[t, ROWS:] = tail.astype(BF16)


def left_kernel(place, hidden_ref, inv_c, inv_o, gain_ref, og_ref, out):
    c = place[0]
    gain = gain_ref[...].astype(F32)
    normeds, ogs = [], []
    for t, inv_ref in ((c, inv_c), (1 - c, inv_o)):
        normeds.append(hidden_ref[t] * inv_ref[0:1] * gain)
        ogs.append(og_ref[t].astype(F32).T)
    out[...] = jnp.concatenate(normeds + ogs, axis=1).astype(BF16)


def right_rows(b, late, back_o, out_o):
    return [late[b, TOK : 2 * TOK], back_o[b, :TOK], late[b, :TOK], out_o[b]]


def early_kernel(place, left_ref, late, back_o, out_o, *outs):
    left = left_ref[...]
    for d, out in zip(EARLY, outs):
        b = lax.rem(place[1] + d, 8)
        out[...] = dot(left, jnp.concatenate(right_rows(b, late, back_o, out_o), axis=0))


def first_kernel(
    place, part, peer, hidden_ref, inv_c, inv_o, sent, gain_ref, og_ref, emb_m, emb_o, *refs
):
    sums, (left_ref, x4, x3, x5, x8) = refs[:3], refs[3:]
    c = place[0]
    xl = place[2]
    gain = gain_ref[...].astype(F32)
    grads = []
    for t, inv_ref in ((c, inv_c), (1 - c, inv_o)):
        inv = inv_ref[0:1]
        tail = jnp.where(t == xl, sent[0, ROWS:].astype(F32), peer[0, ROWS:].astype(F32))
        mean = (tail[0:1] + tail[8:9]) / inv / D2
        hidden = hidden_ref[t]
        scaled = (part[t] + peer[t, :ROWS].astype(F32)) * gain
        og = og_ref[t].astype(F32).T
        grads.append(og + inv * scaled - hidden * inv * inv * inv * mean)
    left = jnp.concatenate(grads, axis=1).astype(BF16)
    left_ref[...] = left
    half = ROWS // 2
    totals = []
    for d, early in zip(EARLY, sums):
        b = lax.rem(place[1] + d, 8)
        right = jnp.concatenate([emb_m[b], emb_o[b]], axis=0)
        totals.append((dot(left, right) + early[...]).astype(BF16))
    x4[...] = totals[0][:half]
    x8[...] = totals[0][half:]
    x3[...] = totals[1]
    x5[...] = totals[2]


def last_kernel(place, left_ref, more_ref, emb_m, emb_o, late, back_o, out_o, *outs):
    left = jnp.concatenate([left_ref[...], more_ref[...]], axis=1)
    for d, out in zip(LATER, outs):
        b = lax.rem(place[1] + d, 8)
        right = [emb_m[b], emb_o[b], *right_rows(b, late, back_o, out_o)]
        out[...] = dot(left, jnp.concatenate(right, axis=0)).astype(BF16)


def end_kernel(mine, above, below, out):
    out[...] = mine[...].astype(F32) + above[...].astype(F32) + below[...].astype(F32)


def join_kernel(half, mine, near, far, out):
    start = half * (ROWS // 2)
    out[...] = (mine[...].astype(F32) + near[...].astype(F32)).astype(BF16)
    rows = pl.ds(start, ROWS // 2)
    total = mine[rows].astype(F32) + near[rows].astype(F32) + far[...].astype(F32)
    out[rows] = total.astype(BF16)


def turn(x):
    return lax.ppermute(x, ("xl", "c"), [(0, 0), (1, 2), (2, 1), (3, 3)])


def up(v):
    return lax.ppermute(v, "z", [(i, (i + 1) % 8) for i in range(8)])


def down(v):
    return lax.ppermute(v, "z", [(i, (i - 1) % 8) for i in range(8)])


def shards(token_ids, embed, proj, grow_op, norm_gain, out_grad):
    c = lax.axis_index("c")
    z = lax.axis_index("z")
    xl = lax.axis_index("xl")
    place = jnp.stack([c, z, xl]).astype(jnp.int32)
    gain = norm_gain.reshape(ROWS, 1)
    proj = proj.reshape(16, COLS, COLS)
    block = sds((8, TOK, COLS))
    work = 2 * TOK * ROWS * 4096

    with jax.named_scope("embedding"):
        ids = lax.all_to_all(
            jnp.broadcast_to(token_ids.reshape(1, 1, TOK), (16, 1, TOK)), OP, 0, 0, tiled=False
        )
        near = up(grow_op), down(grow_op)
        ids, near = lax.optimization_barrier((ids, near))
        ups, downs = [up(near[0])], [down(near[1])]
        ids = ids.reshape(16, TOK)
        vocab = embed.shape[0]
        first = (z * 2 + xl) * vocab
        own = token_ids.reshape(1, TOK)

        def one(k, held=None):
            at = jnp.stack([first, k]).astype(jnp.int32)
            rows, most = call(
                look_kernel,
                [sds((16, SLOTS, COLS)), sds((8, TOK), F32)],
                at,
                ids,
                embed,
                flops=2 * 16 * SLOTS * vocab * COLS,
            )
            rows, held = lax.optimization_barrier((rows, held))
            rows = lax.all_to_all(rows, OP, 0, 0, tiled=False)
            if held:
                step = up(held[0]), down(held[1]), swap(held[2], "xl")
                rows, step = lax.optimization_barrier((rows, step))
                held = (*held[:2], *step)
            part = call(
                functools.partial(place_kernel, vocab),
                sds((TOK, COLS)),
                at,
                own,
                rows,
                flops=2 * 16 * SLOTS * TOK * COLS,
            )
            return part, most[0, 0], held

        half = ROWS // 2
        found, most, held = one(jnp.int32(0), (ups[0], downs[0], out_grad))
        ups, downs, og_peer = [held[0], held[2]], [held[1], held[3]], held[4]
        found = lax.while_loop(
            lambda state: (state[0] * SLOTS).astype(F32) < most,
            lambda state: (state[0] + 1, state[1] + one(state[0])[0]),
            (jnp.int32(1), found),
        )
        emb_part = turn(found[1])
        far = [up(ups[1][:half]), down(downs[1][half:])]

    with jax.named_scope("operator"):
        og = jnp.stack([jnp.where(xl == 0, out_grad, og_peer), jnp.where(xl == 0, og_peer, out_grad)])

    with jax.named_scope("first"):
        emb = exchange(call(spread_kernel, block, emb_part))
        emb, far = lax.optimization_barrier((emb, far))
        first_up, first_down = near
        grow = [grow_op, first_down, *downs, jnp.concatenate(far, axis=0), *ups[::-1], first_up]
        emb_other = swap(emb, "c")

    with jax.named_scope("hidden"):
        pair = sds((2, ROWS, TOK), F32)
        part, sent = call(
            hidden_kernel,
            [pair, sds((2, ROWS, TOK))],
            place,
            emb,
            emb_other,
            *grow,
            flops=work,
        )
        longer = sds((8, 2 * TOK + TAIL, COLS))
        hidden, keep, send = call(
            in_kernel,
            [pair, longer, longer],
            place,
            part,
            swap(sent, "xl"),
            gain,
            og,
            *grow,
            flops=2 * work,
        )

    with jax.named_scope("second"):
        got = exchange(call(second_kernel, longer, keep, swap(send, "c")))
        before, inv = call(mid_kernel, [sds((2 * TOK, COLS)), sds((8, TOK), F32)], got)
        turned, inv_other = lax.optimization_barrier((turn(before), swap(inv, "c")))

    with jax.named_scope("third"):
        keep, send = call(
            proj_kernel, [block, block], place, turned, proj, flops=2 * TOK * COLS * 4096
        )
        got = exchange(
            call(third_kernel, sds((8, 2 * TOK, COLS)), turned, keep, swap(send, "c"))
        )
        out, stat = call(
            out_kernel,
            [sds((2 * TOK, COLS)), sds((TAIL, COLS))],
            place,
            turned,
            got,
            swap(got[:, :TOK], "c"),
            proj,
            flops=2 * TOK * COLS * 4096,
        )

    with jax.named_scope("fourth"):
        late = exchange(call(fourth_kernel, longer, turn(out), stat))
        back_other = swap(late[:, TOK:], "c")
        part, sent = call(
            grad_kernel,
            [pair, sds((2, ROWS + TAIL, TOK))],
            place,
            late,
            back_other,
            *grow,
            flops=work,
        )
        late, sent = lax.optimization_barrier((late, sent))
        out_other = swap(late[:, :TOK], "c")
        peer = swap(sent, "xl")
        right = late, back_other, out_other
        more = call(left_kernel, sds((ROWS, 4 * TOK)), place, hidden, inv, inv_other, gain, og)
        tile = sds((ROWS, COLS))
        early = call(
            early_kernel, [sds((ROWS, COLS), F32)] * 3, place, more, *right, flops=3 * work // 4
        )
        peer, early = lax.optimization_barrier((peer, early))
        half_tile = sds((ROWS // 2, COLS))
        left, *first = call(
            first_kernel,
            [sds((ROWS, 2 * TOK)), half_tile, tile, tile, half_tile],
            place,
            part,
            peer,
            hidden,
            inv,
            inv_other,
            sent,
            gain,
            og,
            emb,
            emb_other,
            *early,
            flops=3 * work // 8,
        )
        x = dict(zip((*EARLY, 8), first))
        later = call(
            last_kernel,
            [tile] * 5,
            place,
            left,
            more,
            emb,
            emb_other,
            *right,
            flops=15 * work // 8,
        )
        x.update(zip(LATER, later))

    def add(a, b):
        return (a.astype(F32) + b.astype(F32)).astype(BF16)

    with jax.named_scope("scatter"):
        up_far = lax.ppermute(x[4], "z", [(i, (i + 2) % 8) for i in range(8)])
        down_far = lax.ppermute(x[8], "z", [(i, (i - 2) % 8) for i in range(8)])
        above, below = up(x[3]), down(x[5])
        near = above, below, up_far, down_far
        above, below, up_far, down_far = lax.optimization_barrier(near)
        above = up(call(functools.partial(join_kernel, 0), tile, x[2], above, up_far))
        below = down(call(functools.partial(join_kernel, 1), tile, x[6], below, down_far))
        above, below = up(add(above, x[1])), down(add(below, x[7]))
        return call(end_kernel, sds((ROWS, COLS), F32), x[0], above, below)


def solution(mesh):
    fine = Mesh(mesh.devices.reshape(8, 2, 4, 2, 2), ("z", "xl", "y", "xh", "c"))
    in_specs = (P(OP), P(OP, TP), P(None, TP), P(TP, OP), P(TP), P(OP, TP))
    return jax.shard_map(shards, mesh=fine, in_specs=in_specs, out_specs=P(TP, OP), check_vma=False)
```

```python
import functools

import jax
import jax.numpy as jnp
import numpy as np
from jax import lax
from jax.experimental import pallas as pl
from jax.experimental.pallas import tpu as pltpu
from jax.sharding import Mesh, PartitionSpec as P

D2 = 6656
EPS = 1e-05
TOK = 128
ROWS = 416
COLS = 256
TAIL = 16
SLOTS = 48
OP = ("z", "xl")
TP = ("y", "xh", "c")
YX = ("y", "xh")
F32 = jnp.float32
BF16 = jnp.bfloat16
NT = (((1,), (1,)), ((), ()))
EARLY = (4, 3, 5)
LATER = (2, 6, 1, 7, 0)


def call(kernel, out_shape, *args, flops=0):
    smem = pl.BlockSpec(memory_space=pltpu.SMEM)
    vmem = pl.BlockSpec(memory_space=pltpu.VMEM)
    single = not isinstance(out_shape, (list, tuple))
    outs = [out_shape] if single else list(out_shape)
    nbytes = sum(int(np.prod(a.shape)) * a.dtype.itemsize for a in list(args) + outs)
    return pl.pallas_call(
        kernel,
        out_shape=out_shape,
        in_specs=[smem if a.dtype == jnp.int32 and a.ndim == 1 else vmem for a in args],
        out_specs=vmem if single else [vmem] * len(outs),
        compiler_params=pltpu.CompilerParams(vmem_limit_bytes=20 * 1024 * 1024),
        cost_estimate=pl.CostEstimate(flops=flops, bytes_accessed=nbytes, transcendentals=0),
    )(*args)


def sds(shape, dtype=BF16):
    return jax.ShapeDtypeStruct(shape, dtype)


def dot(a, b):
    return jnp.dot(a, b, preferred_element_type=F32)


def dot_nt(a, b):
    return lax.dot_general(a, b, NT, preferred_element_type=F32)


def swap(x, axis):
    return lax.ppermute(x, axis, [(0, 1), (1, 0)])


def exchange(x):
    return lax.all_to_all(x, YX, 0, 0, tiled=False)


def ranks(inside, base):
    before = lax.broadcasted_iota(jnp.int32, (TOK, TOK), 0)
    after = lax.broadcasted_iota(jnp.int32, (TOK, TOK), 1)
    marks = jnp.where(inside, 1.0, 0.0).astype(BF16)
    rank = dot(marks, jnp.where(before < after, 1.0, 0.0).astype(BF16))
    return jnp.where(inside, rank - base, -1.0)


def look_kernel(at, ids_ref, table_ref, out_ref, most_ref):
    vocab = table_ref.shape[0]
    most = jnp.zeros((16, 1), F32)
    for v in range(16):
        here = (ids_ref[...] >= v * vocab) & (ids_ref[...] < (v + 1) * vocab)
        most = jnp.maximum(most, jnp.sum(jnp.where(here, 1.0, 0.0), axis=1, keepdims=True))
    most_ref[...] = jnp.broadcast_to(jnp.max(most, axis=0, keepdims=True), (8, TOK))
    ids = ids_ref[...] - at[0]
    key = ranks((ids >= 0) & (ids < vocab), (at[1] * SLOTS).astype(F32))
    ids = ids.astype(F32) + 1.0
    slot = lax.broadcasted_iota(jnp.int32, (SLOTS, TOK), 0).astype(F32)
    lanes = lax.broadcasted_iota(jnp.int32, (4 * SLOTS, vocab), 1).astype(F32)
    table = table_ref[...]
    for g in range(4):
        rows = []
        for o in range(4 * g, 4 * g + 4):
            hit = jnp.where(slot == key[o : o + 1], ids[o : o + 1], 0.0)
            rows.append(jnp.sum(hit, axis=1, keepdims=True) - 1.0)
        hot = jnp.where(lanes == jnp.concatenate(rows, axis=0), 1.0, 0.0).astype(BF16)
        found = dot(hot, table).astype(BF16)
        for o in range(4):
            out_ref[4 * g + o] = found[o * SLOTS : (o + 1) * SLOTS]


def place_kernel(vocab, at, ids_ref, rows_ref, out_ref):
    ids = jnp.broadcast_to(ids_ref[...], (16, TOK))
    first = lax.broadcasted_iota(jnp.int32, (16, TOK), 0) * vocab
    key = ranks((ids >= first) & (ids < first + vocab), (at[1] * SLOTS).astype(F32))
    slot = lax.broadcasted_iota(jnp.int32, (SLOTS, TOK), 0).astype(F32)
    hits = [jnp.where(slot == key[v : v + 1], 1.0, 0.0) for v in range(16)]
    hits = jnp.concatenate(hits, axis=0).T.astype(BF16)
    rows = jnp.concatenate([rows_ref[v] for v in range(16)], axis=0)
    out_ref[...] = dot(hits, rows).astype(BF16)


def split_row(row):
    hi = row.astype(BF16)
    lo = (row - hi.astype(F32)).astype(BF16)
    return jnp.broadcast_to(jnp.concatenate([hi, lo], axis=1), (TAIL, COLS))


def join_row(tail):
    both = tail.astype(F32)[0:1]
    return both[:, :TOK] + both[:, TOK:]


def blocks(place, grow):
    for d in range(8):
        yield lax.rem(place[1] + d, 8), grow[d]


def spread_kernel(rows, out):
    for b in range(8):
        out[b] = rows[...]


def hidden_kernel(place, got, other, *refs):
    grow, (part, sent) = refs[:8], refs[8:]
    c = place[0]
    total = jnp.zeros((ROWS, 2 * TOK), F32)
    for b, cols in blocks(place, grow):
        total += dot_nt(cols[...], jnp.concatenate([got[b], other[b]], axis=0))
    for t, rows in ((c, total[:, :TOK]), (1 - c, total[:, TOK:])):
        part[t] = rows
        sent[t] = rows.astype(BF16)


def back_kernel(place, og, *refs):
    grow, (keep, send) = refs[:8], refs[8:]
    c = place[0]
    left = jnp.concatenate([og[c], og[1 - c]], axis=0)
    for b, cols in blocks(place, grow):
        both = dot(left, cols[...]).astype(BF16)
        keep[b] = both[:TOK]
        send[b] = both[TOK:]


def in_kernel(place, part, peer, gain, *refs):
    grow, (hidden_ref, keep, send) = refs[:8], refs[8:]
    c = place[0]
    left = []
    for t, to in ((c, keep), (1 - c, send)):
        hidden = part[t] + peer[t].astype(F32)
        hidden_ref[t] = hidden
        left.append((hidden * gain[...].astype(F32)).T.astype(BF16))
        tail = split_row(jnp.sum(hidden * hidden, axis=0, keepdims=True))
        for b in range(8):
            to[b, TOK:] = tail
    left = jnp.concatenate(left, axis=0)
    for b, cols in blocks(place, grow):
        both = dot(left, cols[...]).astype(BF16)
        keep[b, :TOK] = both[:TOK]
        send[b, :TOK] = both[TOK:]


def second_kernel(keep, recv, back_keep, back_recv, out):
    tail = split_row(join_row(keep[0, TOK:]) + join_row(recv[0, TOK:]))
    for b in range(8):
        out[b, :TOK] = (keep[b, :TOK].astype(F32) + recv[b, :TOK].astype(F32)).astype(BF16)
        out[b, TOK : 2 * TOK] = (back_keep[b].astype(F32) + back_recv[b].astype(F32)).astype(BF16)
        out[b, 2 * TOK :] = tail


def mid_kernel(got, out, inv_ref):
    both = got[0, : 2 * TOK].astype(F32)
    row = join_row(got[0, 2 * TOK :])
    for b in range(1, 8):
        both += got[b, : 2 * TOK].astype(F32)
        row += join_row(got[b, 2 * TOK :])
    inv = lax.rsqrt(jnp.broadcast_to(row, (TOK, TOK)) / D2 + EPS)
    inv_ref[...] = inv[0:8]
    out[:TOK] = (both[:TOK] * inv.T[:, 0:1]).astype(BF16)
    out[TOK:] = both[TOK:].astype(BF16)


def proj_kernel(place, turned, proj, keep, send):
    c = place[0]
    back = turned[TOK:]
    for b in range(8):
        keep[b] = dot_nt(back, proj[2 * b + c]).astype(BF16)
        send[b] = dot_nt(back, proj[2 * b + 1 - c]).astype(BF16)


def third_kernel(turned, keep, recv, out):
    for b in range(8):
        out[b, :TOK] = turned[:TOK]
        out[b, TOK:] = (keep[b].astype(F32) + recv[b].astype(F32)).astype(BF16)


def out_kernel(place, turned, got, other, proj, out, stat_ref):
    c = place[0]
    total = jnp.zeros((TOK, COLS), F32)
    back = jnp.zeros((TOK, COLS), F32)
    for b in range(8):
        total += dot(got[b, :TOK], proj[2 * b + c])
        total += dot(other[b], proj[2 * b + 1 - c])
        back += got[b, TOK:].astype(F32)
    back = back.astype(BF16)
    out[:TOK] = total.astype(BF16)
    out[TOK:] = back
    stat = jnp.sum(back.astype(F32) * turned[:TOK].astype(F32), axis=1, keepdims=True)
    stat_ref[...] = split_row(jnp.broadcast_to(stat, (TOK, TOK)).T[0:1])


def fourth_kernel(turned, stat, out):
    for b in range(8):
        out[b, : 2 * TOK] = turned[...]
        out[b, 2 * TOK :] = stat[...]


def grad_kernel(place, got, other, *refs):
    grow, (part, sent) = refs[:8], refs[8:]
    c = place[0]
    total = jnp.zeros((ROWS, 2 * TOK), F32)
    for b, cols in blocks(place, grow):
        pair = jnp.concatenate([got[b, TOK : 2 * TOK], other[b, :TOK]], axis=0)
        total += dot_nt(cols[...], pair)
    stat = jnp.zeros((1, TOK), F32)
    for b in range(8):
        stat += join_row(got[b, 2 * TOK :]) + join_row(other[b, TOK:])
    both = split_row(stat)
    tail = jnp.concatenate([both[:8, :TOK].astype(F32), both[:8, TOK:].astype(F32)], axis=0)
    for t, rows in ((c, total[:, :TOK]), (1 - c, total[:, TOK:])):
        part[t] = rows
        sent[t, :ROWS] = rows.astype(BF16)
        sent[t, ROWS:] = tail.astype(BF16)


def left_kernel(place, hidden_ref, inv_c, inv_o, gain_ref, og_ref, out):
    c = place[0]
    gain = gain_ref[...].astype(F32)
    normeds, ogs = [], []
    for t, inv_ref in ((c, inv_c), (1 - c, inv_o)):
        normeds.append(hidden_ref[t] * inv_ref[0:1] * gain)
        ogs.append(og_ref[t].astype(F32).T)
    out[...] = jnp.concatenate(normeds + ogs, axis=1).astype(BF16)


def right_rows(b, late, back_o, out_o):
    return [late[b, TOK : 2 * TOK], back_o[b, :TOK], late[b, :TOK], out_o[b]]


def early_kernel(place, left_ref, late, back_o, out_o, *outs):
    left = left_ref[...]
    for d, out in zip(EARLY, outs):
        b = lax.rem(place[1] + d, 8)
        out[...] = dot(left, jnp.concatenate(right_rows(b, late, back_o, out_o), axis=0))


def first_kernel(
    place, part, peer, hidden_ref, inv_c, inv_o, sent, gain_ref, og_ref, emb_m, emb_o, *refs
):
    sums, (left_ref, x4, x3, x5, x8) = refs[:3], refs[3:]
    c = place[0]
    xl = place[2]
    gain = gain_ref[...].astype(F32)
    grads = []
    for t, inv_ref in ((c, inv_c), (1 - c, inv_o)):
        inv = inv_ref[0:1]
        tail = jnp.where(t == xl, sent[0, ROWS:].astype(F32), peer[0, ROWS:].astype(F32))
        mean = (tail[0:1] + tail[8:9]) / inv / D2
        hidden = hidden_ref[t]
        scaled = (part[t] + peer[t, :ROWS].astype(F32)) * gain
        og = og_ref[t].astype(F32).T
        grads.append(og + inv * scaled - hidden * inv * inv * inv * mean)
    left = jnp.concatenate(grads, axis=1).astype(BF16)
    left_ref[...] = left
    half = ROWS // 2
    totals = []
    for d, early in zip(EARLY, sums):
        b = lax.rem(place[1] + d, 8)
        right = jnp.concatenate([emb_m[b], emb_o[b]], axis=0)
        totals.append((dot(left, right) + early[...]).astype(BF16))
    x4[...] = totals[0][:half]
    x8[...] = totals[0][half:]
    x3[...] = totals[1]
    x5[...] = totals[2]


def last_kernel(place, left_ref, more_ref, emb_m, emb_o, late, back_o, out_o, *outs):
    left = jnp.concatenate([left_ref[...], more_ref[...]], axis=1)
    for d, out in zip(LATER, outs):
        b = lax.rem(place[1] + d, 8)
        right = [emb_m[b], emb_o[b], *right_rows(b, late, back_o, out_o)]
        out[...] = dot(left, jnp.concatenate(right, axis=0)).astype(BF16)


def end_kernel(mine, above, below, out):
    out[...] = mine[...].astype(F32) + above[...].astype(F32) + below[...].astype(F32)


def join_kernel(half, mine, near, far, out):
    start = half * (ROWS // 2)
    out[...] = (mine[...].astype(F32) + near[...].astype(F32)).astype(BF16)
    rows = pl.ds(start, ROWS // 2)
    total = mine[rows].astype(F32) + near[rows].astype(F32) + far[...].astype(F32)
    out[rows] = total.astype(BF16)


def turn(x):
    return lax.ppermute(x, ("xl", "c"), [(0, 0), (1, 2), (2, 1), (3, 3)])


def up(v):
    return lax.ppermute(v, "z", [(i, (i + 1) % 8) for i in range(8)])


def down(v):
    return lax.ppermute(v, "z", [(i, (i - 1) % 8) for i in range(8)])


def shards(token_ids, embed, proj, grow_op, norm_gain, out_grad):
    c = lax.axis_index("c")
    z = lax.axis_index("z")
    xl = lax.axis_index("xl")
    place = jnp.stack([c, z, xl]).astype(jnp.int32)
    gain = norm_gain.reshape(ROWS, 1)
    proj = proj.reshape(16, COLS, COLS)
    block = sds((8, TOK, COLS))
    work = 2 * TOK * ROWS * 4096

    with jax.named_scope("embedding"):
        ids = lax.all_to_all(
            jnp.broadcast_to(token_ids.reshape(1, 1, TOK), (16, 1, TOK)), OP, 0, 0, tiled=False
        )
        near = up(grow_op), down(grow_op)
        ids, near = lax.optimization_barrier((ids, near))
        ups, downs = [up(near[0])], [down(near[1])]
        ids = ids.reshape(16, TOK)
        vocab = embed.shape[0]
        first = (z * 2 + xl) * vocab
        own = token_ids.reshape(1, TOK)

        def one(k, held=None):
            at = jnp.stack([first, k]).astype(jnp.int32)
            rows, most = call(
                look_kernel,
                [sds((16, SLOTS, COLS)), sds((8, TOK), F32)],
                at,
                ids,
                embed,
                flops=2 * 16 * SLOTS * vocab * COLS,
            )
            rows, held = lax.optimization_barrier((rows, held))
            rows = lax.all_to_all(rows, OP, 0, 0, tiled=False)
            if held:
                step = up(held[0]), down(held[1]), swap(held[2], "xl")
                rows, step = lax.optimization_barrier((rows, step))
                held = (*held[:2], *step)
            part = call(
                functools.partial(place_kernel, vocab),
                sds((TOK, COLS)),
                at,
                own,
                rows,
                flops=2 * 16 * SLOTS * TOK * COLS,
            )
            return part, most[0, 0], held

        half = ROWS // 2
        found, most, held = one(jnp.int32(0), (ups[0], downs[0], out_grad))
        ups, downs, og_peer = [held[0], held[2]], [held[1], held[3]], held[4]
        found = lax.while_loop(
            lambda state: (state[0] * SLOTS).astype(F32) < most,
            lambda state: (state[0] + 1, state[1] + one(state[0])[0]),
            (jnp.int32(1), found),
        )
        emb_part = turn(found[1])
        far = [up(ups[1][:half]), down(downs[1][half:])]

    with jax.named_scope("operator"):
        og = jnp.stack([jnp.where(xl == 0, out_grad, og_peer), jnp.where(xl == 0, og_peer, out_grad)])

    with jax.named_scope("first"):
        emb = exchange(call(spread_kernel, block, emb_part))
        emb, far = lax.optimization_barrier((emb, far))
        first_up, first_down = near
        grow = [grow_op, first_down, *downs, jnp.concatenate(far, axis=0), *ups[::-1], first_up]
        emb_other = swap(emb, "c")
        back_keep, back_send = call(back_kernel, [block, block], place, og, *grow, flops=work)
        emb_other, back_send = lax.optimization_barrier((emb_other, back_send))

    with jax.named_scope("hidden"):
        pair = sds((2, ROWS, TOK), F32)
        part, sent = call(
            hidden_kernel,
            [pair, sds((2, ROWS, TOK))],
            place,
            emb,
            emb_other,
            *grow,
            flops=work,
        )
        peer = swap(sent, "xl")
        peer, back_recv = lax.optimization_barrier((peer, swap(back_send, "c")))
        short = sds((8, TOK + TAIL, COLS))
        hidden, keep, send = call(
            in_kernel, [pair, short, short], place, part, peer, gain, *grow, flops=work
        )

    with jax.named_scope("second"):
        longer = sds((8, 2 * TOK + TAIL, COLS))
        got = exchange(
            call(second_kernel, longer, keep, swap(send, "c"), back_keep, back_recv)
        )
        before, inv = call(mid_kernel, [sds((2 * TOK, COLS)), sds((8, TOK), F32)], got)
        turned, inv_other = lax.optimization_barrier((turn(before), swap(inv, "c")))

    with jax.named_scope("third"):
        keep, send = call(
            proj_kernel, [block, block], place, turned, proj, flops=2 * TOK * COLS * 4096
        )
        got = exchange(
            call(third_kernel, sds((8, 2 * TOK, COLS)), turned, keep, swap(send, "c"))
        )
        out, stat = call(
            out_kernel,
            [sds((2 * TOK, COLS)), sds((TAIL, COLS))],
            place,
            turned,
            got,
            swap(got[:, :TOK], "c"),
            proj,
            flops=2 * TOK * COLS * 4096,
        )

    with jax.named_scope("fourth"):
        late = exchange(call(fourth_kernel, longer, turn(out), stat))
        back_other = swap(late[:, TOK:], "c")
        part, sent = call(
            grad_kernel,
            [pair, sds((2, ROWS + TAIL, TOK))],
            place,
            late,
            back_other,
            *grow,
            flops=work,
        )
        late, sent = lax.optimization_barrier((late, sent))
        peer = swap(sent, "xl")
        more = call(left_kernel, sds((ROWS, 4 * TOK)), place, hidden, inv, inv_other, gain, og)
        late, more = lax.optimization_barrier((late, more))
        out_other = swap(late[:, :TOK], "c")
        right = late, back_other, out_other
        tile = sds((ROWS, COLS))
        early = call(
            early_kernel, [sds((ROWS, COLS), F32)] * 3, place, more, *right, flops=3 * work // 4
        )
        peer, early = lax.optimization_barrier((peer, early))
        half_tile = sds((ROWS // 2, COLS))
        left, *first = call(
            first_kernel,
            [sds((ROWS, 2 * TOK)), half_tile, tile, tile, half_tile],
            place,
            part,
            peer,
            hidden,
            inv,
            inv_other,
            sent,
            gain,
            og,
            emb,
            emb_other,
            *early,
            flops=3 * work // 8,
        )
        x = dict(zip((*EARLY, 8), first))
        later = call(
            last_kernel,
            [tile] * 5,
            place,
            left,
            more,
            emb,
            emb_other,
            *right,
            flops=15 * work // 8,
        )
        x.update(zip(LATER, later))

    def add(a, b):
        return (a.astype(F32) + b.astype(F32)).astype(BF16)

    with jax.named_scope("scatter"):
        up_far = lax.ppermute(x[4], "z", [(i, (i + 2) % 8) for i in range(8)])
        down_far = lax.ppermute(x[8], "z", [(i, (i - 2) % 8) for i in range(8)])
        above, below = up(x[3]), down(x[5])
        near = above, below, up_far, down_far
        above, below, up_far, down_far = lax.optimization_barrier(near)
        above = up(call(functools.partial(join_kernel, 0), tile, x[2], above, up_far))
        below = down(call(functools.partial(join_kernel, 1), tile, x[6], below, down_far))
        above, below = up(add(above, x[1])), down(add(below, x[7]))
        return call(end_kernel, sds((ROWS, COLS), F32), x[0], above, below)


def solution(mesh):
    fine = Mesh(mesh.devices.reshape(8, 2, 4, 2, 2), ("z", "xl", "y", "xh", "c"))
    in_specs = (P(OP), P(OP, TP), P(None, TP), P(TP, OP), P(TP), P(OP, TP))
    return jax.shard_map(shards, mesh=fine, in_specs=in_specs, out_specs=P(TP, OP), check_vma=False)
```

```python
import functools

import jax
import jax.numpy as jnp
import numpy as np
from jax import lax
from jax.experimental import pallas as pl
from jax.experimental.pallas import tpu as pltpu
from jax.sharding import Mesh, PartitionSpec as P

D2 = 6656
EPS = 1e-05
TOK = 128
ROWS = 416
COLS = 256
TAIL = 16
SLOTS = 48
OP = ("z", "xl")
TP = ("y", "xh", "c")
YX = ("y", "xh")
F32 = jnp.float32
BF16 = jnp.bfloat16
NT = (((1,), (1,)), ((), ()))
EARLY = (4, 3, 5)
LATER = (2, 6, 1, 7, 0)


def call(kernel, out_shape, *args, flops=0):
    smem = pl.BlockSpec(memory_space=pltpu.SMEM)
    vmem = pl.BlockSpec(memory_space=pltpu.VMEM)
    single = not isinstance(out_shape, (list, tuple))
    outs = [out_shape] if single else list(out_shape)
    nbytes = sum(int(np.prod(a.shape)) * a.dtype.itemsize for a in list(args) + outs)
    return pl.pallas_call(
        kernel,
        out_shape=out_shape,
        in_specs=[smem if a.dtype == jnp.int32 and a.ndim == 1 else vmem for a in args],
        out_specs=vmem if single else [vmem] * len(outs),
        compiler_params=pltpu.CompilerParams(vmem_limit_bytes=20 * 1024 * 1024),
        cost_estimate=pl.CostEstimate(flops=flops, bytes_accessed=nbytes, transcendentals=0),
    )(*args)


def sds(shape, dtype=BF16):
    return jax.ShapeDtypeStruct(shape, dtype)


def dot(a, b):
    return jnp.dot(a, b, preferred_element_type=F32)


def dot_nt(a, b):
    return lax.dot_general(a, b, NT, preferred_element_type=F32)


def swap(x, axis):
    return lax.ppermute(x, axis, [(0, 1), (1, 0)])


def exchange(x):
    return lax.all_to_all(x, YX, 0, 0, tiled=False)


def ranks(inside, base):
    before = lax.broadcasted_iota(jnp.int32, (TOK, TOK), 0)
    after = lax.broadcasted_iota(jnp.int32, (TOK, TOK), 1)
    marks = jnp.where(inside, 1.0, 0.0).astype(BF16)
    rank = dot(marks, jnp.where(before < after, 1.0, 0.0).astype(BF16))
    return jnp.where(inside, rank - base, -1.0)


def look_kernel(at, ids_ref, table_ref, out_ref, most_ref):
    vocab = table_ref.shape[0]
    most = jnp.zeros((16, 1), F32)
    for v in range(16):
        here = (ids_ref[...] >= v * vocab) & (ids_ref[...] < (v + 1) * vocab)
        most = jnp.maximum(most, jnp.sum(jnp.where(here, 1.0, 0.0), axis=1, keepdims=True))
    most_ref[...] = jnp.broadcast_to(jnp.max(most, axis=0, keepdims=True), (8, TOK))
    ids = ids_ref[...] - at[0]
    key = ranks((ids >= 0) & (ids < vocab), (at[1] * SLOTS).astype(F32))
    ids = ids.astype(F32) + 1.0
    slot = lax.broadcasted_iota(jnp.int32, (SLOTS, TOK), 0).astype(F32)
    lanes = lax.broadcasted_iota(jnp.int32, (4 * SLOTS, vocab), 1).astype(F32)
    table = table_ref[...]
    for g in range(4):
        rows = []
        for o in range(4 * g, 4 * g + 4):
            hit = jnp.where(slot == key[o : o + 1], ids[o : o + 1], 0.0)
            rows.append(jnp.sum(hit, axis=1, keepdims=True) - 1.0)
        hot = jnp.where(lanes == jnp.concatenate(rows, axis=0), 1.0, 0.0).astype(BF16)
        found = dot(hot, table).astype(BF16)
        for o in range(4):
            out_ref[4 * g + o] = found[o * SLOTS : (o + 1) * SLOTS]


def place_kernel(vocab, at, ids_ref, rows_ref, out_ref):
    ids = jnp.broadcast_to(ids_ref[...], (16, TOK))
    first = lax.broadcasted_iota(jnp.int32, (16, TOK), 0) * vocab
    key = ranks((ids >= first) & (ids < first + vocab), (at[1] * SLOTS).astype(F32))
    slot = lax.broadcasted_iota(jnp.int32, (SLOTS, TOK), 0).astype(F32)
    hits = [jnp.where(slot == key[v : v + 1], 1.0, 0.0) for v in range(16)]
    hits = jnp.concatenate(hits, axis=0).T.astype(BF16)
    rows = jnp.concatenate([rows_ref[v] for v in range(16)], axis=0)
    out_ref[...] = dot(hits, rows).astype(BF16)


def split_row(row):
    hi = row.astype(BF16)
    lo = (row - hi.astype(F32)).astype(BF16)
    return jnp.broadcast_to(jnp.concatenate([hi, lo], axis=1), (TAIL, COLS))


def join_row(tail):
    both = tail.astype(F32)[0:1]
    return both[:, :TOK] + both[:, TOK:]


def blocks(place, grow):
    for d in range(8):
        yield lax.rem(place[1] + d, 8), grow[d]


def spread_kernel(rows, out):
    for b in range(8):
        out[b] = rows[...]


def hidden_kernel(place, got, other, *refs):
    grow, (part, sent) = refs[:8], refs[8:]
    c = place[0]
    total = jnp.zeros((ROWS, 2 * TOK), F32)
    for b, cols in blocks(place, grow):
        total += dot_nt(cols[...], jnp.concatenate([got[b], other[b]], axis=0))
    for t, rows in ((c, total[:, :TOK]), (1 - c, total[:, TOK:])):
        part[t] = rows
        sent[t] = rows.astype(BF16)


def back_kernel(place, og, *refs):
    grow, (keep, send) = refs[:8], refs[8:]
    c = place[0]
    left = jnp.concatenate([og[c], og[1 - c]], axis=0)
    for b, cols in blocks(place, grow):
        both = dot(left, cols[...]).astype(BF16)
        keep[b] = both[:TOK]
        send[b] = both[TOK:]


def in_kernel(place, part, peer, gain, *refs):
    grow, (hidden_ref, keep, send) = refs[:8], refs[8:]
    c = place[0]
    left = []
    for t, to in ((c, keep), (1 - c, send)):
        hidden = part[t] + peer[t].astype(F32)
        hidden_ref[t] = hidden
        left.append((hidden * gain[...].astype(F32)).T.astype(BF16))
        tail = split_row(jnp.sum(hidden * hidden, axis=0, keepdims=True))
        for b in range(8):
            to[b, TOK:] = tail
    left = jnp.concatenate(left, axis=0)
    for b, cols in blocks(place, grow):
        both = dot(left, cols[...]).astype(BF16)
        keep[b, :TOK] = both[:TOK]
        send[b, :TOK] = both[TOK:]


def second_kernel(keep, recv, back_keep, back_recv, out):
    tail = split_row(join_row(keep[0, TOK:]) + join_row(recv[0, TOK:]))
    for b in range(8):
        out[b, :TOK] = (keep[b, :TOK].astype(F32) + recv[b, :TOK].astype(F32)).astype(BF16)
        out[b, TOK : 2 * TOK] = (back_keep[b].astype(F32) + back_recv[b].astype(F32)).astype(BF16)
        out[b, 2 * TOK :] = tail


def mid_kernel(got, out, inv_ref):
    both = got[0, : 2 * TOK].astype(F32)
    row = join_row(got[0, 2 * TOK :])
    for b in range(1, 8):
        both += got[b, : 2 * TOK].astype(F32)
        row += join_row(got[b, 2 * TOK :])
    inv = lax.rsqrt(jnp.broadcast_to(row, (TOK, TOK)) / D2 + EPS)
    inv_ref[...] = inv[0:8]
    out[:TOK] = (both[:TOK] * inv.T[:, 0:1]).astype(BF16)
    out[TOK:] = both[TOK:].astype(BF16)


def proj_kernel(place, turned, proj, keep, send):
    c = place[0]
    back = turned[TOK:]
    for b in range(8):
        keep[b] = dot_nt(back, proj[2 * b + c]).astype(BF16)
        send[b] = dot_nt(back, proj[2 * b + 1 - c]).astype(BF16)


def third_kernel(turned, keep, recv, out):
    for b in range(8):
        out[b, :TOK] = turned[:TOK]
        out[b, TOK:] = (keep[b].astype(F32) + recv[b].astype(F32)).astype(BF16)


def out_kernel(place, turned, got, other, proj, out, stat_ref):
    c = place[0]
    total = jnp.zeros((TOK, COLS), F32)
    back = jnp.zeros((TOK, COLS), F32)
    for b in range(8):
        total += dot(got[b, :TOK], proj[2 * b + c])
        total += dot(other[b], proj[2 * b + 1 - c])
        back += got[b, TOK:].astype(F32)
    back = back.astype(BF16)
    out[:TOK] = total.astype(BF16)
    out[TOK:] = back
    stat = jnp.sum(back.astype(F32) * turned[:TOK].astype(F32), axis=1, keepdims=True)
    stat_ref[...] = split_row(jnp.broadcast_to(stat, (TOK, TOK)).T[0:1])


def fourth_kernel(turned, stat, out):
    for b in range(8):
        out[b, : 2 * TOK] = turned[...]
        out[b, 2 * TOK :] = stat[...]


def grad_kernel(place, got, other, *refs):
    grow, (part, sent) = refs[:8], refs[8:]
    c = place[0]
    total = jnp.zeros((ROWS, 2 * TOK), F32)
    for b, cols in blocks(place, grow):
        pair = jnp.concatenate([got[b, TOK : 2 * TOK], other[b, :TOK]], axis=0)
        total += dot_nt(cols[...], pair)
    stat = jnp.zeros((1, TOK), F32)
    for b in range(8):
        stat += join_row(got[b, 2 * TOK :]) + join_row(other[b, TOK:])
    both = split_row(stat)
    tail = jnp.concatenate([both[:8, :TOK].astype(F32), both[:8, TOK:].astype(F32)], axis=0)
    for t, rows in ((c, total[:, :TOK]), (1 - c, total[:, TOK:])):
        part[t] = rows
        sent[t, :ROWS] = rows.astype(BF16)
        sent[t, ROWS:] = tail.astype(BF16)


def left_kernel(place, hidden_ref, inv_c, inv_o, gain_ref, og_ref, out):
    c = place[0]
    gain = gain_ref[...].astype(F32)
    normeds, ogs = [], []
    for t, inv_ref in ((c, inv_c), (1 - c, inv_o)):
        normeds.append(hidden_ref[t] * inv_ref[0:1] * gain)
        ogs.append(og_ref[t].astype(F32).T)
    out[...] = jnp.concatenate(normeds + ogs, axis=1).astype(BF16)


def right_rows(b, late, back_o, out_o):
    return [late[b, TOK : 2 * TOK], back_o[b, :TOK], late[b, :TOK], out_o[b]]


def early_kernel(place, left_ref, late, back_o, out_o, *outs):
    left = left_ref[...]
    for d, out in zip(EARLY, outs):
        b = lax.rem(place[1] + d, 8)
        out[...] = dot(left, jnp.concatenate(right_rows(b, late, back_o, out_o), axis=0))


def first_kernel(
    place, part, peer, hidden_ref, inv_c, inv_o, sent, gain_ref, og_ref, emb_m, emb_o, *refs
):
    sums, (left_ref, x4, x3, x5, x8) = refs[:3], refs[3:]
    c = place[0]
    xl = place[2]
    gain = gain_ref[...].astype(F32)
    grads = []
    for t, inv_ref in ((c, inv_c), (1 - c, inv_o)):
        inv = inv_ref[0:1]
        tail = jnp.where(t == xl, sent[0, ROWS:].astype(F32), peer[0, ROWS:].astype(F32))
        mean = (tail[0:1] + tail[8:9]) / inv / D2
        hidden = hidden_ref[t]
        scaled = (part[t] + peer[t, :ROWS].astype(F32)) * gain
        og = og_ref[t].astype(F32).T
        grads.append(og + inv * scaled - hidden * inv * inv * inv * mean)
    left = jnp.concatenate(grads, axis=1).astype(BF16)
    left_ref[...] = left
    half = ROWS // 2
    totals = []
    for d, early in zip(EARLY, sums):
        b = lax.rem(place[1] + d, 8)
        right = jnp.concatenate([emb_m[b], emb_o[b]], axis=0)
        totals.append((dot(left, right) + early[...]).astype(BF16))
    x4[...] = totals[0][:half]
    x8[...] = totals[0][half:]
    x3[...] = totals[1]
    x5[...] = totals[2]


def last_kernel(place, left_ref, more_ref, emb_m, emb_o, late, back_o, out_o, *outs):
    left = jnp.concatenate([left_ref[...], more_ref[...]], axis=1)
    for d, out in zip(LATER, outs):
        b = lax.rem(place[1] + d, 8)
        right = [emb_m[b], emb_o[b], *right_rows(b, late, back_o, out_o)]
        out[...] = dot(left, jnp.concatenate(right, axis=0)).astype(BF16)


def end_kernel(mine, above, below, out):
    out[...] = mine[...].astype(F32) + above[...].astype(F32) + below[...].astype(F32)


def join_kernel(half, mine, near, far, out):
    start = half * (ROWS // 2)
    out[...] = (mine[...].astype(F32) + near[...].astype(F32)).astype(BF16)
    rows = pl.ds(start, ROWS // 2)
    total = mine[rows].astype(F32) + near[rows].astype(F32) + far[...].astype(F32)
    out[rows] = total.astype(BF16)


def turn(x):
    return lax.ppermute(x, ("xl", "c"), [(0, 0), (1, 2), (2, 1), (3, 3)])


def up(v):
    return lax.ppermute(v, "z", [(i, (i + 1) % 8) for i in range(8)])


def down(v):
    return lax.ppermute(v, "z", [(i, (i - 1) % 8) for i in range(8)])


def shards(token_ids, embed, proj, grow_op, norm_gain, out_grad):
    c = lax.axis_index("c")
    z = lax.axis_index("z")
    xl = lax.axis_index("xl")
    place = jnp.stack([c, z, xl]).astype(jnp.int32)
    gain = norm_gain.reshape(ROWS, 1)
    proj = proj.reshape(16, COLS, COLS)
    block = sds((8, TOK, COLS))
    work = 2 * TOK * ROWS * 4096

    with jax.named_scope("embedding"):
        ids = lax.all_to_all(
            jnp.broadcast_to(token_ids.reshape(1, 1, TOK), (16, 1, TOK)), OP, 0, 0, tiled=False
        )
        near = up(grow_op), down(grow_op)
        ids, near = lax.optimization_barrier((ids, near))
        ups, downs = [up(near[0])], [down(near[1])]
        ids = ids.reshape(16, TOK)
        vocab = embed.shape[0]
        first = (z * 2 + xl) * vocab
        own = token_ids.reshape(1, TOK)

        def one(k, held=None):
            at = jnp.stack([first, k]).astype(jnp.int32)
            rows, most = call(
                look_kernel,
                [sds((16, SLOTS, COLS)), sds((8, TOK), F32)],
                at,
                ids,
                embed,
                flops=2 * 16 * SLOTS * vocab * COLS,
            )
            rows, held = lax.optimization_barrier((rows, held))
            rows = lax.all_to_all(rows, OP, 0, 0, tiled=False)
            if held:
                step = up(held[0]), down(held[1]), swap(held[2], "xl")
                rows, step = lax.optimization_barrier((rows, step))
                held = (*held[:2], *step)
            part = call(
                functools.partial(place_kernel, vocab),
                sds((TOK, COLS)),
                at,
                own,
                rows,
                flops=2 * 16 * SLOTS * TOK * COLS,
            )
            return part, most[0, 0], held

        half = ROWS // 2
        found, most, held = one(jnp.int32(0), (ups[0], downs[0], out_grad))
        ups, downs, og_peer = [held[0], held[2]], [held[1], held[3]], held[4]
        found = lax.while_loop(
            lambda state: (state[0] * SLOTS).astype(F32) < most,
            lambda state: (state[0] + 1, state[1] + one(state[0])[0]),
            (jnp.int32(1), found),
        )
        emb_part = turn(found[1])
        far = [up(ups[1][:half]), down(downs[1][half:])]

    with jax.named_scope("operator"):
        og = jnp.stack([jnp.where(xl == 0, out_grad, og_peer), jnp.where(xl == 0, og_peer, out_grad)])

    with jax.named_scope("first"):
        emb = exchange(call(spread_kernel, block, emb_part))
        emb, far = lax.optimization_barrier((emb, far))
        first_up, first_down = near
        grow = [grow_op, first_down, *downs, jnp.concatenate(far, axis=0), *ups[::-1], first_up]
        emb_other = swap(emb, "c")
        back_keep, back_send = call(back_kernel, [block, block], place, og, *grow, flops=work)
        emb_other, back_send = lax.optimization_barrier((emb_other, back_send))

    with jax.named_scope("hidden"):
        pair = sds((2, ROWS, TOK), F32)
        part, sent = call(
            hidden_kernel,
            [pair, sds((2, ROWS, TOK))],
            place,
            emb,
            emb_other,
            *grow,
            flops=work,
        )
        peer = swap(sent, "xl")
        peer, back_recv = lax.optimization_barrier((peer, swap(back_send, "c")))
        short = sds((8, TOK + TAIL, COLS))
        hidden, keep, send = call(
            in_kernel, [pair, short, short], place, part, peer, gain, *grow, flops=work
        )

    with jax.named_scope("second"):
        longer = sds((8, 2 * TOK + TAIL, COLS))
        got = exchange(
            call(second_kernel, longer, keep, swap(send, "c"), back_keep, back_recv)
        )
        before, inv = call(mid_kernel, [sds((2 * TOK, COLS)), sds((8, TOK), F32)], got)
        turned = turn(before)

    with jax.named_scope("third"):
        keep, send = call(
            proj_kernel, [block, block], place, turned, proj, flops=2 * TOK * COLS * 4096
        )
        got = exchange(
            call(third_kernel, sds((8, 2 * TOK, COLS)), turned, keep, swap(send, "c"))
        )
        got, inv = lax.optimization_barrier((got, inv))
        in_other, inv_other = lax.optimization_barrier((swap(got[:, :TOK], "c"), swap(inv, "c")))
        out, stat = call(
            out_kernel,
            [sds((2 * TOK, COLS)), sds((TAIL, COLS))],
            place,
            turned,
            got,
            in_other,
            proj,
            flops=2 * TOK * COLS * 4096,
        )

    with jax.named_scope("fourth"):
        late = exchange(call(fourth_kernel, longer, turn(out), stat))
        back_other = swap(late[:, TOK:], "c")
        part, sent = call(
            grad_kernel,
            [pair, sds((2, ROWS + TAIL, TOK))],
            place,
            late,
            back_other,
            *grow,
            flops=work,
        )
        late, sent = lax.optimization_barrier((late, sent))
        peer = swap(sent, "xl")
        more = call(left_kernel, sds((ROWS, 4 * TOK)), place, hidden, inv, inv_other, gain, og)
        late, more = lax.optimization_barrier((late, more))
        out_other = swap(late[:, :TOK], "c")
        right = late, back_other, out_other
        tile = sds((ROWS, COLS))
        early = call(
            early_kernel, [sds((ROWS, COLS), F32)] * 3, place, more, *right, flops=3 * work // 4
        )
        peer, early = lax.optimization_barrier((peer, early))
        half_tile = sds((ROWS // 2, COLS))
        left, *first = call(
            first_kernel,
            [sds((ROWS, 2 * TOK)), half_tile, tile, tile, half_tile],
            place,
            part,
            peer,
            hidden,
            inv,
            inv_other,
            sent,
            gain,
            og,
            emb,
            emb_other,
            *early,
            flops=3 * work // 8,
        )
        x = dict(zip((*EARLY, 8), first))
        later = call(
            last_kernel,
            [tile] * 5,
            place,
            left,
            more,
            emb,
            emb_other,
            *right,
            flops=15 * work // 8,
        )
        x.update(zip(LATER, later))

    def add(a, b):
        return (a.astype(F32) + b.astype(F32)).astype(BF16)

    with jax.named_scope("scatter"):
        up_far = lax.ppermute(x[4], "z", [(i, (i + 2) % 8) for i in range(8)])
        down_far = lax.ppermute(x[8], "z", [(i, (i - 2) % 8) for i in range(8)])
        above, below = up(x[3]), down(x[5])
        near = above, below, up_far, down_far
        above, below, up_far, down_far = lax.optimization_barrier(near)
        above = up(call(functools.partial(join_kernel, 0), tile, x[2], above, up_far))
        below = down(call(functools.partial(join_kernel, 1), tile, x[6], below, down_far))
        above, below = up(add(above, x[1])), down(add(below, x[7]))
        return call(end_kernel, sds((ROWS, COLS), F32), x[0], above, below)


def solution(mesh):
    fine = Mesh(mesh.devices.reshape(8, 2, 4, 2, 2), ("z", "xl", "y", "xh", "c"))
    in_specs = (P(OP), P(OP, TP), P(None, TP), P(TP, OP), P(TP), P(OP, TP))
    return jax.shard_map(shards, mesh=fine, in_specs=in_specs, out_specs=P(TP, OP), check_vma=False)
```

```python
import functools

import jax
import jax.numpy as jnp
import numpy as np
from jax import lax
from jax.experimental import pallas as pl
from jax.experimental.pallas import tpu as pltpu
from jax.sharding import Mesh, PartitionSpec as P

D2 = 6656
EPS = 1e-05
TOK = 128
ROWS = 416
COLS = 256
TAIL = 16
SLOTS = 48
OP = ("z", "xl")
TP = ("y", "xh", "c")
YX = ("y", "xh")
F32 = jnp.float32
BF16 = jnp.bfloat16
NT = (((1,), (1,)), ((), ()))
EARLY = (4, 3, 5)
LATER = (2, 6, 1, 7, 0)


def call(kernel, out_shape, *args, flops=0):
    smem = pl.BlockSpec(memory_space=pltpu.SMEM)
    vmem = pl.BlockSpec(memory_space=pltpu.VMEM)
    single = not isinstance(out_shape, (list, tuple))
    outs = [out_shape] if single else list(out_shape)
    nbytes = sum(int(np.prod(a.shape)) * a.dtype.itemsize for a in list(args) + outs)
    return pl.pallas_call(
        kernel,
        out_shape=out_shape,
        in_specs=[smem if a.dtype == jnp.int32 and a.ndim == 1 else vmem for a in args],
        out_specs=vmem if single else [vmem] * len(outs),
        compiler_params=pltpu.CompilerParams(vmem_limit_bytes=20 * 1024 * 1024),
        cost_estimate=pl.CostEstimate(flops=flops, bytes_accessed=nbytes, transcendentals=0),
    )(*args)


def sds(shape, dtype=BF16):
    return jax.ShapeDtypeStruct(shape, dtype)


def dot(a, b):
    return jnp.dot(a, b, preferred_element_type=F32)


def dot_nt(a, b):
    return lax.dot_general(a, b, NT, preferred_element_type=F32)


def swap(x, axis):
    return lax.ppermute(x, axis, [(0, 1), (1, 0)])


def exchange(x):
    return lax.all_to_all(x, YX, 0, 0, tiled=False)


def ranks(inside, base):
    before = lax.broadcasted_iota(jnp.int32, (TOK, TOK), 0)
    after = lax.broadcasted_iota(jnp.int32, (TOK, TOK), 1)
    marks = jnp.where(inside, 1.0, 0.0).astype(BF16)
    rank = dot(marks, jnp.where(before < after, 1.0, 0.0).astype(BF16))
    return jnp.where(inside, rank - base, -1.0)


def look_kernel(at, ids_ref, table_ref, out_ref, most_ref):
    vocab = table_ref.shape[0]
    most = jnp.zeros((16, 1), F32)
    for v in range(16):
        here = (ids_ref[...] >= v * vocab) & (ids_ref[...] < (v + 1) * vocab)
        most = jnp.maximum(most, jnp.sum(jnp.where(here, 1.0, 0.0), axis=1, keepdims=True))
    most_ref[...] = jnp.broadcast_to(jnp.max(most, axis=0, keepdims=True), (8, TOK))
    ids = ids_ref[...] - at[0]
    key = ranks((ids >= 0) & (ids < vocab), (at[1] * SLOTS).astype(F32))
    ids = ids.astype(F32) + 1.0
    slot = lax.broadcasted_iota(jnp.int32, (SLOTS, TOK), 0).astype(F32)
    lanes = lax.broadcasted_iota(jnp.int32, (4 * SLOTS, vocab), 1).astype(F32)
    table = table_ref[...]
    for g in range(4):
        rows = []
        for o in range(4 * g, 4 * g + 4):
            hit = jnp.where(slot == key[o : o + 1], ids[o : o + 1], 0.0)
            rows.append(jnp.sum(hit, axis=1, keepdims=True) - 1.0)
        hot = jnp.where(lanes == jnp.concatenate(rows, axis=0), 1.0, 0.0).astype(BF16)
        found = dot(hot, table).astype(BF16)
        for o in range(4):
            out_ref[4 * g + o] = found[o * SLOTS : (o + 1) * SLOTS]


def place_kernel(vocab, at, ids_ref, rows_ref, out_ref):
    ids = jnp.broadcast_to(ids_ref[...], (16, TOK))
    first = lax.broadcasted_iota(jnp.int32, (16, TOK), 0) * vocab
    key = ranks((ids >= first) & (ids < first + vocab), (at[1] * SLOTS).astype(F32))
    slot = lax.broadcasted_iota(jnp.int32, (SLOTS, TOK), 0).astype(F32)
    hits = [jnp.where(slot == key[v : v + 1], 1.0, 0.0) for v in range(16)]
    hits = jnp.concatenate(hits, axis=0).T.astype(BF16)
    rows = jnp.concatenate([rows_ref[v] for v in range(16)], axis=0)
    out_ref[...] = dot(hits, rows).astype(BF16)


def split_row(row):
    hi = row.astype(BF16)
    lo = (row - hi.astype(F32)).astype(BF16)
    return jnp.broadcast_to(jnp.concatenate([hi, lo], axis=1), (TAIL, COLS))


def join_row(tail):
    both = tail.astype(F32)[0:1]
    return both[:, :TOK] + both[:, TOK:]


def blocks(place, grow):
    for d in range(8):
        yield lax.rem(place[1] + d, 8), grow[d]


def spread_kernel(rows, out):
    for b in range(8):
        out[b] = rows[...]


def hidden_kernel(place, got, other, *refs):
    grow, (part, sent) = refs[:8], refs[8:]
    c = place[0]
    total = jnp.zeros((ROWS, 2 * TOK), F32)
    for b, cols in blocks(place, grow):
        total += dot_nt(cols[...], jnp.concatenate([got[b], other[b]], axis=0))
    for t, rows in ((c, total[:, :TOK]), (1 - c, total[:, TOK:])):
        part[t] = rows
        sent[t] = rows.astype(BF16)


def back_kernel(place, og, *refs):
    grow, (keep, send) = refs[:8], refs[8:]
    c = place[0]
    left = jnp.concatenate([og[c], og[1 - c]], axis=0)
    for b, cols in blocks(place, grow):
        both = dot(left, cols[...]).astype(BF16)
        keep[b] = both[:TOK]
        send[b] = both[TOK:]


def in_kernel(place, part, peer, gain, *refs):
    grow, (hidden_ref, keep, send) = refs[:8], refs[8:]
    c = place[0]
    left = []
    for t, to in ((c, keep), (1 - c, send)):
        hidden = part[t] + peer[t].astype(F32)
        hidden_ref[t] = hidden
        left.append((hidden * gain[...].astype(F32)).T.astype(BF16))
        tail = split_row(jnp.sum(hidden * hidden, axis=0, keepdims=True))
        for b in range(8):
            to[b, TOK:] = tail
    left = jnp.concatenate(left, axis=0)
    for b, cols in blocks(place, grow):
        both = dot(left, cols[...]).astype(BF16)
        keep[b, :TOK] = both[:TOK]
        send[b, :TOK] = both[TOK:]


def second_kernel(keep, recv, back_keep, back_recv, out):
    tail = split_row(join_row(keep[0, TOK:]) + join_row(recv[0, TOK:]))
    for b in range(8):
        out[b, :TOK] = (keep[b, :TOK].astype(F32) + recv[b, :TOK].astype(F32)).astype(BF16)
        out[b, TOK : 2 * TOK] = (back_keep[b].astype(F32) + back_recv[b].astype(F32)).astype(BF16)
        out[b, 2 * TOK :] = tail


def mid_kernel(got, out, inv_ref):
    both = got[0, : 2 * TOK].astype(F32)
    row = join_row(got[0, 2 * TOK :])
    for b in range(1, 8):
        both += got[b, : 2 * TOK].astype(F32)
        row += join_row(got[b, 2 * TOK :])
    inv = lax.rsqrt(jnp.broadcast_to(row, (TOK, TOK)) / D2 + EPS)
    inv_ref[...] = inv[0:8]
    out[:TOK] = (both[:TOK] * inv.T[:, 0:1]).astype(BF16)
    out[TOK:] = both[TOK:].astype(BF16)


def proj_kernel(place, turned, proj, keep, send):
    c = place[0]
    back = turned[TOK:]
    for b in range(8):
        keep[b] = dot_nt(back, proj[2 * b + c]).astype(BF16)
        send[b] = dot_nt(back, proj[2 * b + 1 - c]).astype(BF16)


def third_kernel(turned, keep, recv, out):
    for b in range(8):
        out[b, :TOK] = turned[:TOK]
        out[b, TOK:] = (keep[b].astype(F32) + recv[b].astype(F32)).astype(BF16)


def out_kernel(place, turned, got, other, proj, out, stat_ref):
    c = place[0]
    total = jnp.zeros((TOK, COLS), F32)
    back = jnp.zeros((TOK, COLS), F32)
    for b in range(8):
        total += dot(got[b, :TOK], proj[2 * b + c])
        total += dot(other[b], proj[2 * b + 1 - c])
        back += got[b, TOK:].astype(F32)
    back = back.astype(BF16)
    out[:TOK] = total.astype(BF16)
    out[TOK:] = back
    stat = jnp.sum(back.astype(F32) * turned[:TOK].astype(F32), axis=1, keepdims=True)
    stat_ref[...] = split_row(jnp.broadcast_to(stat, (TOK, TOK)).T[0:1])


def fourth_kernel(turned, stat, out):
    for b in range(8):
        out[b, : 2 * TOK] = turned[...]
        out[b, 2 * TOK :] = stat[...]


def grad_kernel(place, got, other, *refs):
    grow, (part, sent) = refs[:8], refs[8:]
    c = place[0]
    total = jnp.zeros((ROWS, 2 * TOK), F32)
    for b, cols in blocks(place, grow):
        pair = jnp.concatenate([got[b, TOK : 2 * TOK], other[b, :TOK]], axis=0)
        total += dot_nt(cols[...], pair)
    stat = jnp.zeros((1, TOK), F32)
    for b in range(8):
        stat += join_row(got[b, 2 * TOK :]) + join_row(other[b, TOK:])
    both = split_row(stat).astype(F32)
    tail = jnp.concatenate([both[:8, :TOK], both[:8, TOK:]], axis=0)
    for t, rows in ((c, total[:, :TOK]), (1 - c, total[:, TOK:])):
        part[t] = rows
        sent[t, :ROWS] = rows.astype(BF16)
        sent[t, ROWS:] = tail.astype(BF16)


def left_kernel(place, hidden_ref, inv_c, inv_o, gain_ref, og_ref, out):
    c = place[0]
    gain = gain_ref[...].astype(F32)
    normeds, ogs = [], []
    for t, inv_ref in ((c, inv_c), (1 - c, inv_o)):
        normeds.append(hidden_ref[t] * inv_ref[0:1] * gain)
        ogs.append(og_ref[t].astype(F32).T)
    out[...] = jnp.concatenate(normeds + ogs, axis=1).astype(BF16)


def right_rows(b, late, back_o, out_o):
    return [late[b, TOK : 2 * TOK], back_o[b, :TOK], late[b, :TOK], out_o[b]]


def early_kernel(place, left_ref, late, back_o, out_o, *outs):
    left = left_ref[...]
    for d, out in zip(EARLY, outs):
        b = lax.rem(place[1] + d, 8)
        out[...] = dot(left, jnp.concatenate(right_rows(b, late, back_o, out_o), axis=0))


def first_kernel(
    place, part, peer, hidden_ref, inv_c, inv_o, sent, gain_ref, og_ref, emb_m, emb_o, *refs
):
    sums, (left_ref, x4, x3, x5, x8) = refs[:3], refs[3:]
    c = place[0]
    xl = place[2]
    gain = gain_ref[...].astype(F32)
    grads = []
    for t, inv_ref in ((c, inv_c), (1 - c, inv_o)):
        inv = inv_ref[0:1]
        tail = jnp.where(t == xl, sent[0, ROWS:].astype(F32), peer[0, ROWS:].astype(F32))
        mean = (tail[0:1] + tail[8:9]) / inv / D2
        hidden = hidden_ref[t]
        scaled = (part[t] + peer[t, :ROWS].astype(F32)) * gain
        og = og_ref[t].astype(F32).T
        grads.append(og + inv * scaled - hidden * inv * inv * inv * mean)
    left = jnp.concatenate(grads, axis=1).astype(BF16)
    left_ref[...] = left
    half = ROWS // 2
    totals = []
    for d, early in zip(EARLY, sums):
        b = lax.rem(place[1] + d, 8)
        right = jnp.concatenate([emb_m[b], emb_o[b]], axis=0)
        totals.append((dot(left, right) + early[...]).astype(BF16))
    x4[...] = totals[0][:half]
    x8[...] = totals[0][half:]
    x3[...] = totals[1]
    x5[...] = totals[2]


def last_kernel(place, left_ref, more_ref, emb_m, emb_o, late, back_o, out_o, *outs):
    left = jnp.concatenate([left_ref[...], more_ref[...]], axis=1)
    for d, out in zip(LATER, outs):
        b = lax.rem(place[1] + d, 8)
        right = [emb_m[b], emb_o[b], *right_rows(b, late, back_o, out_o)]
        out[...] = dot(left, jnp.concatenate(right, axis=0)).astype(BF16)


def end_kernel(mine, above, below, out):
    out[...] = mine[...].astype(F32) + above[...].astype(F32) + below[...].astype(F32)


def join_kernel(half, mine, near, far, out):
    start = half * (ROWS // 2)
    out[...] = (mine[...].astype(F32) + near[...].astype(F32)).astype(BF16)
    rows = pl.ds(start, ROWS // 2)
    total = mine[rows].astype(F32) + near[rows].astype(F32) + far[...].astype(F32)
    out[rows] = total.astype(BF16)


def turn(x):
    return lax.ppermute(x, ("xl", "c"), [(0, 0), (1, 2), (2, 1), (3, 3)])


def up(v):
    return lax.ppermute(v, "z", [(i, (i + 1) % 8) for i in range(8)])


def down(v):
    return lax.ppermute(v, "z", [(i, (i - 1) % 8) for i in range(8)])


def shards(token_ids, embed, proj, grow_op, norm_gain, out_grad):
    c = lax.axis_index("c")
    z = lax.axis_index("z")
    xl = lax.axis_index("xl")
    place = jnp.stack([c, z, xl]).astype(jnp.int32)
    gain = norm_gain.reshape(ROWS, 1)
    proj = proj.reshape(16, COLS, COLS)
    block = sds((8, TOK, COLS))
    work = 2 * TOK * ROWS * 4096

    with jax.named_scope("embedding"):
        ids = lax.all_to_all(
            jnp.broadcast_to(token_ids.reshape(1, 1, TOK), (16, 1, TOK)), OP, 0, 0, tiled=False
        )
        near = up(grow_op), down(grow_op)
        ids, near = lax.optimization_barrier((ids, near))
        ups, downs = [up(near[0])], [down(near[1])]
        ids = ids.reshape(16, TOK)
        vocab = embed.shape[0]
        first = (z * 2 + xl) * vocab
        own = token_ids.reshape(1, TOK)

        def one(k, held=None):
            at = jnp.stack([first, k]).astype(jnp.int32)
            rows, most = call(
                look_kernel,
                [sds((16, SLOTS, COLS)), sds((8, TOK), F32)],
                at,
                ids,
                embed,
                flops=2 * 16 * SLOTS * vocab * COLS,
            )
            rows, held = lax.optimization_barrier((rows, held))
            rows = lax.all_to_all(rows, OP, 0, 0, tiled=False)
            if held:
                step = up(held[0]), down(held[1]), swap(held[2], "xl")
                rows, step = lax.optimization_barrier((rows, step))
                held = (*held[:2], *step)
            part = call(
                functools.partial(place_kernel, vocab),
                sds((TOK, COLS)),
                at,
                own,
                rows,
                flops=2 * 16 * SLOTS * TOK * COLS,
            )
            return part, most[0, 0], held

        half = ROWS // 2
        found, most, held = one(jnp.int32(0), (ups[0], downs[0], out_grad))
        ups, downs, og_peer = [held[0], held[2]], [held[1], held[3]], held[4]
        found = lax.while_loop(
            lambda state: (state[0] * SLOTS).astype(F32) < most,
            lambda state: (state[0] + 1, state[1] + one(state[0])[0]),
            (jnp.int32(1), found),
        )
        emb_part = turn(found[1])
        far = [up(ups[1][:half]), down(downs[1][half:])]

    with jax.named_scope("operator"):
        og = jnp.stack([jnp.where(xl == 0, out_grad, og_peer), jnp.where(xl == 0, og_peer, out_grad)])

    with jax.named_scope("first"):
        emb = exchange(call(spread_kernel, block, emb_part))
        emb, far = lax.optimization_barrier((emb, far))
        first_up, first_down = near
        grow = [grow_op, first_down, *downs, jnp.concatenate(far, axis=0), *ups[::-1], first_up]
        emb_other = swap(emb, "c")
        back_keep, back_send = call(back_kernel, [block, block], place, og, *grow, flops=work)
        emb_other, back_send = lax.optimization_barrier((emb_other, back_send))

    with jax.named_scope("hidden"):
        pair = sds((2, ROWS, TOK), F32)
        part, sent = call(
            hidden_kernel,
            [pair, sds((2, ROWS, TOK))],
            place,
            emb,
            emb_other,
            *grow,
            flops=work,
        )
        peer = swap(sent, "xl")
        peer, back_recv = lax.optimization_barrier((peer, swap(back_send, "c")))
        short = sds((8, TOK + TAIL, COLS))
        hidden, keep, send = call(
            in_kernel, [pair, short, short], place, part, peer, gain, *grow, flops=work
        )

    with jax.named_scope("second"):
        longer = sds((8, 2 * TOK + TAIL, COLS))
        got = exchange(
            call(second_kernel, longer, keep, swap(send, "c"), back_keep, back_recv)
        )
        before, inv = call(mid_kernel, [sds((2 * TOK, COLS)), sds((8, TOK), F32)], got)
        turned, inv_other = lax.optimization_barrier((turn(before), swap(inv, "c")))

    with jax.named_scope("third"):
        keep, send = call(
            proj_kernel, [block, block], place, turned, proj, flops=2 * TOK * COLS * 4096
        )
        got = exchange(
            call(third_kernel, sds((8, 2 * TOK, COLS)), turned, keep, swap(send, "c"))
        )
        out, stat = call(
            out_kernel,
            [sds((2 * TOK, COLS)), sds((TAIL, COLS))],
            place,
            turned,
            got,
            swap(got[:, :TOK], "c"),
            proj,
            flops=2 * TOK * COLS * 4096,
        )

    with jax.named_scope("fourth"):
        late = exchange(call(fourth_kernel, longer, turn(out), stat))
        back_other = swap(late[:, TOK:], "c")
        part, sent = call(
            grad_kernel,
            [pair, sds((2, ROWS + TAIL, TOK))],
            place,
            late,
            back_other,
            *grow,
            flops=work,
        )
        late, sent = lax.optimization_barrier((late, sent))
        peer = swap(sent, "xl")
        more = call(left_kernel, sds((ROWS, 4 * TOK)), place, hidden, inv, inv_other, gain, og)
        late, more = lax.optimization_barrier((late, more))
        out_other = swap(late[:, :TOK], "c")
        right = late, back_other, out_other
        tile = sds((ROWS, COLS))
        early = call(
            early_kernel, [sds((ROWS, COLS), F32)] * 3, place, more, *right, flops=3 * work // 4
        )
        peer, early = lax.optimization_barrier((peer, early))
        half_tile = sds((ROWS // 2, COLS))
        left, *first = call(
            first_kernel,
            [sds((ROWS, 2 * TOK)), half_tile, tile, tile, half_tile],
            place,
            part,
            peer,
            hidden,
            inv,
            inv_other,
            sent,
            gain,
            og,
            emb,
            emb_other,
            *early,
            flops=3 * work // 8,
        )
        x = dict(zip((*EARLY, 8), first))
        later = call(
            last_kernel,
            [tile] * 5,
            place,
            left,
            more,
            emb,
            emb_other,
            *right,
            flops=15 * work // 8,
        )
        x.update(zip(LATER, later))

    def add(a, b):
        return (a.astype(F32) + b.astype(F32)).astype(BF16)

    with jax.named_scope("scatter"):
        up_far = lax.ppermute(x[4], "z", [(i, (i + 2) % 8) for i in range(8)])
        down_far = lax.ppermute(x[8], "z", [(i, (i - 2) % 8) for i in range(8)])
        above, below = up(x[3]), down(x[5])
        near = above, below, up_far, down_far
        above, below, up_far, down_far = lax.optimization_barrier(near)
        above = up(call(functools.partial(join_kernel, 0), tile, x[2], above, up_far))
        below = down(call(functools.partial(join_kernel, 1), tile, x[6], below, down_far))
        above, below = up(add(above, x[1])), down(add(below, x[7]))
        return call(end_kernel, sds((ROWS, COLS), F32), x[0], above, below)


def solution(mesh):
    fine = Mesh(mesh.devices.reshape(8, 2, 4, 2, 2), ("z", "xl", "y", "xh", "c"))
    in_specs = (P(OP), P(OP, TP), P(None, TP), P(TP, OP), P(TP), P(OP, TP))
    return jax.shard_map(shards, mesh=fine, in_specs=in_specs, out_specs=P(TP, OP), check_vma=False)
```

```python
import functools

import jax
import jax.numpy as jnp
import numpy as np
from jax import lax
from jax.experimental import pallas as pl
from jax.experimental.pallas import tpu as pltpu
from jax.sharding import Mesh, PartitionSpec as P

D2 = 6656
EPS = 1e-05
TOK = 128
ROWS = 416
COLS = 256
TAIL = 16
SLOTS = 48
OP = ("z", "xl")
TP = ("y", "xh", "c")
YX = ("y", "xh")
F32 = jnp.float32
BF16 = jnp.bfloat16
NT = (((1,), (1,)), ((), ()))
EARLY = (4, 3, 5)
LATER = (2, 6, 1, 7, 0)


def call(kernel, out_shape, *args, flops=0):
    smem = pl.BlockSpec(memory_space=pltpu.SMEM)
    vmem = pl.BlockSpec(memory_space=pltpu.VMEM)
    single = not isinstance(out_shape, (list, tuple))
    outs = [out_shape] if single else list(out_shape)
    nbytes = sum(int(np.prod(a.shape)) * a.dtype.itemsize for a in list(args) + outs)
    return pl.pallas_call(
        kernel,
        out_shape=out_shape,
        in_specs=[smem if a.dtype == jnp.int32 and a.ndim == 1 else vmem for a in args],
        out_specs=vmem if single else [vmem] * len(outs),
        compiler_params=pltpu.CompilerParams(vmem_limit_bytes=20 * 1024 * 1024),
        cost_estimate=pl.CostEstimate(flops=flops, bytes_accessed=nbytes, transcendentals=0),
    )(*args)


def sds(shape, dtype=BF16):
    return jax.ShapeDtypeStruct(shape, dtype)


def dot(a, b):
    return jnp.dot(a, b, preferred_element_type=F32)


def dot_nt(a, b):
    return lax.dot_general(a, b, NT, preferred_element_type=F32)


def swap(x, axis):
    return lax.ppermute(x, axis, [(0, 1), (1, 0)])


def exchange(x):
    return lax.all_to_all(x, YX, 0, 0, tiled=False)


def ranks(inside, base):
    before = lax.broadcasted_iota(jnp.int32, (TOK, TOK), 0)
    after = lax.broadcasted_iota(jnp.int32, (TOK, TOK), 1)
    marks = jnp.where(inside, 1.0, 0.0).astype(BF16)
    rank = dot(marks, jnp.where(before < after, 1.0, 0.0).astype(BF16))
    return jnp.where(inside, rank - base, -1.0)


def ids_kernel(ids, out):
    for o in range(16):
        out[o] = ids[...]


def look_kernel(at, ids_ref, table_ref, out_ref, most_ref):
    vocab = table_ref.shape[0]
    most = jnp.zeros((16, 1), F32)
    for v in range(16):
        here = (ids_ref[...] >= v * vocab) & (ids_ref[...] < (v + 1) * vocab)
        most = jnp.maximum(most, jnp.sum(jnp.where(here, 1.0, 0.0), axis=1, keepdims=True))
    most_ref[...] = jnp.broadcast_to(jnp.max(most, axis=0, keepdims=True), (8, TOK))
    ids = ids_ref[...] - at[0]
    key = ranks((ids >= 0) & (ids < vocab), (at[1] * SLOTS).astype(F32))
    ids = ids.astype(F32) + 1.0
    slot = lax.broadcasted_iota(jnp.int32, (SLOTS, TOK), 0).astype(F32)
    lanes = lax.broadcasted_iota(jnp.int32, (4 * SLOTS, vocab), 1).astype(F32)
    table = table_ref[...]
    for g in range(4):
        rows = []
        for o in range(4 * g, 4 * g + 4):
            hit = jnp.where(slot == key[o : o + 1], ids[o : o + 1], 0.0)
            rows.append(jnp.sum(hit, axis=1, keepdims=True) - 1.0)
        hot = jnp.where(lanes == jnp.concatenate(rows, axis=0), 1.0, 0.0).astype(BF16)
        found = dot(hot, table).astype(BF16)
        for o in range(4):
            out_ref[4 * g + o] = found[o * SLOTS : (o + 1) * SLOTS]


def place_kernel(vocab, at, ids_ref, rows_ref, out_ref):
    ids = jnp.broadcast_to(ids_ref[...], (16, TOK))
    first = lax.broadcasted_iota(jnp.int32, (16, TOK), 0) * vocab
    key = ranks((ids >= first) & (ids < first + vocab), (at[1] * SLOTS).astype(F32))
    slot = lax.broadcasted_iota(jnp.int32, (SLOTS, TOK), 0).astype(F32)
    hits = [jnp.where(slot == key[v : v + 1], 1.0, 0.0) for v in range(16)]
    hits = jnp.concatenate(hits, axis=0).T.astype(BF16)
    rows = jnp.concatenate([rows_ref[v] for v in range(16)], axis=0)
    out_ref[...] = dot(hits, rows).astype(BF16)


def split_row(row):
    hi = row.astype(BF16)
    lo = (row - hi.astype(F32)).astype(BF16)
    return jnp.broadcast_to(jnp.concatenate([hi, lo], axis=1), (TAIL, COLS))


def join_row(tail):
    both = tail.astype(F32)[0:1]
    return both[:, :TOK] + both[:, TOK:]


def blocks(place, grow):
    for d in range(8):
        yield lax.rem(place[1] + d, 8), grow[d]


def spread_kernel(rows, out):
    for b in range(8):
        out[b] = rows[...]


def hidden_kernel(place, got, other, *refs):
    grow, (part, sent) = refs[:8], refs[8:]
    c = place[0]
    total = jnp.zeros((ROWS, 2 * TOK), F32)
    for b, cols in blocks(place, grow):
        total += dot_nt(cols[...], jnp.concatenate([got[b], other[b]], axis=0))
    for t, rows in ((c, total[:, :TOK]), (1 - c, total[:, TOK:])):
        part[t] = rows
        sent[t] = rows.astype(BF16)


def back_kernel(place, og, *refs):
    grow, (keep, send) = refs[:8], refs[8:]
    c = place[0]
    left = jnp.concatenate([og[c], og[1 - c]], axis=0)
    for b, cols in blocks(place, grow):
        both = dot(left, cols[...]).astype(BF16)
        keep[b] = both[:TOK]
        send[b] = both[TOK:]


def in_kernel(place, part, peer, gain, *refs):
    grow, (hidden_ref, keep, send) = refs[:8], refs[8:]
    c = place[0]
    left = []
    for t, to in ((c, keep), (1 - c, send)):
        hidden = part[t] + peer[t].astype(F32)
        hidden_ref[t] = hidden
        left.append((hidden * gain[...].astype(F32)).T.astype(BF16))
        tail = split_row(jnp.sum(hidden * hidden, axis=0, keepdims=True))
        for b in range(8):
            to[b, TOK:] = tail
    left = jnp.concatenate(left, axis=0)
    for b, cols in blocks(place, grow):
        both = dot(left, cols[...]).astype(BF16)
        keep[b, :TOK] = both[:TOK]
        send[b, :TOK] = both[TOK:]


def second_kernel(keep, recv, back_keep, back_recv, out):
    tail = split_row(join_row(keep[0, TOK:]) + join_row(recv[0, TOK:]))
    for b in range(8):
        out[b, :TOK] = (keep[b, :TOK].astype(F32) + recv[b, :TOK].astype(F32)).astype(BF16)
        out[b, TOK : 2 * TOK] = (back_keep[b].astype(F32) + back_recv[b].astype(F32)).astype(BF16)
        out[b, 2 * TOK :] = tail


def mid_kernel(got, out, inv_ref):
    both = got[0, : 2 * TOK].astype(F32)
    row = join_row(got[0, 2 * TOK :])
    for b in range(1, 8):
        both += got[b, : 2 * TOK].astype(F32)
        row += join_row(got[b, 2 * TOK :])
    inv = lax.rsqrt(jnp.broadcast_to(row, (TOK, TOK)) / D2 + EPS)
    inv_ref[...] = inv[0:8]
    out[:TOK] = (both[:TOK] * inv.T[:, 0:1]).astype(BF16)
    out[TOK:] = both[TOK:].astype(BF16)


def proj_kernel(place, turned, proj, keep, send):
    c = place[0]
    back = turned[TOK:]
    for b in range(8):
        keep[b] = dot_nt(back, proj[2 * b + c]).astype(BF16)
        send[b] = dot_nt(back, proj[2 * b + 1 - c]).astype(BF16)


def third_kernel(turned, keep, recv, out):
    for b in range(8):
        out[b, :TOK] = turned[:TOK]
        out[b, TOK:] = (keep[b].astype(F32) + recv[b].astype(F32)).astype(BF16)


def out_kernel(place, turned, got, other, proj, out, stat_ref):
    c = place[0]
    total = jnp.zeros((TOK, COLS), F32)
    back = jnp.zeros((TOK, COLS), F32)
    for b in range(8):
        total += dot(got[b, :TOK], proj[2 * b + c])
        total += dot(other[b], proj[2 * b + 1 - c])
        back += got[b, TOK:].astype(F32)
    back = back.astype(BF16)
    out[:TOK] = total.astype(BF16)
    out[TOK:] = back
    stat = jnp.sum(back.astype(F32) * turned[:TOK].astype(F32), axis=1, keepdims=True)
    stat_ref[...] = split_row(jnp.broadcast_to(stat, (TOK, TOK)).T[0:1])


def fourth_kernel(turned, stat, out):
    for b in range(8):
        out[b, : 2 * TOK] = turned[...]
        out[b, 2 * TOK :] = stat[...]


def grad_kernel(place, got, other, *refs):
    grow, (part, sent) = refs[:8], refs[8:]
    c = place[0]
    total = jnp.zeros((ROWS, 2 * TOK), F32)
    for b, cols in blocks(place, grow):
        pair = jnp.concatenate([got[b, TOK : 2 * TOK], other[b, :TOK]], axis=0)
        total += dot_nt(cols[...], pair)
    stat = jnp.zeros((1, TOK), F32)
    for b in range(8):
        stat += join_row(got[b, 2 * TOK :]) + join_row(other[b, TOK:])
    both = split_row(stat).astype(F32)
    tail = jnp.concatenate([both[:8, :TOK], both[:8, TOK:]], axis=0)
    for t, rows in ((c, total[:, :TOK]), (1 - c, total[:, TOK:])):
        part[t] = rows
        sent[t, :ROWS] = rows.astype(BF16)
        sent[t, ROWS:] = tail.astype(BF16)


def left_kernel(place, hidden_ref, inv_c, inv_o, gain_ref, og_ref, out):
    c = place[0]
    gain = gain_ref[...].astype(F32)
    normeds, ogs = [], []
    for t, inv_ref in ((c, inv_c), (1 - c, inv_o)):
        normeds.append(hidden_ref[t] * inv_ref[0:1] * gain)
        ogs.append(og_ref[t].astype(F32).T)
    out[...] = jnp.concatenate(normeds + ogs, axis=1).astype(BF16)


def right_rows(b, late, back_o, out_o):
    return [late[b, TOK : 2 * TOK], back_o[b, :TOK], late[b, :TOK], out_o[b]]


def early_kernel(place, left_ref, late, back_o, out_o, *outs):
    left = left_ref[...]
    for d, out in zip(EARLY, outs):
        b = lax.rem(place[1] + d, 8)
        out[...] = dot(left, jnp.concatenate(right_rows(b, late, back_o, out_o), axis=0))


def first_kernel(
    place, part, peer, hidden_ref, inv_c, inv_o, sent, gain_ref, og_ref, emb_m, emb_o, *refs
):
    sums, (left_ref, x4, x3, x5, x8) = refs[:3], refs[3:]
    c = place[0]
    xl = place[2]
    gain = gain_ref[...].astype(F32)
    grads = []
    for t, inv_ref in ((c, inv_c), (1 - c, inv_o)):
        inv = inv_ref[0:1]
        tail = jnp.where(t == xl, sent[0, ROWS:].astype(F32), peer[0, ROWS:].astype(F32))
        mean = (tail[0:1] + tail[8:9]) / inv / D2
        hidden = hidden_ref[t]
        scaled = (part[t] + peer[t, :ROWS].astype(F32)) * gain
        og = og_ref[t].astype(F32).T
        grads.append(og + inv * scaled - hidden * inv * inv * inv * mean)
    left = jnp.concatenate(grads, axis=1).astype(BF16)
    left_ref[...] = left
    half = ROWS // 2
    totals = []
    for d, early in zip(EARLY, sums):
        b = lax.rem(place[1] + d, 8)
        right = jnp.concatenate([emb_m[b], emb_o[b]], axis=0)
        totals.append((dot(left, right) + early[...]).astype(BF16))
    x4[...] = totals[0][:half]
    x8[...] = totals[0][half:]
    x3[...] = totals[1]
    x5[...] = totals[2]


def last_kernel(place, left_ref, more_ref, emb_m, emb_o, late, back_o, out_o, *outs):
    left = jnp.concatenate([left_ref[...], more_ref[...]], axis=1)
    for d, out in zip(LATER, outs):
        b = lax.rem(place[1] + d, 8)
        right = [emb_m[b], emb_o[b], *right_rows(b, late, back_o, out_o)]
        out[...] = dot(left, jnp.concatenate(right, axis=0)).astype(BF16)


def end_kernel(mine, above, below, out):
    out[...] = mine[...].astype(F32) + above[...].astype(F32) + below[...].astype(F32)


def join_kernel(half, mine, near, far, out):
    start = half * (ROWS // 2)
    out[...] = (mine[...].astype(F32) + near[...].astype(F32)).astype(BF16)
    rows = pl.ds(start, ROWS // 2)
    total = mine[rows].astype(F32) + near[rows].astype(F32) + far[...].astype(F32)
    out[rows] = total.astype(BF16)


def turn(x):
    return lax.ppermute(x, ("xl", "c"), [(0, 0), (1, 2), (2, 1), (3, 3)])


def up(v):
    return lax.ppermute(v, "z", [(i, (i + 1) % 8) for i in range(8)])


def down(v):
    return lax.ppermute(v, "z", [(i, (i - 1) % 8) for i in range(8)])


def shards(token_ids, embed, proj, grow_op, norm_gain, out_grad):
    c = lax.axis_index("c")
    z = lax.axis_index("z")
    xl = lax.axis_index("xl")
    place = jnp.stack([c, z, xl]).astype(jnp.int32)
    gain = norm_gain.reshape(ROWS, 1)
    proj = proj.reshape(16, COLS, COLS)
    block = sds((8, TOK, COLS))
    work = 2 * TOK * ROWS * 4096

    with jax.named_scope("embedding"):
        ids = lax.all_to_all(
            call(ids_kernel, sds((16, 1, TOK), jnp.int32), token_ids.reshape(1, TOK)),
            OP,
            0,
            0,
            tiled=False,
        )
        near = up(grow_op), down(grow_op)
        ids, near = lax.optimization_barrier((ids, near))
        ups, downs = [up(near[0])], [down(near[1])]
        ids = ids.reshape(16, TOK)
        vocab = embed.shape[0]
        first = (z * 2 + xl) * vocab
        own = token_ids.reshape(1, TOK)

        def one(k, held=None):
            at = jnp.stack([first, k]).astype(jnp.int32)
            rows, most = call(
                look_kernel,
                [sds((16, SLOTS, COLS)), sds((8, TOK), F32)],
                at,
                ids,
                embed,
                flops=2 * 16 * SLOTS * vocab * COLS,
            )
            rows, held = lax.optimization_barrier((rows, held))
            rows = lax.all_to_all(rows, OP, 0, 0, tiled=False)
            if held:
                step = up(held[0]), down(held[1]), swap(held[2], "xl")
                rows, step = lax.optimization_barrier((rows, step))
                held = (*held[:2], *step)
            part = call(
                functools.partial(place_kernel, vocab),
                sds((TOK, COLS)),
                at,
                own,
                rows,
                flops=2 * 16 * SLOTS * TOK * COLS,
            )
            return part, most[0, 0], held

        half = ROWS // 2
        found, most, held = one(jnp.int32(0), (ups[0], downs[0], out_grad))
        ups, downs, og_peer = [held[0], held[2]], [held[1], held[3]], held[4]
        found = lax.while_loop(
            lambda state: (state[0] * SLOTS).astype(F32) < most,
            lambda state: (state[0] + 1, state[1] + one(state[0])[0]),
            (jnp.int32(1), found),
        )
        emb_part = turn(found[1])
        far = [up(ups[1][:half]), down(downs[1][half:])]

    with jax.named_scope("operator"):
        og = jnp.stack([jnp.where(xl == 0, out_grad, og_peer), jnp.where(xl == 0, og_peer, out_grad)])

    with jax.named_scope("first"):
        emb = exchange(call(spread_kernel, block, emb_part))
        emb, far = lax.optimization_barrier((emb, far))
        first_up, first_down = near
        grow = [grow_op, first_down, *downs, jnp.concatenate(far, axis=0), *ups[::-1], first_up]
        emb_other = swap(emb, "c")
        back_keep, back_send = call(back_kernel, [block, block], place, og, *grow, flops=work)
        emb_other, back_send = lax.optimization_barrier((emb_other, back_send))

    with jax.named_scope("hidden"):
        pair = sds((2, ROWS, TOK), F32)
        part, sent = call(
            hidden_kernel,
            [pair, sds((2, ROWS, TOK))],
            place,
            emb,
            emb_other,
            *grow,
            flops=work,
        )
        peer = swap(sent, "xl")
        peer, back_recv = lax.optimization_barrier((peer, swap(back_send, "c")))
        short = sds((8, TOK + TAIL, COLS))
        hidden, keep, send = call(
            in_kernel, [pair, short, short], place, part, peer, gain, *grow, flops=work
        )

    with jax.named_scope("second"):
        longer = sds((8, 2 * TOK + TAIL, COLS))
        got = exchange(
            call(second_kernel, longer, keep, swap(send, "c"), back_keep, back_recv)
        )
        before, inv = call(mid_kernel, [sds((2 * TOK, COLS)), sds((8, TOK), F32)], got)
        turned, inv_other = lax.optimization_barrier((turn(before), swap(inv, "c")))

    with jax.named_scope("third"):
        keep, send = call(
            proj_kernel, [block, block], place, turned, proj, flops=2 * TOK * COLS * 4096
        )
        got = exchange(
            call(third_kernel, sds((8, 2 * TOK, COLS)), turned, keep, swap(send, "c"))
        )
        out, stat = call(
            out_kernel,
            [sds((2 * TOK, COLS)), sds((TAIL, COLS))],
            place,
            turned,
            got,
            swap(got[:, :TOK], "c"),
            proj,
            flops=2 * TOK * COLS * 4096,
        )

    with jax.named_scope("fourth"):
        late = exchange(call(fourth_kernel, longer, turn(out), stat))
        back_other = swap(late[:, TOK:], "c")
        part, sent = call(
            grad_kernel,
            [pair, sds((2, ROWS + TAIL, TOK))],
            place,
            late,
            back_other,
            *grow,
            flops=work,
        )
        late, sent = lax.optimization_barrier((late, sent))
        peer = swap(sent, "xl")
        more = call(left_kernel, sds((ROWS, 4 * TOK)), place, hidden, inv, inv_other, gain, og)
        late, more = lax.optimization_barrier((late, more))
        out_other = swap(late[:, :TOK], "c")
        right = late, back_other, out_other
        tile = sds((ROWS, COLS))
        early = call(
            early_kernel, [sds((ROWS, COLS), F32)] * 3, place, more, *right, flops=3 * work // 4
        )
        peer, early = lax.optimization_barrier((peer, early))
        half_tile = sds((ROWS // 2, COLS))
        left, *first = call(
            first_kernel,
            [sds((ROWS, 2 * TOK)), half_tile, tile, tile, half_tile],
            place,
            part,
            peer,
            hidden,
            inv,
            inv_other,
            sent,
            gain,
            og,
            emb,
            emb_other,
            *early,
            flops=3 * work // 8,
        )
        x = dict(zip((*EARLY, 8), first))
        later = call(
            last_kernel,
            [tile] * 5,
            place,
            left,
            more,
            emb,
            emb_other,
            *right,
            flops=15 * work // 8,
        )
        x.update(zip(LATER, later))

    def add(a, b):
        return (a.astype(F32) + b.astype(F32)).astype(BF16)

    with jax.named_scope("scatter"):
        up_far = lax.ppermute(x[4], "z", [(i, (i + 2) % 8) for i in range(8)])
        down_far = lax.ppermute(x[8], "z", [(i, (i - 2) % 8) for i in range(8)])
        above, below = up(x[3]), down(x[5])
        near = above, below, up_far, down_far
        above, below, up_far, down_far = lax.optimization_barrier(near)
        above = up(call(functools.partial(join_kernel, 0), tile, x[2], above, up_far))
        below = down(call(functools.partial(join_kernel, 1), tile, x[6], below, down_far))
        above, below = up(add(above, x[1])), down(add(below, x[7]))
        return call(end_kernel, sds((ROWS, COLS), F32), x[0], above, below)


def solution(mesh):
    fine = Mesh(mesh.devices.reshape(8, 2, 4, 2, 2), ("z", "xl", "y", "xh", "c"))
    in_specs = (P(OP), P(OP, TP), P(None, TP), P(TP, OP), P(TP), P(OP, TP))
    return jax.shard_map(shards, mesh=fine, in_specs=in_specs, out_specs=P(TP, OP), check_vma=False)
```
